32 devices in a mesh: dp: 8 (over z, x), section: 4 (over y, core).
Axes of the slice: x: 2, y: 2, z: 4, core: 2. Of those that a mesh axis runs over, the one named last changes fastest.
Arguments:
- tokens: bfloat16 [16384, 768], P(('dp', 'section')), may hold values from -6 to 6
- cotangent: bfloat16 [16384, 768], P(('dp', 'section')), may hold values from -6 to 6
- doc_ids: int32 [16, 1024], P('dp'), may hold values from 0 to 7, never falling along the last dimension, each value on 1 to 512 neighbouring positions
- gain_attn: float32 [4, 768], P('section'), may hold values from 0.5 to 1.5
- w_qkv: bfloat16 [4, 768, 2304], P('section'), may hold values from -0.21875 to 0.21875
- w_out: bfloat16 [4, 768, 768], P('section'), may hold values from -1.75 to 1.75
- gain_mlp: float32 [4, 768], P('section'), may hold values from 0.5 to 1.5
- w_up: bfloat16 [4, 768, 3072], P('section'), may hold values from -0.21875 to 0.21875
- w_down: bfloat16 [4, 3072, 768], P('section'), may hold values from -0.109375 to 0.109375
Outputs:
- output: bfloat16 [16384, 768], P(('dp', 'section'))
- input_grad: bfloat16 [16384, 768], P(('dp', 'section'))
- grad_gain_attn: float32 [4, 768], P('section', 'dp')
- grad_qkv: float32 [4, 768, 2304], P('section', 'dp')
- grad_out: float32 [4, 768, 768], P('section', 'dp')
- grad_gain_mlp: float32 [4, 768], P('section', 'dp')
- grad_up: float32 [4, 768, 3072], P('section', 'dp')
- grad_down: float32 [4, 3072, 768], P('section', 'dp')
The draws below stay inside these ranges and needn't reach their ends.
Inputs may be any that keep to these rules, and one draw needn't show every extreme that they name: `doc_ids`: along each packed row of 1024 tokens the numbers never fall; each of the 8 documents of a row has 1 to 512 tokens, and one has exactly 512.
All inputs are finite; a program needn't handle non-finite values.
Results may differ from the reference program's by a relative error of at most 0.025.
Values may be sent and summed in bfloat16 or wider, within the bound.
A program may use at most 512 MiB of HBM per device.

```python
import math
from functools import partial
import jax
import jax.numpy as jnp
import numpy as np
from jax import lax

D = 768
HEADS = 12
HD = 64
FF = 3072
SEQ = 1024
SEGS = 8
LAYERS = 4
ROWS = 16
TOKENS = 16384


def block_scale(stream_key, shape, cuts, low, largest):
    def one(axis_at, blocks):
        steps = jax.random.uniform(jax.random.fold_in(jax.random.fold_in(stream_key, 6), axis_at), (blocks,), jnp.float32, low / len(cuts), largest / len(cuts))
        return jnp.repeat(jnp.exp(steps), shape[axis_at] // blocks).reshape((-1,) + (1,) * (len(shape) - axis_at - 1))

    factor_of = one(*cuts[0])
    for cut in cuts[1:]:
        factor_of = factor_of * one(*cut)
    return factor_of


def profile(amount, total, reach, lean):
    loads = [(1 << 20) // math.isqrt(rank ** lean) + 1 for rank in range(2, amount + 1)]
    rest, given = total - reach - (amount - 1), [1] * (amount - 1)
    while rest > 0:
        free = [i for i in range(amount - 1) if given[i] < reach]
        pool, remaining = sum([loads[i] for i in free]), rest
        for i in free:
            extra = min(reach - given[i], max(1, remaining * loads[i] // pool), rest)
            given[i] = given[i] + extra
            rest = rest - extra
    return np.array([reach] + given)


def uneven_parts(stream_key, number_of, total, most, skew):
    if number_of == 2:
        one = jax.random.randint(stream_key, (), max(1, total - most), min(most, total - 1) + 1)
        return jnp.stack([one, total - one])
    tallies = jnp.asarray(profile(number_of, total, most, skew), jnp.int32)
    couples = (number_of - 1) // 2
    donor, sink = tallies[1:1 + 2 * couples:2], tallies[2:2 + 2 * couples:2]
    room = jnp.minimum(donor - 1, most - sink)
    moved = jax.random.randint(jax.random.fold_in(stream_key, 1), (couples,), 0, 1 << 20) % (room + 1)
    tallies = tallies.at[1:1 + 2 * couples:2].set(donor - moved).at[2:2 + 2 * couples:2].set(sink + moved)
    return tallies[jax.random.permutation(jax.random.fold_in(stream_key, 2), number_of)]


def normal_values(own_key, extent, deviation, bound, pieces=(), held_as=jnp.bfloat16):
    values = jax.random.normal(own_key, extent, jnp.float32) * deviation
    if len(pieces) > 0:
        values = block_scale(own_key, extent, pieces, -0.22, 0.18) * values
    return jnp.clip(values, min=-bound, max=bound).astype(held_as)


def setup_inputs(seed: int = 0) -> dict:
    arg_keys = jax.random.split(jax.random.key(seed), 10)
    return {
        "tokens": normal_values(arg_keys[0], (TOKENS, D), 1.0, 6.0, ((0, 32),)),
        "cotangent": normal_values(arg_keys[1], (TOKENS, D), 1.0, 6.0, ((0, 32),)),
        "doc_ids": jax.vmap(lambda own: jnp.searchsorted(jnp.cumsum(uneven_parts(own, SEGS, SEQ, SEQ // 2, 2)), jnp.arange(SEQ), side="right"))(jax.random.split(arg_keys[2], ROWS)).reshape((ROWS, SEQ)).astype(jnp.int32),
        "gain_attn": jnp.clip(1.0 + 0.1 * jax.random.normal(arg_keys[3], (LAYERS, D), jnp.float32), 0.5, 1.5),
        "w_qkv": normal_values(arg_keys[4], (LAYERS, D, 3 * D), D ** -0.5, 0.21875, ((0, 4),)),
        "w_out": normal_values(arg_keys[5], (LAYERS, D, D), (max(D // 64, 1)) ** -0.5, 1.75, ((0, 4),)),
        "gain_mlp": jnp.clip(1.0 + 0.1 * jax.random.normal(arg_keys[6], (LAYERS, D), jnp.float32), 0.5, 1.5),
        "w_up": normal_values(arg_keys[7], (LAYERS, D, FF), D ** -0.5, 0.21875, ((0, 4),)),
        "w_down": normal_values(arg_keys[8], (LAYERS, FF, D), FF ** -0.5, 0.109375, ((0, 4),)),
    }


epsilon = 1e-05
neg_big = -1e+30

@jax.custom_vjp
def low(v):
    return lax.optimization_barrier(v.astype(jnp.bfloat16)).astype(jnp.float32)

@jax.custom_vjp
def low_back(v):
    return v

def low_keep(v):
    return (low(v), None)

def low_pass(kept, grad):
    return (grad,)

def back_keep(v):
    return (v, None)

def back_low(kept, grad):
    return (low(grad),)
low.defvjp(low_keep, low_pass)
low_back.defvjp(back_keep, back_low)

def highest_dot(left_side, right_side):
    return jnp.dot(left_side, right_side, precision=lax.Precision.HIGHEST, preferred_element_type=jnp.float32)

def scaled_norm(values, gain_vec):
    factor = lax.rsqrt(lax.optimization_barrier(jnp.mean(values * values, axis=-1, keepdims=True)) + epsilon)
    return values * factor * gain_vec

def center_rows(values):
    return values - lax.optimization_barrier(jnp.mean(values, axis=-1, keepdims=True))

def attend_row(packed):
    triple, row_docs = packed
    queries = triple[:, :D].reshape(SEQ, HEADS, HD)
    keys_all = triple[:, D:2 * D].reshape(SEQ, HEADS, HD)
    values_all = triple[:, 2 * D:].reshape(SEQ, HEADS, HD)
    scores = jnp.einsum('qhd,khd->hqk', queries, keys_all, precision=lax.Precision.HIGHEST) * HD ** (-0.5)
    scores = low_back(scores)
    positions = jnp.arange(SEQ)
    allowed = (positions[None, :] <= positions[:, None]) & (row_docs[:, None] == row_docs[None, :])
    scores = jnp.where(allowed[None], scores, neg_big)
    attn_probs = low(jax.nn.softmax(scores, axis=-1))
    mixed_heads = jnp.einsum('hqk,khd->qhd', attn_probs, values_all, precision=lax.Precision.HIGHEST)
    return mixed_heads.reshape(SEQ, D)

def layer_forward(stream, doc_ids, gain_a, weight_qkv, weight_o, gain_m, weight_up, weight_down):
    normed_attn = low(scaled_norm(stream, gain_a))
    triple = low_back(low(highest_dot(normed_attn, weight_qkv)))
    row_triples = triple.reshape(-1, SEQ, 3 * D)
    mixed_heads = lax.map(jax.checkpoint(attend_row), (row_triples, doc_ids)).reshape(-1, D)
    mixed_heads = low_back(low(mixed_heads))
    branch = low_back(highest_dot(mixed_heads, weight_o))
    middle = stream + center_rows(branch)
    normed_mlp = low(scaled_norm(middle, gain_m))
    hidden = low_back(highest_dot(normed_mlp, weight_up))
    active = low(jax.nn.gelu(hidden, approximate=True))
    branch = low_back(highest_dot(active, weight_down))
    return middle + center_rows(branch)

def forward_all(doc_ids, inputs, gains_a, weights_qkv, weights_o, gains_m, weights_up, weights_down):
    stream = center_rows(inputs)
    for depth in range(LAYERS):
        if depth > 0:
            stream = low_back(low(stream))
        stream = layer_forward(stream, doc_ids, gains_a[depth], weights_qkv[depth], weights_o[depth], gains_m[depth], weights_up[depth], weights_down[depth])
    return stream

def reference(tokens, cotangent, doc_ids, gain_attn, w_qkv, w_out, gain_mlp, w_up, w_down):
    floats = (tokens.astype(jnp.float32), gain_attn.astype(jnp.float32), w_qkv.astype(jnp.float32), w_out.astype(jnp.float32), gain_mlp.astype(jnp.float32), w_up.astype(jnp.float32), w_down.astype(jnp.float32))
    result, pullback = jax.vjp(partial(forward_all, doc_ids), *floats)
    grads = pullback(cotangent.astype(jnp.float32))
    return (result.astype(jnp.bfloat16), grads[0].astype(jnp.bfloat16), grads[1], grads[2], grads[3], grads[4], grads[5], grads[6])
```

```python
import functools

import jax
import jax.numpy as jnp
from jax import lax
from jax.experimental import pallas as pl
from jax.experimental.pallas import tpu as pltpu
from jax.sharding import PartitionSpec as P

D = 768
HEADS = 12
HD = 64
FF = 3072
C = 256
WIN = 3
PAIRS = HEADS // 2
EPS = 1e-05
NEG = -1e30
MESH = pl.DeviceIdType.MESH
BF16 = jnp.bfloat16
F32 = jnp.float32
VMEM_LIMIT = 60 * 1024 * 1024


def dot(a, b):
    return jnp.dot(a, b, preferred_element_type=F32)


def dot_nt(a, b):
    return lax.dot_general(a, b, (((1,), (1,)), ((), ())), preferred_element_type=F32)


def row_mean(v):
    return jnp.mean(v, axis=-1, keepdims=True)


def greet(section, sections):
    dp = lax.axis_index("dp")
    barrier = pltpu.get_barrier_semaphore()
    for step in range(1, sections):
        other = lax.rem(section + step, sections)
        pl.semaphore_signal(barrier, inc=1, device_id=(dp, other), device_id_type=MESH)
    pl.semaphore_wait(barrier, sections - 1)


def lane_masks():
    lane = lax.broadcasted_iota(jnp.int32, (1, 2 * HD), 1)
    low = (lane < HD).astype(F32)
    return low.astype(BF16), (1.0 - low).astype(BF16), lane < HD


def two_heads(pair, low, high):
    return jnp.concatenate([pair * low, pair * high], axis=0)


def await_arrival(buf, sem):
    pltpu.make_async_copy(buf, buf, sem).wait()


def scatter_rows(section, sections, per, rows, inbox, sems, send_sems, target):
    dp = lax.axis_index("dp")
    for piece in range(per):
        slot = section * per + piece

        @pl.when(section != target)
        def _():
            pltpu.make_async_remote_copy(
                rows.at[piece],
                inbox.at[slot],
                send_sems.at[piece],
                sems.at[slot],
                device_id=(dp, target),
                device_id_type=MESH,
            ).start()

        @pl.when(section == target)
        def _():
            pltpu.make_async_copy(rows.at[piece], inbox.at[slot], sems.at[slot]).start()


def drain_rows(section, sections, per, rows, send_sems, target):
    for piece in range(per):

        @pl.when(section != target)
        def _():
            pltpu.make_async_copy(rows.at[piece], rows.at[piece], send_sems.at[piece]).wait()


def pass_on(section, chunk, per, last, step, outbox, inbox, result, sends, arrivals, landed, kept):
    dp = lax.axis_index("dp")
    owner = chunk // per

    @pl.when(section != last)
    def _():
        pltpu.make_async_remote_copy(
            outbox.at[chunk],
            inbox.at[chunk],
            sends.at[chunk],
            arrivals.at[chunk],
            device_id=(dp, section + step),
            device_id_type=MESH,
        ).start()

    @pl.when((section == last) & (owner != last))
    def _():
        pltpu.make_async_remote_copy(
            outbox.at[chunk],
            result.at[lax.rem(chunk, per)],
            sends.at[chunk],
            landed.at[lax.rem(chunk, per)],
            device_id=(dp, owner),
            device_id_type=MESH,
        ).start()

    @pl.when((section == last) & (owner == last))
    def _():
        pltpu.make_async_copy(
            outbox.at[chunk], result.at[lax.rem(chunk, per)], kept.at[lax.rem(chunk, per)]
        ).start()


def settle(section, chunks, per, last, outbox, result, sends, landed, kept):
    def one(chunk, carry):
        @pl.when((section != last) | (chunk // per != last))
        def _():
            await_arrival(outbox.at[chunk], sends.at[chunk])

        return carry

    lax.fori_loop(0, chunks, one, 0)
    for piece in range(per):

        @pl.when(section != last)
        def _():
            await_arrival(result.at[piece], landed.at[piece])

        @pl.when(section == last)
        def _():
            await_arrival(result.at[piece], kept.at[piece])


def forward_kernel(
    sections,
    tokens,
    doc_q,
    doc_k,
    gain_a,
    gain_m,
    w_qkv,
    w_out,
    w_up,
    w_down,
    result,
    s_x,
    s_q,
    s_k,
    s_v,
    s_na,
    s_mixed,
    s_lse,
    s_mid,
    s_nm,
    s_act,
    s_dg,
    inbox,
    outbox,
    kbuf,
    vbuf,
    bias,
    b_q,
    b_na,
    b_mixed,
    b_lse,
    b_mid,
    b_nm,
    b_act,
    b_dg,
    arrivals,
    sends,
    first_sends,
    landed,
    kept,
    saves,
):
    section = lax.axis_index("section")
    chunks = inbox.shape[0]
    per = tokens.shape[0]
    greet(section, sections)
    scatter_rows(section, sections, per, tokens, inbox, arrivals, first_sends, 0)
    low, high, is_low = lane_masks()
    kbuf[pl.ds(0, 2 * C), :] = jnp.zeros((2 * C, D), BF16)
    vbuf[pl.ds(0, 2 * C), :] = jnp.zeros((2 * C, D), BF16)
    centered = jnp.where(section == 0, 1.0, 0.0).astype(F32)

    def stores(chunk, slot):
        here = pl.ds(pl.multiple_of((chunk + 2) * C, C), C)
        pairs = (
            (inbox.at[chunk], s_x),
            (kbuf.at[here], s_k),
            (vbuf.at[here], s_v),
            (b_q.at[slot], s_q),
            (b_na.at[slot], s_na),
            (b_mixed.at[slot], s_mixed),
            (b_lse.at[slot], s_lse),
            (b_mid.at[slot], s_mid),
            (b_nm.at[slot], s_nm),
            (b_act.at[slot], s_act),
            (b_dg.at[slot], s_dg),
        )
        return [
            pltpu.make_async_copy(src, dst.at[chunk], saves.at[kind, slot])
            for kind, (src, dst) in enumerate(pairs)
        ]

    def one_chunk(chunk, carry):
        slot = lax.rem(chunk, 2)

        @pl.when(chunk >= 2)
        def _():
            for copy in stores(chunk - 2, slot):
                copy.wait()

        todo = stores(chunk, slot)
        await_arrival(inbox.at[chunk], arrivals.at[chunk])
        todo[0].start()
        x = inbox[chunk].astype(F32)
        x = x - centered * row_mean(x)
        na = (x * lax.rsqrt(row_mean(x * x) + EPS) * gain_a[...]).astype(BF16)
        b_na[slot] = na
        todo[4].start()
        b_q[slot] = (dot(na, w_qkv[:, :D]).astype(BF16) * (HD**-0.5)).astype(BF16)
        here = pl.ds(pl.multiple_of((chunk + 2) * C, C), C)
        kbuf[here, :] = dot(na, w_qkv[:, D : 2 * D]).astype(BF16)
        vbuf[here, :] = dot(na, w_qkv[:, 2 * D :]).astype(BF16)
        todo[1].start()
        todo[2].start()
        todo[3].start()
        for part in range(WIN):
            allowed = doc_q[chunk] == doc_k[chunk + part]
            if part == WIN - 1:
                row = lax.broadcasted_iota(jnp.int32, (C, C), 0)
                col = lax.broadcasted_iota(jnp.int32, (C, C), 1)
                allowed = allowed & (col <= row)
            bias[:, part * C : (part + 1) * C] = jnp.where(allowed, 0.0, NEG)
        window = pl.ds(pl.multiple_of(chunk * C, C), WIN * C)
        lane = lax.broadcasted_iota(jnp.int32, (1, 128), 1)
        lse_all = jnp.zeros((C, 128), F32)
        for pair in range(PAIRS):
            lanes = slice(pair * 2 * HD, (pair + 1) * 2 * HD)
            q2 = two_heads(b_q[slot, :, lanes], low, high)
            s = dot_nt(q2, kbuf[window, lanes]).reshape(2, C, WIN * C) + bias[...][None]
            top = jnp.max(s, axis=-1, keepdims=True)
            e = jnp.exp(s - top)
            total = jnp.sum(e, axis=-1, keepdims=True)
            o = dot(e.astype(BF16).reshape(2 * C, WIN * C), vbuf[window, lanes])
            o = o.reshape(2, C, 2 * HD) * (1.0 / total)
            b_mixed[slot, :, lanes] = jnp.where(is_low, o[0], o[1]).astype(BF16)
            lse = top + jnp.log(total)
            lse_all = jnp.where(lane == 2 * pair, lse[0], lse_all)
            lse_all = jnp.where(lane == 2 * pair + 1, lse[1], lse_all)
        b_lse[slot] = jnp.transpose(lse_all)[:16]
        todo[5].start()
        todo[6].start()
        branch = dot(b_mixed[slot], w_out[...])
        mid = x + branch - row_mean(branch)
        b_mid[slot] = mid
        todo[7].start()
        nm = (mid * lax.rsqrt(row_mean(mid * mid) + EPS) * gain_m[...]).astype(BF16)
        b_nm[slot] = nm
        todo[8].start()
        k0 = 0.7978845608028654
        k1 = 0.044715
        for part in range(FF // D):
            cols = slice(part * D, (part + 1) * D)
            h = dot(nm, w_up[:, cols])
            h2 = h * h
            t = jnp.tanh(h * (k0 + (k0 * k1) * h2))
            half = 0.5 + 0.5 * t
            b_act[slot, :, cols] = (h * half).astype(BF16)
            slope = half + (h * (1.0 - t * t)) * (0.5 * k0 + (1.5 * k0 * k1) * h2)
            b_dg[slot, :, cols] = slope.astype(BF16)
        todo[9].start()
        todo[10].start()
        branch = dot(b_act[slot], w_down[...])
        outbox[chunk] = (b_mid[slot] + branch - row_mean(branch)).astype(BF16)
        pass_on(section, chunk, per, sections - 1, 1, outbox, inbox, result, sends, arrivals, landed, kept)
        return carry

    lax.fori_loop(0, chunks, one_chunk, 0)
    for chunk in (chunks - 2, chunks - 1):
        for copy in stores(chunk, chunk % 2):
            copy.wait()
    drain_rows(section, sections, per, tokens, first_sends, 0)
    settle(section, chunks, per, sections - 1, outbox, result, sends, landed, kept)


def backward_kernel(
    sections,
    cotangent,
    doc_qr,
    doc_kc,
    gain_a,
    gain_m,
    w_qkv,
    w_out,
    w_up,
    w_down,
    s_x,
    s_q,
    s_k,
    s_v,
    s_mixed,
    s_lse,
    s_mid,
    s_dg,
    result,
    gains,
    s_db,
    s_dh,
    s_da,
    s_dt,
    inbox,
    outbox,
    kbuf,
    vbuf,
    bias,
    dk_acc,
    dv_acc,
    lse_d,
    marks,
    b_x,
    b_q,
    b_mixed,
    b_lse,
    b_mid,
    b_dg,
    b_db,
    b_dh,
    b_da,
    b_dt,
    arrivals,
    sends,
    first_sends,
    landed,
    kept,
    loads,
    saves,
    kv_sems,
):
    section = lax.axis_index("section")
    chunks = inbox.shape[0]
    per = cotangent.shape[0]
    last = sections - 1

    def fetches(chunk, slot):
        pairs = (
            (s_dg, b_dg),
            (s_mid, b_mid),
            (s_mixed, b_mixed),
            (s_q, b_q),
            (s_lse, b_lse),
            (s_x, b_x),
        )
        return [
            pltpu.make_async_copy(src.at[chunk], dst.at[slot], loads.at[kind, slot])
            for kind, (src, dst) in enumerate(pairs)
        ]

    def stores(chunk, slot):
        pairs = ((b_db, s_db), (b_dh, s_dh), (b_da, s_da), (b_dt, s_dt))
        return [
            pltpu.make_async_copy(src.at[slot], dst.at[chunk], saves.at[kind, slot])
            for kind, (src, dst) in enumerate(pairs)
        ]

    kv_copies = [
        pltpu.make_async_copy(s_k, kbuf.at[pl.ds(2 * C, chunks * C)], kv_sems.at[0]),
        pltpu.make_async_copy(s_v, vbuf.at[pl.ds(2 * C, chunks * C)], kv_sems.at[1]),
    ]
    for copy in fetches(chunks - 1, 0):
        copy.start()
    for copy in kv_copies:
        copy.start()
    greet(section, sections)
    scatter_rows(section, sections, per, cotangent, inbox, arrivals, first_sends, last)
    low, high, _ = lane_masks()
    kbuf[pl.ds(0, 2 * C), :] = jnp.zeros((2 * C, D), BF16)
    vbuf[pl.ds(0, 2 * C), :] = jnp.zeros((2 * C, D), BF16)
    dk_acc[...] = jnp.zeros_like(dk_acc)
    dv_acc[...] = jnp.zeros_like(dv_acc)
    gains[...] = jnp.zeros_like(gains)
    owner_of = lax.broadcasted_iota(jnp.int32, (D, 128), 0) // HD
    marks[...] = (owner_of == lax.broadcasted_iota(jnp.int32, (D, 128), 1)).astype(F32).astype(BF16)
    centered = jnp.where(section == 0, 1.0, 0.0).astype(F32)
    for copy in kv_copies:
        copy.wait()

    def folded(v):
        return jnp.sum(v.reshape(C // 8, 8, D), axis=0)

    def one_chunk(step, carry):
        chunk = chunks - 1 - step
        slot = lax.rem(step, 2)

        @pl.when(step + 1 < chunks)
        def _():
            for copy in fetches(chunk - 1, 1 - slot):
                copy.start()

        @pl.when(step >= 2)
        def _():
            for copy in stores(chunk + 2, slot):
                copy.wait()

        for copy in fetches(chunk, slot):
            copy.wait()
        todo = stores(chunk, slot)
        await_arrival(inbox.at[chunk], arrivals.at[chunk])
        g = inbox[chunk].astype(F32)
        db = (g - row_mean(g)).astype(BF16)
        b_db[slot] = db
        todo[0].start()
        for part in range(FF // D):
            cols = slice(part * D, (part + 1) * D)
            d_active = dot_nt(db, w_down[cols, :])
            b_dh[slot, :, cols] = (d_active * b_dg[slot, :, cols].astype(F32)).astype(BF16)
        todo[1].start()
        dn = dot_nt(b_dh[slot], w_up[...])
        mid = b_mid[slot]
        factor = lax.rsqrt(row_mean(mid * mid) + EPS)
        unit = mid * factor
        gains[1] += folded(dn * unit)
        dn = dn * gain_m[...]
        d_mid = g + factor * (dn - unit * row_mean(dn * unit))
        da = (d_mid - row_mean(d_mid)).astype(BF16)
        b_da[slot] = da
        todo[2].start()
        b_mid[slot] = d_mid
        dmix = dot_nt(da, w_out[...]).astype(BF16)
        prod = dmix.astype(F32) * b_mixed[slot].astype(F32)
        top = prod.astype(BF16)
        rest = (prod - top.astype(F32)).astype(BF16)
        inner = dot(top, marks[...]) + dot(rest, marks[...])
        lse_d[...] = jnp.transpose(inner)[:16]
        for part in range(WIN):
            allowed = doc_kc[chunk + part] == doc_qr[chunk]
            if part == WIN - 1:
                key = lax.broadcasted_iota(jnp.int32, (C, C), 0)
                query = lax.broadcasted_iota(jnp.int32, (C, C), 1)
                allowed = allowed & (key <= query)
            bias[part * C : (part + 1) * C, :] = jnp.where(allowed, 0.0, NEG)
        window = pl.ds(pl.multiple_of(chunk * C, C), WIN * C)
        for pair in range(PAIRS):
            lanes = slice(pair * 2 * HD, (pair + 1) * 2 * HD)
            q2 = two_heads(b_q[slot, :, lanes], low, high)
            do2 = two_heads(dmix[:, lanes], low, high)
            keys = kbuf[window, lanes]
            values = vbuf[window, lanes]
            both = jnp.concatenate([bias[...], bias[...]], axis=1)
            lse = jnp.concatenate(
                [b_lse[slot, 2 * pair : 2 * pair + 1, :], b_lse[slot, 2 * pair + 1 : 2 * pair + 2, :]], axis=1
            )
            inner = jnp.concatenate(
                [lse_d[2 * pair : 2 * pair + 1, :], lse_d[2 * pair + 1 : 2 * pair + 2, :]], axis=1
            )
            probs = jnp.exp(dot_nt(keys, q2) + both - lse)
            ds = (probs * (dot_nt(values, do2) - inner)).astype(BF16)
            dv = dot(probs.astype(BF16), do2)
            dk = dot(ds, q2)
            for part in range(WIN):
                place = lax.rem(chunk + part, WIN)
                rows = slice(part * C, (part + 1) * C)
                dv_acc[place, :, lanes] += dv[rows]
                dk_acc[place, :, lanes] += dk[rows]
            dq = dot(jnp.transpose(keys), ds)
            dq = jnp.concatenate([dq[:HD, :C], dq[HD:, C:]], axis=0)
            b_dt[slot, :, lanes] = (jnp.transpose(dq) * (HD**-0.5)).astype(BF16)
        done = lax.rem(chunk + WIN - 1, WIN)
        b_dt[slot, :, D : 2 * D] = dk_acc[done].astype(BF16)
        b_dt[slot, :, 2 * D :] = dv_acc[done].astype(BF16)
        dk_acc[done] = jnp.zeros((C, D), F32)
        dv_acc[done] = jnp.zeros((C, D), F32)
        todo[3].start()
        dn = dot_nt(b_dt[slot], w_qkv[...])
        x = b_x[slot].astype(F32)
        x = x - centered * row_mean(x)
        factor = lax.rsqrt(row_mean(x * x) + EPS)
        unit = x * factor
        gains[0] += folded(dn * unit)
        dn = dn * gain_a[...]
        grad = b_mid[slot] + factor * (dn - unit * row_mean(dn * unit))
        grad = grad - centered * row_mean(grad)
        outbox[chunk] = grad.astype(BF16)
        pass_on(section, chunk, per, 0, -1, outbox, inbox, result, sends, arrivals, landed, kept)
        return carry

    lax.fori_loop(0, chunks, one_chunk, 0)
    for step in (chunks - 2, chunks - 1):
        for copy in stores(chunks - 1 - step, step % 2):
            copy.wait()
    drain_rows(section, sections, per, cotangent, first_sends, last)
    settle(section, chunks, per, 0, outbox, result, sends, landed, kept)


ANY = pl.BlockSpec(memory_space=pl.ANY)
IN_VMEM = pl.BlockSpec(memory_space=pltpu.VMEM)
DMA = pltpu.SemaphoreType.DMA


def forward(sections, chunks, tokens, doc_q, doc_k, weights):
    per = chunks // sections
    sds = jax.ShapeDtypeStruct
    saved = (
        ("x", (C, D), BF16),
        ("q", (C, D), BF16),
        ("k", (C, D), BF16),
        ("v", (C, D), BF16),
        ("na", (C, D), BF16),
        ("mixed", (C, D), BF16),
        ("lse", (16, C), F32),
        ("mid", (C, D), F32),
        ("nm", (C, D), BF16),
        ("act", (C, FF), BF16),
        ("dg", (C, FF), BF16),
    )
    staged = [entry for entry in saved if entry[0] not in ("x", "k", "v")]
    outs = pl.pallas_call(
        functools.partial(forward_kernel, sections),
        out_shape=[sds((per, C, D), BF16)] + [sds((chunks,) + s, t) for _, s, t in saved],
        in_specs=[ANY] + [IN_VMEM] * 8,
        out_specs=[ANY] * (1 + len(saved)),
        scratch_shapes=[
            pltpu.VMEM((chunks, C, D), BF16),
            pltpu.VMEM((chunks, C, D), BF16),
            pltpu.VMEM(((chunks + 2) * C, D), BF16),
            pltpu.VMEM(((chunks + 2) * C, D), BF16),
            pltpu.VMEM((C, WIN * C), F32),
        ]
        + [pltpu.VMEM((2,) + s, t) for _, s, t in staged]
        + [DMA((chunks,)), DMA((chunks,)), DMA((per,)), DMA((per,)), DMA((per,)), DMA((11, 2))],
        compiler_params=pltpu.CompilerParams(
            collective_id=0, has_side_effects=True, vmem_limit_bytes=VMEM_LIMIT
        ),
        name="layer_forward",
    )(tokens.reshape(per, C, D), doc_q, doc_k, *weights)
    return outs[0], {name: out for (name, _, _), out in zip(saved, outs[1:])}


def backward(sections, chunks, cotangent, doc_qr, doc_kc, weights, kept):
    per = chunks // sections
    sds = jax.ShapeDtypeStruct
    fetched = (
        ((C, D), BF16),
        ((C, D), BF16),
        ((C, D), BF16),
        ((16, C), F32),
        ((C, D), F32),
        ((C, FF), BF16),
    )
    saved = ((C, D), (C, FF), (C, D), (C, 3 * D))
    outs = pl.pallas_call(
        functools.partial(backward_kernel, sections),
        out_shape=[sds((per, C, D), BF16), sds((2, 8, D), F32)] + [sds((chunks,) + s, BF16) for s in saved],
        in_specs=[ANY] + [IN_VMEM] * 8 + [ANY] * 8,
        out_specs=[ANY, IN_VMEM] + [ANY] * len(saved),
        scratch_shapes=[
            pltpu.VMEM((chunks, C, D), BF16),
            pltpu.VMEM((chunks, C, D), BF16),
            pltpu.VMEM(((chunks + 2) * C, D), BF16),
            pltpu.VMEM(((chunks + 2) * C, D), BF16),
            pltpu.VMEM((WIN * C, C), F32),
            pltpu.VMEM((WIN, C, D), F32),
            pltpu.VMEM((WIN, C, D), F32),
            pltpu.VMEM((16, C), F32),
            pltpu.VMEM((D, 128), BF16),
        ]
        + [pltpu.VMEM((2,) + s, t) for s, t in fetched]
        + [pltpu.VMEM((2,) + s, BF16) for s in saved]
        + [DMA((chunks,)), DMA((chunks,)), DMA((per,)), DMA((per,)), DMA((per,))]
        + [DMA((6, 2)), DMA((4, 2)), DMA((2,))],
        compiler_params=pltpu.CompilerParams(
            collective_id=1, has_side_effects=True, vmem_limit_bytes=VMEM_LIMIT
        ),
        name="layer_backward",
    )(
        cotangent.reshape(per, C, D),
        doc_qr,
        doc_kc,
        *weights,
        kept["x"],
        kept["q"],
        kept["k"].reshape(chunks * C, D),
        kept["v"].reshape(chunks * C, D),
        kept["mixed"],
        kept["lse"],
        kept["mid"],
        kept["dg"],
    )
    return outs


def matmul_lt(left_side, right_side):
    rows = left_side.shape[0] * left_side.shape[1]
    return lax.dot_general(
        left_side.reshape(rows, -1),
        right_side.reshape(rows, -1),
        (((0,), (0,)), ((), ())),
        preferred_element_type=F32,
    )


def body(tokens, cotangent, doc_ids, gain_attn, w_qkv, w_out, gain_mlp, w_up, w_down):
    sections = lax.axis_size("section")
    rows, seq = doc_ids.shape
    chunks = rows * seq // C
    docs = doc_ids + 1 + 16 * jnp.arange(rows, dtype=jnp.int32)[:, None]
    docs_q = docs.reshape(chunks, C)
    docs_k = jnp.concatenate([jnp.zeros((2, C), jnp.int32), docs_q])
    weights = (gain_attn, gain_mlp, w_qkv[0], w_out[0], w_up[0], w_down[0])
    output, kept = forward(sections, chunks, tokens, docs_q[:, :, None], docs_k[:, None, :], weights)
    input_grad, gains, db, dh, da, dt = backward(
        sections, chunks, cotangent, docs_q[:, None, :], docs_k[:, :, None], weights, kept
    )
    gains = jnp.sum(gains, axis=1)
    grads = (
        gains[0],
        matmul_lt(kept["na"], dt),
        matmul_lt(kept["mixed"], da),
        gains[1],
        matmul_lt(kept["nm"], dh),
        matmul_lt(kept["act"], db),
    )
    shards = lax.psum_scatter(grads, "dp", scatter_dimension=0, tiled=True)
    return (
        output.reshape(tokens.shape),
        input_grad.reshape(cotangent.shape),
        *(shard[None] for shard in shards),
    )


def solution(mesh):
    rows = P(("dp", "section"), None)
    layer = P("section", None)
    matrix = P("section", None, None)
    in_specs = (rows, rows, P("dp", None), layer, matrix, matrix, layer, matrix, matrix)
    split = P("section", "dp")
    split_matrix = P("section", "dp", None)
    out_specs = (rows, rows, split, split_matrix, split_matrix, split, split_matrix, split_matrix)
    return jax.shard_map(body, mesh=mesh, in_specs=in_specs, out_specs=out_specs, check_vma=False)
```

```python
import functools

import jax
import jax.numpy as jnp
from jax import lax
from jax.experimental import pallas as pl
from jax.experimental.pallas import tpu as pltpu
from jax.sharding import PartitionSpec as P

D = 768
HEADS = 12
HD = 64
FF = 3072
C = 256
WIN = 3
PAIRS = HEADS // 2
EPS = 1e-05
NEG = -1e30
MESH = pl.DeviceIdType.MESH
BF16 = jnp.bfloat16
F32 = jnp.float32
VMEM_LIMIT = 60 * 1024 * 1024


def dot(a, b):
    return jnp.dot(a, b, preferred_element_type=F32)


def dot_nt(a, b):
    return lax.dot_general(a, b, (((1,), (1,)), ((), ())), preferred_element_type=F32)


def row_mean(v):
    return jnp.mean(v, axis=-1, keepdims=True)


def greet(section, sections):
    dp = lax.axis_index("dp")
    barrier = pltpu.get_barrier_semaphore()
    for step in range(1, sections):
        other = lax.rem(section + step, sections)
        pl.semaphore_signal(barrier, inc=1, device_id=(dp, other), device_id_type=MESH)
    pl.semaphore_wait(barrier, sections - 1)


def lane_masks():
    lane = lax.broadcasted_iota(jnp.int32, (1, 2 * HD), 1)
    low = (lane < HD).astype(F32)
    return low.astype(BF16), (1.0 - low).astype(BF16), lane < HD


def two_heads(pair, low, high):
    return jnp.concatenate([pair * low, pair * high], axis=0)


def await_arrival(buf, sem):
    pltpu.make_async_copy(buf, buf, sem).wait()


def scatter_rows(section, sections, per, rows, inbox, sems, send_sems, target):
    dp = lax.axis_index("dp")
    for piece in range(per):
        slot = section * per + piece

        @pl.when(section != target)
        def _():
            pltpu.make_async_remote_copy(
                rows.at[piece],
                inbox.at[slot],
                send_sems.at[piece],
                sems.at[slot],
                device_id=(dp, target),
                device_id_type=MESH,
            ).start()

        @pl.when(section == target)
        def _():
            pltpu.make_async_copy(rows.at[piece], inbox.at[slot], sems.at[slot]).start()


def drain_rows(section, sections, per, rows, send_sems, target):
    for piece in range(per):

        @pl.when(section != target)
        def _():
            pltpu.make_async_copy(rows.at[piece], rows.at[piece], send_sems.at[piece]).wait()


def pass_on(section, chunk, per, last, step, outbox, inbox, result, sends, arrivals, landed, kept):
    dp = lax.axis_index("dp")
    owner = chunk // per

    @pl.when(section != last)
    def _():
        pltpu.make_async_remote_copy(
            outbox.at[chunk],
            inbox.at[chunk],
            sends.at[chunk],
            arrivals.at[chunk],
            device_id=(dp, section + step),
            device_id_type=MESH,
        ).start()

    @pl.when((section == last) & (owner != last))
    def _():
        pltpu.make_async_remote_copy(
            outbox.at[chunk],
            result.at[lax.rem(chunk, per)],
            sends.at[chunk],
            landed.at[lax.rem(chunk, per)],
            device_id=(dp, owner),
            device_id_type=MESH,
        ).start()

    @pl.when((section == last) & (owner == last))
    def _():
        pltpu.make_async_copy(
            outbox.at[chunk], result.at[lax.rem(chunk, per)], kept.at[lax.rem(chunk, per)]
        ).start()


def settle(section, chunks, per, last, outbox, result, sends, landed, kept):
    def one(chunk, carry):
        @pl.when((section != last) | (chunk // per != last))
        def _():
            await_arrival(outbox.at[chunk], sends.at[chunk])

        return carry

    lax.fori_loop(0, chunks, one, 0)
    for piece in range(per):

        @pl.when(section != last)
        def _():
            await_arrival(result.at[piece], landed.at[piece])

        @pl.when(section == last)
        def _():
            await_arrival(result.at[piece], kept.at[piece])


def forward_kernel(
    sections,
    tokens,
    doc_q,
    doc_k,
    gain_a,
    gain_m,
    w_qkv,
    w_out,
    w_up,
    w_down,
    result,
    s_x,
    s_q,
    s_k,
    s_v,
    s_na,
    s_mixed,
    s_lse,
    s_mid,
    s_nm,
    s_act,
    s_dg,
    inbox,
    outbox,
    kbuf,
    vbuf,
    bias,
    b_q,
    b_na,
    b_mixed,
    b_lse,
    b_mid,
    b_nm,
    b_act,
    b_dg,
    arrivals,
    sends,
    first_sends,
    landed,
    kept,
    saves,
):
    section = lax.axis_index("section")
    chunks = inbox.shape[0]
    per = tokens.shape[0]
    greet(section, sections)
    scatter_rows(section, sections, per, tokens, inbox, arrivals, first_sends, 0)
    low, high, is_low = lane_masks()
    kbuf[pl.ds(0, 2 * C), :] = jnp.zeros((2 * C, D), BF16)
    vbuf[pl.ds(0, 2 * C), :] = jnp.zeros((2 * C, D), BF16)
    centered = jnp.where(section == 0, 1.0, 0.0).astype(F32)

    def stores(chunk, slot):
        here = pl.ds(pl.multiple_of((chunk + 2) * C, C), C)
        pairs = (
            (inbox.at[chunk], s_x),
            (kbuf.at[here], s_k),
            (vbuf.at[here], s_v),
            (b_q.at[slot], s_q),
            (b_na.at[slot], s_na),
            (b_mixed.at[slot], s_mixed),
            (b_lse.at[slot], s_lse),
            (b_mid.at[slot], s_mid),
            (b_nm.at[slot], s_nm),
            (b_act.at[slot], s_act),
            (b_dg.at[slot], s_dg),
        )
        return [
            pltpu.make_async_copy(src, dst.at[chunk], saves.at[kind, slot])
            for kind, (src, dst) in enumerate(pairs)
        ]

    def one_chunk(chunk, carry):
        slot = lax.rem(chunk, 2)

        @pl.when(chunk >= 2)
        def _():
            for copy in stores(chunk - 2, slot):
                copy.wait()

        todo = stores(chunk, slot)
        await_arrival(inbox.at[chunk], arrivals.at[chunk])
        todo[0].start()
        x = inbox[chunk].astype(F32)
        x = x - centered * row_mean(x)
        na = (x * lax.rsqrt(row_mean(x * x) + EPS) * gain_a[...]).astype(BF16)
        b_na[slot] = na
        todo[4].start()
        b_q[slot] = (dot(na, w_qkv[:, :D]).astype(BF16) * (HD**-0.5)).astype(BF16)
        here = pl.ds(pl.multiple_of((chunk + 2) * C, C), C)
        kbuf[here, :] = dot(na, w_qkv[:, D : 2 * D]).astype(BF16)
        vbuf[here, :] = dot(na, w_qkv[:, 2 * D :]).astype(BF16)
        todo[1].start()
        todo[2].start()
        todo[3].start()
        for part in range(WIN):
            allowed = doc_q[chunk] == doc_k[chunk + part]
            if part == WIN - 1:
                row = lax.broadcasted_iota(jnp.int32, (C, C), 0)
                col = lax.broadcasted_iota(jnp.int32, (C, C), 1)
                allowed = allowed & (col <= row)
            bias[:, part * C : (part + 1) * C] = jnp.where(allowed, 0.0, NEG)
        window = pl.ds(pl.multiple_of(chunk * C, C), WIN * C)
        lane = lax.broadcasted_iota(jnp.int32, (1, 128), 1)
        lse_all = jnp.zeros((C, 128), F32)
        for pair in range(PAIRS):
            lanes = slice(pair * 2 * HD, (pair + 1) * 2 * HD)
            q2 = two_heads(b_q[slot, :, lanes], low, high)
            s = dot_nt(q2, kbuf[window, lanes]).reshape(2, C, WIN * C) + bias[...][None]
            top = jnp.max(s, axis=-1, keepdims=True)
            e = jnp.exp(s - top)
            total = jnp.sum(e, axis=-1, keepdims=True)
            o = dot(e.astype(BF16).reshape(2 * C, WIN * C), vbuf[window, lanes])
            o = o.reshape(2, C, 2 * HD) * (1.0 / total)
            b_mixed[slot, :, lanes] = jnp.where(is_low, o[0], o[1]).astype(BF16)
            lse = top + jnp.log(total)
            lse_all = jnp.where(lane == 2 * pair, lse[0], lse_all)
            lse_all = jnp.where(lane == 2 * pair + 1, lse[1], lse_all)
        b_lse[slot] = jnp.transpose(lse_all)[:16]
        todo[5].start()
        todo[6].start()
        branch = dot(b_mixed[slot], w_out[...])
        mid = x + branch - row_mean(branch)
        b_mid[slot] = mid
        todo[7].start()
        nm = (mid * lax.rsqrt(row_mean(mid * mid) + EPS) * gain_m[...]).astype(BF16)
        b_nm[slot] = nm
        todo[8].start()
        k0 = 0.7978845608028654
        k1 = 0.044715
        for part in range(FF // D):
            cols = slice(part * D, (part + 1) * D)
            h = dot(nm, w_up[:, cols])
            h2 = h * h
            t = jnp.tanh(h * (k0 + (k0 * k1) * h2))
            half = 0.5 + 0.5 * t
            b_act[slot, :, cols] = (h * half).astype(BF16)
            slope = half + (h * (1.0 - t * t)) * (0.5 * k0 + (1.5 * k0 * k1) * h2)
            b_dg[slot, :, cols] = slope.astype(BF16)
        todo[9].start()
        todo[10].start()
        branch = dot(b_act[slot], w_down[...])
        outbox[chunk] = (b_mid[slot] + branch - row_mean(branch)).astype(BF16)
        pass_on(section, chunk, per, sections - 1, 1, outbox, inbox, result, sends, arrivals, landed, kept)
        return carry

    lax.fori_loop(0, chunks, one_chunk, 0)
    for chunk in (chunks - 2, chunks - 1):
        for copy in stores(chunk, chunk % 2):
            copy.wait()
    drain_rows(section, sections, per, tokens, first_sends, 0)
    settle(section, chunks, per, sections - 1, outbox, result, sends, landed, kept)


def backward_kernel(
    sections,
    cotangent,
    doc_qr,
    doc_kc,
    gain_a,
    gain_m,
    w_qkv,
    w_out,
    w_up,
    w_down,
    s_x,
    s_q,
    s_k,
    s_v,
    s_mixed,
    s_lse,
    s_mid,
    s_dg,
    result,
    gains,
    s_db,
    s_dh,
    s_da,
    s_dt,
    inbox,
    outbox,
    kbuf,
    vbuf,
    bias,
    dk_acc,
    dv_acc,
    lse_d,
    marks,
    b_x,
    b_q,
    b_mixed,
    b_lse,
    b_mid,
    b_dg,
    b_db,
    b_dh,
    b_da,
    b_dt,
    arrivals,
    sends,
    first_sends,
    landed,
    kept,
    loads,
    saves,
    kv_sems,
):
    section = lax.axis_index("section")
    chunks = inbox.shape[0]
    per = cotangent.shape[0]
    last = sections - 1

    def fetches(chunk, slot):
        pairs = (
            (s_dg, b_dg),
            (s_mid, b_mid),
            (s_mixed, b_mixed),
            (s_q, b_q),
            (s_lse, b_lse),
            (s_x, b_x),
        )
        return [
            pltpu.make_async_copy(src.at[chunk], dst.at[slot], loads.at[kind, slot])
            for kind, (src, dst) in enumerate(pairs)
        ]

    def stores(chunk, slot):
        pairs = ((b_db, s_db), (b_dh, s_dh), (b_da, s_da), (b_dt, s_dt))
        return [
            pltpu.make_async_copy(src.at[slot], dst.at[chunk], saves.at[kind, slot])
            for kind, (src, dst) in enumerate(pairs)
        ]

    kv_copies = [
        pltpu.make_async_copy(s_k, kbuf.at[pl.ds(2 * C, chunks * C)], kv_sems.at[0]),
        pltpu.make_async_copy(s_v, vbuf.at[pl.ds(2 * C, chunks * C)], kv_sems.at[1]),
    ]
    for copy in fetches(chunks - 1, 0):
        copy.start()
    for copy in kv_copies:
        copy.start()
    greet(section, sections)
    scatter_rows(section, sections, per, cotangent, inbox, arrivals, first_sends, last)
    low, high, _ = lane_masks()
    kbuf[pl.ds(0, 2 * C), :] = jnp.zeros((2 * C, D), BF16)
    vbuf[pl.ds(0, 2 * C), :] = jnp.zeros((2 * C, D), BF16)
    dk_acc[...] = jnp.zeros_like(dk_acc)
    dv_acc[...] = jnp.zeros_like(dv_acc)
    gains[...] = jnp.zeros_like(gains)
    owner_of = lax.broadcasted_iota(jnp.int32, (D, 128), 0) // HD
    marks[...] = (owner_of == lax.broadcasted_iota(jnp.int32, (D, 128), 1)).astype(F32).astype(BF16)
    centered = jnp.where(section == 0, 1.0, 0.0).astype(F32)
    for copy in kv_copies:
        copy.wait()

    def folded(v):
        return jnp.sum(v.reshape(C // 8, 8, D), axis=0)

    def one_chunk(step, carry):
        chunk = chunks - 1 - step
        slot = lax.rem(step, 2)

        @pl.when(step + 1 < chunks)
        def _():
            for copy in fetches(chunk - 1, 1 - slot):
                copy.start()

        @pl.when(step >= 2)
        def _():
            for copy in stores(chunk + 2, slot):
                copy.wait()

        for copy in fetches(chunk, slot):
            copy.wait()
        todo = stores(chunk, slot)
        await_arrival(inbox.at[chunk], arrivals.at[chunk])
        g = inbox[chunk].astype(F32)
        db = (g - row_mean(g)).astype(BF16)
        b_db[slot] = db
        todo[0].start()
        for part in range(FF // D):
            cols = slice(part * D, (part + 1) * D)
            d_active = dot_nt(db, w_down[cols, :])
            b_dh[slot, :, cols] = (d_active * b_dg[slot, :, cols].astype(F32)).astype(BF16)
        todo[1].start()
        dn = dot_nt(b_dh[slot], w_up[...])
        mid = b_mid[slot]
        factor = lax.rsqrt(row_mean(mid * mid) + EPS)
        unit = mid * factor
        gains[1] += folded(dn * unit)
        dn = dn * gain_m[...]
        d_mid = g + factor * (dn - unit * row_mean(dn * unit))
        da = (d_mid - row_mean(d_mid)).astype(BF16)
        b_da[slot] = da
        todo[2].start()
        b_mid[slot] = d_mid
        dmix = dot_nt(da, w_out[...]).astype(BF16)
        prod = dmix.astype(F32) * b_mixed[slot].astype(F32)
        top = prod.astype(BF16)
        rest = (prod - top.astype(F32)).astype(BF16)
        inner = dot(top, marks[...]) + dot(rest, marks[...])
        lse_d[...] = jnp.transpose(inner)[:16]
        for part in range(WIN):
            allowed = doc_kc[chunk + part] == doc_qr[chunk]
            if part == WIN - 1:
                key = lax.broadcasted_iota(jnp.int32, (C, C), 0)
                query = lax.broadcasted_iota(jnp.int32, (C, C), 1)
                allowed = allowed & (key <= query)
            bias[part * C : (part + 1) * C, :] = jnp.where(allowed, 0.0, NEG)
        window = pl.ds(pl.multiple_of(chunk * C, C), WIN * C)
        for pair in range(PAIRS):
            lanes = slice(pair * 2 * HD, (pair + 1) * 2 * HD)
            q2 = two_heads(b_q[slot, :, lanes], low, high)
            do2 = two_heads(dmix[:, lanes], low, high)
            keys = kbuf[window, lanes]
            values = vbuf[window, lanes]
            both = jnp.concatenate([bias[...], bias[...]], axis=1)
            lse = jnp.concatenate(
                [b_lse[slot, 2 * pair : 2 * pair + 1, :], b_lse[slot, 2 * pair + 1 : 2 * pair + 2, :]], axis=1
            )
            inner = jnp.concatenate(
                [lse_d[2 * pair : 2 * pair + 1, :], lse_d[2 * pair + 1 : 2 * pair + 2, :]], axis=1
            )
            probs = jnp.exp(dot_nt(keys, q2) + both - lse)
            ds = (probs * (dot_nt(values, do2) - inner)).astype(BF16)
            dv = dot(probs.astype(BF16), do2)
            dk = dot(ds, q2)
            for part in range(WIN):
                place = lax.rem(chunk + part, WIN)
                rows = slice(part * C, (part + 1) * C)
                dv_acc[place, :, lanes] += dv[rows]
                dk_acc[place, :, lanes] += dk[rows]
            dq = dot(jnp.transpose(keys), ds)
            dq = jnp.concatenate([dq[:HD, :C], dq[HD:, C:]], axis=0)
            b_dt[slot, :, lanes] = (jnp.transpose(dq) * (HD**-0.5)).astype(BF16)
        done = lax.rem(chunk + WIN - 1, WIN)
        b_dt[slot, :, D : 2 * D] = dk_acc[done].astype(BF16)
        b_dt[slot, :, 2 * D :] = dv_acc[done].astype(BF16)
        dk_acc[done] = jnp.zeros((C, D), F32)
        dv_acc[done] = jnp.zeros((C, D), F32)
        todo[3].start()
        dn = dot_nt(b_dt[slot], w_qkv[...])
        x = b_x[slot].astype(F32)
        x = x - centered * row_mean(x)
        factor = lax.rsqrt(row_mean(x * x) + EPS)
        unit = x * factor
        gains[0] += folded(dn * unit)
        dn = dn * gain_a[...]
        grad = b_mid[slot] + factor * (dn - unit * row_mean(dn * unit))
        grad = grad - centered * row_mean(grad)
        outbox[chunk] = grad.astype(BF16)
        pass_on(section, chunk, per, 0, -1, outbox, inbox, result, sends, arrivals, landed, kept)
        return carry

    lax.fori_loop(0, chunks, one_chunk, 0)
    for step in (chunks - 2, chunks - 1):
        for copy in stores(chunks - 1 - step, step % 2):
            copy.wait()
    drain_rows(section, sections, per, cotangent, first_sends, last)
    settle(section, chunks, per, 0, outbox, result, sends, landed, kept)


ANY = pl.BlockSpec(memory_space=pl.ANY)
IN_VMEM = pl.BlockSpec(memory_space=pltpu.VMEM)
DMA = pltpu.SemaphoreType.DMA


def forward(sections, chunks, tokens, doc_q, doc_k, weights):
    per = chunks // sections
    sds = jax.ShapeDtypeStruct
    saved = (
        ("x", (C, D), BF16),
        ("q", (C, D), BF16),
        ("k", (C, D), BF16),
        ("v", (C, D), BF16),
        ("na", (C, D), BF16),
        ("mixed", (C, D), BF16),
        ("lse", (16, C), F32),
        ("mid", (C, D), F32),
        ("nm", (C, D), BF16),
        ("act", (C, FF), BF16),
        ("dg", (C, FF), BF16),
    )
    staged = [entry for entry in saved if entry[0] not in ("x", "k", "v")]
    outs = pl.pallas_call(
        functools.partial(forward_kernel, sections),
        out_shape=[sds((per, C, D), BF16)] + [sds((chunks,) + s, t) for _, s, t in saved],
        in_specs=[ANY] + [IN_VMEM] * 8,
        out_specs=[ANY] * (1 + len(saved)),
        scratch_shapes=[
            pltpu.VMEM((chunks, C, D), BF16),
            pltpu.VMEM((chunks, C, D), BF16),
            pltpu.VMEM(((chunks + 2) * C, D), BF16),
            pltpu.VMEM(((chunks + 2) * C, D), BF16),
            pltpu.VMEM((C, WIN * C), F32),
        ]
        + [pltpu.VMEM((2,) + s, t) for _, s, t in staged]
        + [DMA((chunks,)), DMA((chunks,)), DMA((per,)), DMA((per,)), DMA((per,)), DMA((11, 2))],
        compiler_params=pltpu.CompilerParams(
            collective_id=0, has_side_effects=True, vmem_limit_bytes=VMEM_LIMIT
        ),
        name="layer_forward",
    )(tokens.reshape(per, C, D), doc_q, doc_k, *weights)
    return outs[0], {name: out for (name, _, _), out in zip(saved, outs[1:])}


def backward(sections, chunks, cotangent, doc_qr, doc_kc, weights, kept):
    per = chunks // sections
    sds = jax.ShapeDtypeStruct
    fetched = (
        ((C, D), BF16),
        ((C, D), BF16),
        ((C, D), BF16),
        ((16, C), F32),
        ((C, D), F32),
        ((C, FF), BF16),
    )
    saved = ((C, D), (C, FF), (C, D), (C, 3 * D))
    outs = pl.pallas_call(
        functools.partial(backward_kernel, sections),
        out_shape=[sds((per, C, D), BF16), sds((2, 8, D), F32)] + [sds((chunks,) + s, BF16) for s in saved],
        in_specs=[ANY] + [IN_VMEM] * 8 + [ANY] * 8,
        out_specs=[ANY, IN_VMEM] + [ANY] * len(saved),
        scratch_shapes=[
            pltpu.VMEM((chunks, C, D), BF16),
            pltpu.VMEM((chunks, C, D), BF16),
            pltpu.VMEM(((chunks + 2) * C, D), BF16),
            pltpu.VMEM(((chunks + 2) * C, D), BF16),
            pltpu.VMEM((WIN * C, C), F32),
            pltpu.VMEM((WIN, C, D), F32),
            pltpu.VMEM((WIN, C, D), F32),
            pltpu.VMEM((16, C), F32),
            pltpu.VMEM((D, 128), BF16),
        ]
        + [pltpu.VMEM((2,) + s, t) for s, t in fetched]
        + [pltpu.VMEM((2,) + s, BF16) for s in saved]
        + [DMA((chunks,)), DMA((chunks,)), DMA((per,)), DMA((per,)), DMA((per,))]
        + [DMA((6, 2)), DMA((4, 2)), DMA((2,))],
        compiler_params=pltpu.CompilerParams(
            collective_id=1, has_side_effects=True, vmem_limit_bytes=VMEM_LIMIT
        ),
        name="layer_backward",
    )(
        cotangent.reshape(per, C, D),
        doc_qr,
        doc_kc,
        *weights,
        kept["x"],
        kept["q"],
        kept["k"].reshape(chunks * C, D),
        kept["v"].reshape(chunks * C, D),
        kept["mixed"],
        kept["lse"],
        kept["mid"],
        kept["dg"],
    )
    return outs


def matmul_lt(left_side, right_side):
    rows = left_side.shape[0] * left_side.shape[1]
    return lax.dot_general(
        left_side.reshape(rows, -1),
        right_side.reshape(rows, -1),
        (((0,), (0,)), ((), ())),
        preferred_element_type=F32,
    )


UNIT = 256
UNITS = 9 + 3 + 12 + 12
NARROW = 9 + 3 + 12
X_LAG = 4
Z_LAG = 6


def dot_tn(a, b):
    return lax.dot_general(a, b, (((0,), (0,)), ((), ())), preferred_element_type=F32)


def weight_grad_kernel(
    s_na,
    s_dt,
    s_mixed,
    s_da,
    s_nm,
    s_dh,
    s_act,
    s_db,
    gains,
    o_qkv,
    o_out,
    o_up,
    o_down,
    o_gains,
    left,
    right,
    act,
    made,
    from_x,
    from_z,
    total,
    gain_own,
    gain_in,
    left_sems,
    right_sems,
    act_sem,
    x_sends,
    x_arrivals,
    z_sends,
    z_arrivals,
    out_sem,
    gain_sends,
    gain_arrivals,
):
    section = lax.axis_index("section")
    dp = lax.axis_index("dp")
    x, z = lax.rem(dp, 2), dp // 2
    partner = dp + 1 - 2 * x

    def load_left(src, slot):
        return pltpu.make_async_copy(src, left.at[slot], left_sems.at[slot])

    def load_right(src, column, slot):
        columns = pl.ds(pl.multiple_of(column * UNIT, UNIT), UNIT)
        return pltpu.make_async_copy(src.at[:, columns], right.at[slot], right_sems.at[slot])

    def start_right(unit):
        slot = lax.rem(unit, 2)

        @pl.when(unit < 9)
        def _():
            load_right(s_dt, unit, slot).start()

        @pl.when((unit >= 9) & (unit < 12))
        def _():
            load_right(s_da, unit - 9, slot).start()

        @pl.when((unit >= 12) & (unit < NARROW))
        def _():
            load_right(s_dh, unit - 12, slot).start()

    load_left(s_na, 0).start()
    start_right(0)
    load_left(s_mixed, 1).start()
    pltpu.make_async_copy(s_act, act, act_sem).start()
    gain_own[...] = jnp.sum(gains[...], axis=1, keepdims=True) + jnp.zeros((2, 8, D), F32)

    barrier = pltpu.get_barrier_semaphore()
    for step in range(1, 8):
        other = lax.rem(dp + step, 8)
        pl.semaphore_signal(barrier, inc=1, device_id=(other, section), device_id_type=MESH)
    pl.semaphore_wait(barrier, 7)

    def gain_copy(step):
        other = lax.rem(dp + step, 8)
        return pltpu.make_async_remote_copy(
            gain_own,
            gain_in.at[step - 1],
            gain_sends.at[step - 1],
            gain_arrivals.at[step - 1],
            device_id=(other, section),
            device_id_type=MESH,
        )

    for step in range(1, 8):
        gain_copy(step).start()

    def send_x(unit):
        pltpu.make_async_remote_copy(
            made.at[unit, 1 - x],
            from_x.at[unit],
            x_sends.at[unit],
            x_arrivals.at[unit],
            device_id=(partner, section),
            device_id_type=MESH,
        ).start()

    def send_z(unit, step):
        target = lax.rem(z + step, 4)
        pltpu.make_async_remote_copy(
            made.at[unit, x, target],
            from_z.at[unit, 3 - step],
            z_sends.at[unit],
            z_arrivals.at[unit],
            device_id=(target * 2 + x, section),
            device_id_type=MESH,
        ).start()

    def deliver(unit):
        for first, end, ref in ((0, 9, o_qkv), (9, 12, o_out), (12, NARROW, o_up)):

            @pl.when((unit >= first) & (unit < end))
            def _():
                columns = pl.ds(pl.multiple_of((unit - first) * UNIT, UNIT), UNIT)
                pltpu.make_async_copy(total.at[unit], ref.at[:, columns], out_sem).start()

        @pl.when(unit >= NARROW)
        def _():
            column, row = (unit - NARROW) // 4, lax.rem(unit - NARROW, 4)
            columns = pl.ds(pl.multiple_of(column * UNIT, UNIT), UNIT)
            rows = pl.ds(pl.multiple_of(row * 96, 96), 96)
            pltpu.make_async_copy(total.at[unit], o_down.at[rows, columns], out_sem).start()

    def advance(now):
        @pl.when((now >= X_LAG) & (now - X_LAG < UNITS))
        def _():
            unit = now - X_LAG
            await_arrival(from_x.at[unit], x_arrivals.at[unit])
            made[unit, x] = (made[unit, x].astype(F32) + from_x[unit].astype(F32)).astype(BF16)
            for step in range(1, 4):
                send_z(unit, step)

        @pl.when((now >= Z_LAG) & (now - Z_LAG < UNITS))
        def _():
            unit = now - Z_LAG
            await_arrival(from_z.at[unit], z_arrivals.at[unit])
            got = from_z[unit].astype(F32)
            total[unit] = made[unit, x, z].astype(F32) + got[0] + got[1] + got[2]
            deliver(unit)

    def narrow(unit, carry):
        slot = lax.rem(unit, 2)
        side = jnp.where((unit >= 9) & (unit < 12), 1, 0)

        @pl.when(unit == 9)
        def _():
            load_left(s_nm, 0).start()

        @pl.when(unit == 12)
        def _():
            load_left(s_db, 1).start()

        start_right(unit + 1)

        @pl.when((unit == 0) | (unit == 12))
        def _():
            load_left(s_na, 0).wait()

        @pl.when(unit == 9)
        def _():
            load_left(s_mixed, 1).wait()

        load_right(s_dt, 0, slot).wait()
        grad = dot_tn(left[side], right[slot]).astype(BF16)
        for shard in range(8):
            made[unit, shard % 2, shard // 2] = grad[shard * 96 : (shard + 1) * 96]
        send_x(unit)
        advance(unit)
        return carry

    lax.fori_loop(0, NARROW, narrow, 0)
    load_left(s_db, 1).wait()
    pltpu.make_async_copy(s_act, act, act_sem).wait()

    def wide(step, carry):
        column, shard = step // 8, lax.rem(step, 8)
        columns = pl.ds(pl.multiple_of(column * UNIT, UNIT), UNIT)
        rows = pl.ds(pl.multiple_of(shard * 384, 384), 384)
        grad = dot_tn(act[:, rows], left[1, :, columns]).astype(BF16)
        first = NARROW + 4 * column
        for part in range(4):
            made[first + part, lax.rem(shard, 2), shard // 2] = grad[part * 96 : (part + 1) * 96]

        @pl.when(shard == 7)
        def _():
            for part in range(4):
                send_x(first + part)

        @pl.when(lax.rem(step, 2) == 1)
        def _():
            advance(NARROW + step // 2)

        return carry

    lax.fori_loop(0, 24, wide, 0)

    def drain(now, carry):
        advance(now)
        return carry

    lax.fori_loop(UNITS, UNITS + Z_LAG, drain, 0)
    for step in range(1, 8):
        gain_copy(step).wait()
    sums = gain_own[:, 0:1]
    for step in range(7):
        sums = sums + gain_in[step, :, 0:1]
    o_gains[...] = sums

    def sent(unit, carry):
        await_arrival(from_x.at[unit], x_sends.at[unit])
        await_arrival(from_z.at[unit], z_sends.at[unit])
        return carry

    lax.fori_loop(0, UNITS, sent, 0)
    await_arrival(total, out_sem)


def weight_grads(na, dt, mixed, da, nm, dh, act, db, gains):
    tokens = na.shape[0] * na.shape[1]
    sds = jax.ShapeDtypeStruct
    operands = [v.reshape(tokens, -1) for v in (na, dt, mixed, da, nm, dh, act, db)]
    return pl.pallas_call(
        weight_grad_kernel,
        out_shape=[
            sds((96, 3 * D), F32),
            sds((96, D), F32),
            sds((96, FF), F32),
            sds((384, D), F32),
            sds((2, 1, D), F32),
        ],
        in_specs=[ANY] * 8 + [IN_VMEM],
        out_specs=[ANY] * 4 + [IN_VMEM],
        scratch_shapes=[
            pltpu.VMEM((2, tokens, D), BF16),
            pltpu.VMEM((2, tokens, UNIT), BF16),
            pltpu.VMEM((tokens, FF), BF16),
            pltpu.VMEM((UNITS, 2, 4, 96, UNIT), BF16),
            pltpu.VMEM((UNITS, 4, 96, UNIT), BF16),
            pltpu.VMEM((UNITS, 3, 96, UNIT), BF16),
            pltpu.VMEM((UNITS, 96, UNIT), F32),
            pltpu.VMEM((2, 8, D), F32),
            pltpu.VMEM((7, 2, 8, D), F32),
            DMA((2,)),
            DMA((2,)),
            DMA,
            DMA((UNITS,)),
            DMA((UNITS,)),
            DMA((UNITS,)),
            DMA((UNITS,)),
            DMA,
            DMA((7,)),
            DMA((7,)),
        ],
        compiler_params=pltpu.CompilerParams(
            collective_id=2, has_side_effects=True, vmem_limit_bytes=VMEM_LIMIT
        ),
        name="weight_grads",
    )(*operands, gains)


def body(tokens, cotangent, doc_ids, gain_attn, w_qkv, w_out, gain_mlp, w_up, w_down):
    sections = lax.axis_size("section")
    rows, seq = doc_ids.shape
    chunks = rows * seq // C
    docs = doc_ids + 1 + 16 * jnp.arange(rows, dtype=jnp.int32)[:, None]
    docs_q = docs.reshape(chunks, C)
    docs_k = jnp.concatenate([jnp.zeros((2, C), jnp.int32), docs_q])
    weights = (gain_attn, gain_mlp, w_qkv[0], w_out[0], w_up[0], w_down[0])
    output, kept = forward(sections, chunks, tokens, docs_q[:, :, None], docs_k[:, None, :], weights)
    input_grad, gains, db, dh, da, dt = backward(
        sections, chunks, cotangent, docs_q[:, None, :], docs_k[:, :, None], weights, kept
    )
    if lax.axis_size("dp") == 8 and chunks == 8:
        qkv, out, up, down, gains = weight_grads(
            kept["na"], dt, kept["mixed"], da, kept["nm"], dh, kept["act"], db, gains
        )
        gains = lax.dynamic_slice(gains, (0, 0, lax.axis_index("dp") * 96), (2, 1, 96))
        shards = (gains[0, 0], qkv, out, gains[1, 0], up, down)
    else:
        gains = jnp.sum(gains, axis=1)
        grads = (
            gains[0],
            matmul_lt(kept["na"], dt),
            matmul_lt(kept["mixed"], da),
            gains[1],
            matmul_lt(kept["nm"], dh),
            matmul_lt(kept["act"], db),
        )
        shards = lax.psum_scatter(grads, "dp", scatter_dimension=0, tiled=True)
    return (
        output.reshape(tokens.shape),
        input_grad.reshape(cotangent.shape),
        *(shard[None] for shard in shards),
    )


def solution(mesh):
    rows = P(("dp", "section"), None)
    layer = P("section", None)
    matrix = P("section", None, None)
    in_specs = (rows, rows, P("dp", None), layer, matrix, matrix, layer, matrix, matrix)
    split = P("section", "dp")
    split_matrix = P("section", "dp", None)
    out_specs = (rows, rows, split, split_matrix, split_matrix, split, split_matrix, split_matrix)
    return jax.shard_map(body, mesh=mesh, in_specs=in_specs, out_specs=out_specs, check_vma=False)
```

```python
import functools

import jax
import jax.numpy as jnp
from jax import lax
from jax.experimental import pallas as pl
from jax.experimental.pallas import tpu as pltpu
from jax.sharding import PartitionSpec as P

D = 768
HEADS = 12
HD = 64
FF = 3072
C = 256
WIN = 3
PAIRS = HEADS // 2
EPS = 1e-05
NEG = -1e30
MESH = pl.DeviceIdType.MESH
BF16 = jnp.bfloat16
F32 = jnp.float32
VMEM_LIMIT = 60 * 1024 * 1024


def dot(a, b):
    return jnp.dot(a, b, preferred_element_type=F32)


def dot_nt(a, b):
    return lax.dot_general(a, b, (((1,), (1,)), ((), ())), preferred_element_type=F32)


def row_mean(v):
    return jnp.mean(v, axis=-1, keepdims=True)


def greet(section, sections):
    dp = lax.axis_index("dp")
    barrier = pltpu.get_barrier_semaphore()
    for step in range(1, sections):
        other = lax.rem(section + step, sections)
        pl.semaphore_signal(barrier, inc=1, device_id=(dp, other), device_id_type=MESH)
    pl.semaphore_wait(barrier, sections - 1)


def lane_masks():
    lane = lax.broadcasted_iota(jnp.int32, (1, 2 * HD), 1)
    low = (lane < HD).astype(F32)
    return low.astype(BF16), (1.0 - low).astype(BF16), lane < HD


def two_heads(pair, low, high):
    return jnp.concatenate([pair * low, pair * high], axis=0)


def await_arrival(buf, sem):
    pltpu.make_async_copy(buf, buf, sem).wait()


def scatter_rows(section, sections, per, rows, inbox, sems, send_sems, target):
    dp = lax.axis_index("dp")
    for piece in range(per):
        slot = section * per + piece

        @pl.when(section != target)
        def _():
            pltpu.make_async_remote_copy(
                rows.at[piece],
                inbox.at[slot],
                send_sems.at[piece],
                sems.at[slot],
                device_id=(dp, target),
                device_id_type=MESH,
            ).start()

        @pl.when(section == target)
        def _():
            pltpu.make_async_copy(rows.at[piece], inbox.at[slot], sems.at[slot]).start()


def drain_rows(section, sections, per, rows, send_sems, target):
    for piece in range(per):

        @pl.when(section != target)
        def _():
            pltpu.make_async_copy(rows.at[piece], rows.at[piece], send_sems.at[piece]).wait()


def pass_on(section, chunk, per, last, step, outbox, inbox, result, sends, arrivals, landed, kept):
    dp = lax.axis_index("dp")
    owner = chunk // per

    @pl.when(section != last)
    def _():
        pltpu.make_async_remote_copy(
            outbox.at[chunk],
            inbox.at[chunk],
            sends.at[chunk],
            arrivals.at[chunk],
            device_id=(dp, section + step),
            device_id_type=MESH,
        ).start()

    @pl.when((section == last) & (owner != last))
    def _():
        pltpu.make_async_remote_copy(
            outbox.at[chunk],
            result.at[lax.rem(chunk, per)],
            sends.at[chunk],
            landed.at[lax.rem(chunk, per)],
            device_id=(dp, owner),
            device_id_type=MESH,
        ).start()

    @pl.when((section == last) & (owner == last))
    def _():
        pltpu.make_async_copy(
            outbox.at[chunk], result.at[lax.rem(chunk, per)], kept.at[lax.rem(chunk, per)]
        ).start()


def settle(section, chunks, per, last, outbox, result, sends, landed, kept):
    def one(chunk, carry):
        @pl.when((section != last) | (chunk // per != last))
        def _():
            await_arrival(outbox.at[chunk], sends.at[chunk])

        return carry

    lax.fori_loop(0, chunks, one, 0)
    for piece in range(per):

        @pl.when(section != last)
        def _():
            await_arrival(result.at[piece], landed.at[piece])

        @pl.when(section == last)
        def _():
            await_arrival(result.at[piece], kept.at[piece])


def fill_bias(docs, chunk, bias, keys_down):
    per_row = docs.shape[1] // C
    row, place = chunk // per_row, lax.rem(chunk, per_row)

    def numbers(block):
        start = pl.multiple_of(jnp.maximum(block, 0) * C, C)
        return docs[pl.ds(row, 1), pl.ds(start, C)].astype(F32)

    def upright(line):
        return jnp.transpose(jnp.broadcast_to(line, (128, C)))

    queries = numbers(place)
    if not keys_down:
        queries = upright(queries)
    for part in range(WIN):
        keys = numbers(place - (WIN - 1) + part)
        if keys_down:
            keys = upright(keys)
        for half in range(C // 128):
            lanes = slice(half * 128, (half + 1) * 128)
            allowed = keys == queries[:, lanes] if keys_down else queries == keys[:, lanes]
            if part == WIN - 1:
                down = lax.broadcasted_iota(jnp.int32, (C, 128), 0)
                across = lax.broadcasted_iota(jnp.int32, (C, 128), 1) + half * 128
                allowed = allowed & ((down <= across) if keys_down else (across <= down))
            term = jnp.where(allowed, 0.0, NEG)
            if keys_down:
                bias[part * C : (part + 1) * C, lanes] = term
            else:
                bias[:, part * C + half * 128 : part * C + (half + 1) * 128] = term


def by_blocks(docs, chunk, attend):
    place = lax.rem(chunk, docs.shape[1] // C)
    for blocks in range(1, WIN + 1):

        @pl.when((place == blocks - 1) if blocks < WIN else (place >= WIN - 1))
        def _():
            attend(blocks)


def forward_kernel(
    sections,
    tokens,
    docs,
    gain_a,
    gain_m,
    h_qkv,
    h_out,
    h_up,
    h_down,
    result,
    s_x,
    s_q,
    s_k,
    s_v,
    s_na,
    s_mixed,
    s_lse,
    s_mid,
    s_nm,
    s_act,
    s_dg,
    w_qkv,
    w_out,
    w_up,
    w_down,
    inbox,
    outbox,
    kbuf,
    vbuf,
    bias,
    b_q,
    b_na,
    b_mixed,
    b_lse,
    b_mid,
    b_nm,
    b_act,
    b_dg,
    arrivals,
    sends,
    first_sends,
    landed,
    kept,
    saves,
    weight_sems,
):
    section = lax.axis_index("section")
    chunks = inbox.shape[0]
    per = tokens.shape[0]
    weights = [
        pltpu.make_async_copy(src, dst, weight_sems.at[kind])
        for kind, (src, dst) in enumerate(
            ((h_qkv, w_qkv), (h_out, w_out), (h_up, w_up), (h_down, w_down))
        )
    ]
    for copy in weights:
        copy.start()

    def at_first(chunk, copy):
        @pl.when(chunk == 0)
        def _():
            copy.wait()

    greet(section, sections)
    scatter_rows(section, sections, per, tokens, inbox, arrivals, first_sends, 0)
    low, high, is_low = lane_masks()
    centered = jnp.where(section == 0, 1.0, 0.0).astype(F32)

    def stores(chunk, slot):
        here = pl.ds(pl.multiple_of(chunk * C, C), C)
        pairs = (
            (inbox.at[chunk], s_x),
            (kbuf.at[here], s_k),
            (vbuf.at[here], s_v),
            (b_q.at[slot], s_q),
            (b_na.at[slot], s_na),
            (b_mixed.at[slot], s_mixed),
            (b_lse.at[slot], s_lse),
            (b_mid.at[slot], s_mid),
            (b_nm.at[slot], s_nm),
            (b_act.at[slot], s_act),
            (b_dg.at[slot], s_dg),
        )
        return [
            pltpu.make_async_copy(src, dst.at[chunk], saves.at[kind, slot])
            for kind, (src, dst) in enumerate(pairs)
        ]

    def one_chunk(chunk, carry):
        slot = lax.rem(chunk, 2)

        @pl.when(chunk >= 2)
        def _():
            for copy in stores(chunk - 2, slot):
                copy.wait()

        todo = stores(chunk, slot)
        at_first(chunk, weights[0])
        fill_bias(docs, chunk, bias, False)
        await_arrival(inbox.at[chunk], arrivals.at[chunk])
        todo[0].start()
        x = inbox[chunk].astype(F32)
        x = x - centered * row_mean(x)
        na = (x * lax.rsqrt(row_mean(x * x) + EPS) * gain_a[...]).astype(BF16)
        b_na[slot] = na
        todo[4].start()
        b_q[slot] = (dot(na, w_qkv[:, :D]).astype(BF16) * (HD**-0.5)).astype(BF16)
        here = pl.ds(pl.multiple_of(chunk * C, C), C)
        kbuf[here, :] = dot(na, w_qkv[:, D : 2 * D]).astype(BF16)
        vbuf[here, :] = dot(na, w_qkv[:, 2 * D :]).astype(BF16)
        todo[1].start()
        todo[2].start()
        todo[3].start()
        lane = lax.broadcasted_iota(jnp.int32, (1, 128), 1)

        def attend(blocks):
            window = pl.ds(pl.multiple_of((chunk - blocks + 1) * C, C), blocks * C)
            masked = slice((WIN - blocks) * C, WIN * C)
            lse_all = jnp.zeros((C, 128), F32)
            for pair in range(PAIRS):
                lanes = slice(pair * 2 * HD, (pair + 1) * 2 * HD)
                q2 = two_heads(b_q[slot, :, lanes], low, high)
                s = dot_nt(q2, kbuf[window, lanes]).reshape(2, C, blocks * C) + bias[:, masked][None]
                top = jnp.max(s, axis=-1, keepdims=True)
                e = jnp.exp(s - top)
                total = jnp.sum(e, axis=-1, keepdims=True)
                o = dot(e.astype(BF16).reshape(2 * C, blocks * C), vbuf[window, lanes])
                o = o.reshape(2, C, 2 * HD) * (1.0 / total)
                b_mixed[slot, :, lanes] = jnp.where(is_low, o[0], o[1]).astype(BF16)
                lse = top + jnp.log(total)
                lse_all = jnp.where(lane == 2 * pair, lse[0], lse_all)
                lse_all = jnp.where(lane == 2 * pair + 1, lse[1], lse_all)
            b_lse[slot] = jnp.transpose(lse_all)[:16]

        by_blocks(docs, chunk, attend)
        todo[5].start()
        todo[6].start()
        at_first(chunk, weights[1])
        branch = dot(b_mixed[slot], w_out[...])
        mid = x + branch - row_mean(branch)
        b_mid[slot] = mid
        todo[7].start()
        nm = (mid * lax.rsqrt(row_mean(mid * mid) + EPS) * gain_m[...]).astype(BF16)
        b_nm[slot] = nm
        todo[8].start()
        at_first(chunk, weights[2])
        k0 = 0.7978845608028654
        k1 = 0.044715
        for part in range(FF // D):
            cols = slice(part * D, (part + 1) * D)
            h = dot(nm, w_up[:, cols])
            h2 = h * h
            t = jnp.tanh(h * (k0 + (k0 * k1) * h2))
            half = 0.5 + 0.5 * t
            b_act[slot, :, cols] = (h * half).astype(BF16)
            slope = half + (h * (1.0 - t * t)) * (0.5 * k0 + (1.5 * k0 * k1) * h2)
            b_dg[slot, :, cols] = slope.astype(BF16)
        todo[9].start()
        todo[10].start()
        at_first(chunk, weights[3])
        branch = dot(b_act[slot], w_down[...])
        outbox[chunk] = (b_mid[slot] + branch - row_mean(branch)).astype(BF16)
        pass_on(section, chunk, per, sections - 1, 1, outbox, inbox, result, sends, arrivals, landed, kept)
        return carry

    lax.fori_loop(0, chunks, one_chunk, 0)
    for chunk in (chunks - 2, chunks - 1):
        for copy in stores(chunk, chunk % 2):
            copy.wait()
    drain_rows(section, sections, per, tokens, first_sends, 0)
    settle(section, chunks, per, sections - 1, outbox, result, sends, landed, kept)


def backward_kernel(
    sections,
    cotangent,
    docs,
    gain_a,
    gain_m,
    h_qkv,
    h_out,
    h_up,
    h_down,
    s_x,
    s_q,
    s_k,
    s_v,
    s_mixed,
    s_lse,
    s_mid,
    s_dg,
    result,
    gains,
    s_db,
    s_dh,
    s_da,
    s_dt,
    w_qkv,
    w_out,
    w_up,
    w_down,
    inbox,
    outbox,
    kbuf,
    vbuf,
    bias,
    dk_acc,
    dv_acc,
    lse_d,
    b_dmix,
    marks,
    b_x,
    b_q,
    b_mixed,
    b_lse,
    b_mid,
    b_dg,
    b_db,
    b_dh,
    b_da,
    b_dt,
    arrivals,
    sends,
    first_sends,
    landed,
    kept,
    loads,
    saves,
    kv_sems,
    weight_sems,
):
    section = lax.axis_index("section")
    chunks = inbox.shape[0]
    per = cotangent.shape[0]
    last = sections - 1

    def fetches(chunk, slot):
        pairs = (
            (s_dg, b_dg),
            (s_mid, b_mid),
            (s_mixed, b_mixed),
            (s_q, b_q),
            (s_lse, b_lse),
            (s_x, b_x),
        )
        return [
            pltpu.make_async_copy(src.at[chunk], dst.at[slot], loads.at[kind, slot])
            for kind, (src, dst) in enumerate(pairs)
        ]

    def stores(chunk, slot):
        pairs = ((b_db, s_db), (b_dh, s_dh), (b_da, s_da), (b_dt, s_dt))
        return [
            pltpu.make_async_copy(src.at[slot], dst.at[chunk], saves.at[kind, slot])
            for kind, (src, dst) in enumerate(pairs)
        ]

    kv_copies = [
        pltpu.make_async_copy(s_k, kbuf, kv_sems.at[0]),
        pltpu.make_async_copy(s_v, vbuf, kv_sems.at[1]),
    ]
    weights = [
        pltpu.make_async_copy(src, dst, weight_sems.at[kind])
        for kind, (src, dst) in enumerate(
            ((h_down, w_down), (h_up, w_up), (h_out, w_out), (h_qkv, w_qkv))
        )
    ]
    weights[0].start()
    for copy in fetches(chunks - 1, 0):
        copy.start()
    weights[1].start()
    weights[2].start()
    for copy in kv_copies:
        copy.start()
    weights[3].start()

    def at_first(step, copy):
        @pl.when(step == 0)
        def _():
            copy.wait()

    greet(section, sections)
    scatter_rows(section, sections, per, cotangent, inbox, arrivals, first_sends, last)
    low, high, _ = lane_masks()
    dk_acc[...] = jnp.zeros_like(dk_acc)
    dv_acc[...] = jnp.zeros_like(dv_acc)
    gains[...] = jnp.zeros_like(gains)
    owner_of = lax.broadcasted_iota(jnp.int32, (D, 128), 0) // HD
    marks[...] = (owner_of == lax.broadcasted_iota(jnp.int32, (D, 128), 1)).astype(F32).astype(BF16)
    centered = jnp.where(section == 0, 1.0, 0.0).astype(F32)

    def folded(v):
        return jnp.sum(v.reshape(C // 8, 8, D), axis=0)

    def one_chunk(step, carry):
        chunk = chunks - 1 - step
        slot = lax.rem(step, 2)

        @pl.when(step + 1 < chunks)
        def _():
            for copy in fetches(chunk - 1, 1 - slot):
                copy.start()

        @pl.when(step >= 2)
        def _():
            for copy in stores(chunk + 2, slot):
                copy.wait()

        for copy in fetches(chunk, slot):
            copy.wait()
        todo = stores(chunk, slot)
        at_first(step, weights[0])
        fill_bias(docs, chunk, bias, True)
        await_arrival(inbox.at[chunk], arrivals.at[chunk])
        g = inbox[chunk].astype(F32)
        db = (g - row_mean(g)).astype(BF16)
        b_db[slot] = db
        todo[0].start()
        for part in range(FF // D):
            cols = slice(part * D, (part + 1) * D)
            d_active = dot_nt(db, w_down[cols, :])
            b_dh[slot, :, cols] = (d_active * b_dg[slot, :, cols].astype(F32)).astype(BF16)
        todo[1].start()
        at_first(step, weights[1])
        dn = dot_nt(b_dh[slot], w_up[...])
        mid = b_mid[slot]
        factor = lax.rsqrt(row_mean(mid * mid) + EPS)
        unit = mid * factor
        gains[1] += folded(dn * unit)
        dn = dn * gain_m[...]
        d_mid = g + factor * (dn - unit * row_mean(dn * unit))
        da = (d_mid - row_mean(d_mid)).astype(BF16)
        b_da[slot] = da
        todo[2].start()
        b_mid[slot] = d_mid
        at_first(step, weights[2])
        dmix = dot_nt(da, w_out[...]).astype(BF16)
        b_dmix[...] = dmix
        prod = dmix.astype(F32) * b_mixed[slot].astype(F32)
        top = prod.astype(BF16)
        rest = (prod - top.astype(F32)).astype(BF16)
        inner = dot(top, marks[...]) + dot(rest, marks[...])
        lse_d[...] = jnp.transpose(inner)[:16]
        for copy in kv_copies:
            at_first(step, copy)

        def attend(blocks):
            window = pl.ds(pl.multiple_of((chunk - blocks + 1) * C, C), blocks * C)
            masked = slice((WIN - blocks) * C, WIN * C)
            for pair in range(PAIRS):
                lanes = slice(pair * 2 * HD, (pair + 1) * 2 * HD)
                q2 = two_heads(b_q[slot, :, lanes], low, high)
                do2 = two_heads(b_dmix[:, lanes], low, high)
                keys = kbuf[window, lanes]
                values = vbuf[window, lanes]
                both = jnp.concatenate([bias[masked, :], bias[masked, :]], axis=1)
                even, odd = slice(2 * pair, 2 * pair + 1), slice(2 * pair + 1, 2 * pair + 2)
                lse = jnp.concatenate([b_lse[slot, even, :], b_lse[slot, odd, :]], axis=1)
                inner = jnp.concatenate([lse_d[even, :], lse_d[odd, :]], axis=1)
                probs = jnp.exp(dot_nt(keys, q2) + both - lse)
                ds = (probs * (dot_nt(values, do2) - inner)).astype(BF16)
                dv = dot(probs.astype(BF16), do2)
                dk = dot(ds, q2)
                for part in range(blocks):
                    place = lax.rem(chunk - blocks + 1 + part, WIN)
                    rows = slice(part * C, (part + 1) * C)
                    dv_acc[place, :, lanes] += dv[rows]
                    dk_acc[place, :, lanes] += dk[rows]
                dq = dot(jnp.transpose(keys), ds)
                dq = jnp.concatenate([dq[:HD, :C], dq[HD:, C:]], axis=0)
                b_dt[slot, :, lanes] = (jnp.transpose(dq) * (HD**-0.5)).astype(BF16)

        by_blocks(docs, chunk, attend)
        done = lax.rem(chunk, WIN)
        b_dt[slot, :, D : 2 * D] = dk_acc[done].astype(BF16)
        b_dt[slot, :, 2 * D :] = dv_acc[done].astype(BF16)
        dk_acc[done] = jnp.zeros((C, D), F32)
        dv_acc[done] = jnp.zeros((C, D), F32)
        todo[3].start()
        at_first(step, weights[3])
        dn = dot_nt(b_dt[slot], w_qkv[...])
        x = b_x[slot].astype(F32)
        x = x - centered * row_mean(x)
        factor = lax.rsqrt(row_mean(x * x) + EPS)
        unit = x * factor
        gains[0] += folded(dn * unit)
        dn = dn * gain_a[...]
        grad = b_mid[slot] + factor * (dn - unit * row_mean(dn * unit))
        grad = grad - centered * row_mean(grad)
        outbox[chunk] = grad.astype(BF16)
        pass_on(section, chunk, per, 0, -1, outbox, inbox, result, sends, arrivals, landed, kept)
        return carry

    lax.fori_loop(0, chunks, one_chunk, 0)
    for step in (chunks - 2, chunks - 1):
        for copy in stores(chunks - 1 - step, step % 2):
            copy.wait()
    drain_rows(section, sections, per, cotangent, first_sends, last)
    settle(section, chunks, per, 0, outbox, result, sends, landed, kept)


ANY = pl.BlockSpec(memory_space=pl.ANY)
IN_VMEM = pl.BlockSpec(memory_space=pltpu.VMEM)
DMA = pltpu.SemaphoreType.DMA


WEIGHTS = [pltpu.VMEM(shape, BF16) for shape in ((D, 3 * D), (D, D), (D, FF), (FF, D))]


def forward(sections, chunks, tokens, docs, weights):
    per = chunks // sections
    sds = jax.ShapeDtypeStruct
    saved = (
        ("x", (C, D), BF16),
        ("q", (C, D), BF16),
        ("k", (C, D), BF16),
        ("v", (C, D), BF16),
        ("na", (C, D), BF16),
        ("mixed", (C, D), BF16),
        ("lse", (16, C), F32),
        ("mid", (C, D), F32),
        ("nm", (C, D), BF16),
        ("act", (C, FF), BF16),
        ("dg", (C, FF), BF16),
    )
    staged = [entry for entry in saved if entry[0] not in ("x", "k", "v")]
    outs = pl.pallas_call(
        functools.partial(forward_kernel, sections),
        out_shape=[sds((per, C, D), BF16)] + [sds((chunks,) + s, t) for _, s, t in saved],
        in_specs=[ANY] + [IN_VMEM] * 3 + [ANY] * 4,
        out_specs=[ANY] * (1 + len(saved)),
        scratch_shapes=WEIGHTS
        + [
            pltpu.VMEM((chunks, C, D), BF16),
            pltpu.VMEM((chunks, C, D), BF16),
            pltpu.VMEM((chunks * C, D), BF16),
            pltpu.VMEM((chunks * C, D), BF16),
            pltpu.VMEM((C, WIN * C), F32),
        ]
        + [pltpu.VMEM((2,) + s, t) for _, s, t in staged]
        + [DMA((chunks,)), DMA((chunks,)), DMA((per,)), DMA((per,)), DMA((per,)), DMA((11, 2)), DMA((4,))],
        compiler_params=pltpu.CompilerParams(
            collective_id=0, has_side_effects=True, vmem_limit_bytes=VMEM_LIMIT
        ),
        name="layer_forward",
    )(tokens.reshape(per, C, D), docs, *weights)
    return outs[0], {name: out for (name, _, _), out in zip(saved, outs[1:])}


def backward(sections, chunks, cotangent, docs, weights, kept):
    per = chunks // sections
    sds = jax.ShapeDtypeStruct
    fetched = (
        ((C, D), BF16),
        ((C, D), BF16),
        ((C, D), BF16),
        ((16, C), F32),
        ((C, D), F32),
        ((C, FF), BF16),
    )
    saved = ((C, D), (C, FF), (C, D), (C, 3 * D))
    outs = pl.pallas_call(
        functools.partial(backward_kernel, sections),
        out_shape=[sds((per, C, D), BF16), sds((2, 8, D), F32)] + [sds((chunks,) + s, BF16) for s in saved],
        in_specs=[ANY] + [IN_VMEM] * 3 + [ANY] * 12,
        out_specs=[ANY, IN_VMEM] + [ANY] * len(saved),
        scratch_shapes=WEIGHTS
        + [
            pltpu.VMEM((chunks, C, D), BF16),
            pltpu.VMEM((chunks, C, D), BF16),
            pltpu.VMEM((chunks * C, D), BF16),
            pltpu.VMEM((chunks * C, D), BF16),
            pltpu.VMEM((WIN * C, C), F32),
            pltpu.VMEM((WIN, C, D), F32),
            pltpu.VMEM((WIN, C, D), F32),
            pltpu.VMEM((16, C), F32),
            pltpu.VMEM((C, D), BF16),
            pltpu.VMEM((D, 128), BF16),
        ]
        + [pltpu.VMEM((2,) + s, t) for s, t in fetched]
        + [pltpu.VMEM((2,) + s, BF16) for s in saved]
        + [DMA((chunks,)), DMA((chunks,)), DMA((per,)), DMA((per,)), DMA((per,))]
        + [DMA((6, 2)), DMA((4, 2)), DMA((2,)), DMA((4,))],
        compiler_params=pltpu.CompilerParams(
            collective_id=1, has_side_effects=True, vmem_limit_bytes=VMEM_LIMIT
        ),
        name="layer_backward",
    )(
        cotangent.reshape(per, C, D),
        docs,
        *weights,
        kept["x"],
        kept["q"],
        kept["k"].reshape(chunks * C, D),
        kept["v"].reshape(chunks * C, D),
        kept["mixed"],
        kept["lse"],
        kept["mid"],
        kept["dg"],
    )
    return outs


def matmul_lt(left_side, right_side):
    rows = left_side.shape[0] * left_side.shape[1]
    return lax.dot_general(
        left_side.reshape(rows, -1),
        right_side.reshape(rows, -1),
        (((0,), (0,)), ((), ())),
        preferred_element_type=F32,
    )


UNIT = 256
UNITS = 9 + 3 + 12 + 12
NARROW = 9 + 3 + 12
LAGS = (4, 8, 12)


def pair_first(unit):
    return lax.rem(unit, 4) != 3


def dot_tn(a, b):
    return lax.dot_general(a, b, (((0,), (0,)), ((), ())), preferred_element_type=F32)


def weight_grad_kernel(
    s_na,
    s_dt,
    s_mixed,
    s_da,
    s_nm,
    s_dh,
    s_act,
    s_db,
    gains,
    o_qkv,
    o_out,
    o_up,
    o_down,
    o_gains,
    left,
    right,
    act,
    made,
    got_a,
    got_b,
    got_c,
    total,
    gain_own,
    gain_in,
    left_sems,
    right_sems,
    act_sem,
    a_sends,
    a_arrivals,
    b_sends,
    b_arrivals,
    c_sends,
    c_arrivals,
    out_sem,
    gain_sends,
    gain_arrivals,
):
    section = lax.axis_index("section")
    dp = lax.axis_index("dp")
    x, near, far = lax.rem(dp, 2), lax.rem(dp // 2, 2), dp // 4
    over_x, over_near, over_far = dp + 1 - 2 * x, dp + 2 - 4 * near, dp + 4 - 8 * far

    def load_left(src, slot):
        return pltpu.make_async_copy(src, left.at[slot], left_sems.at[slot])

    def load_right(src, column, slot):
        columns = pl.ds(pl.multiple_of(column * UNIT, UNIT), UNIT)
        return pltpu.make_async_copy(src.at[:, columns], right.at[slot], right_sems.at[slot])

    def start_right(unit):
        slot = lax.rem(unit, 2)

        @pl.when(unit < 9)
        def _():
            load_right(s_dt, unit, slot).start()

        @pl.when((unit >= 9) & (unit < 12))
        def _():
            load_right(s_da, unit - 9, slot).start()

        @pl.when((unit >= 12) & (unit < NARROW))
        def _():
            load_right(s_dh, unit - 12, slot).start()

    load_left(s_na, 0).start()
    start_right(0)
    load_left(s_mixed, 1).start()
    pltpu.make_async_copy(s_act, act, act_sem).start()
    gain_own[...] = jnp.sum(gains[...], axis=1, keepdims=True) + jnp.zeros((2, 8, D), F32)

    barrier = pltpu.get_barrier_semaphore()
    for step in range(1, 8):
        other = lax.rem(dp + step, 8)
        pl.semaphore_signal(barrier, inc=1, device_id=(other, section), device_id_type=MESH)
    pl.semaphore_wait(barrier, 7)

    def gain_copy(step):
        other = lax.rem(dp + step, 8)
        return pltpu.make_async_remote_copy(
            gain_own,
            gain_in.at[step - 1],
            gain_sends.at[step - 1],
            gain_arrivals.at[step - 1],
            device_id=(other, section),
            device_id_type=MESH,
        )

    for step in range(1, 8):
        gain_copy(step).start()

    def send(unit, src, dst, sends, arrivals, to):
        pltpu.make_async_remote_copy(
            src,
            dst.at[unit],
            sends.at[unit],
            arrivals.at[unit],
            device_id=(to, section),
            device_id_type=MESH,
        ).start()

    def first_add(unit):
        @pl.when(pair_first(unit))
        def _():
            send(unit, made.at[unit, 1 - x], got_a, a_sends, a_arrivals, over_x)

        @pl.when(jnp.logical_not(pair_first(unit)))
        def _():
            send(unit, made.at[unit, :, 1 - near], got_a, a_sends, a_arrivals, over_near)

    def second_add(unit):
        await_arrival(got_a.at[unit], a_arrivals.at[unit])

        @pl.when(pair_first(unit))
        def _():
            made[unit, x] = (made[unit, x].astype(F32) + got_a[unit].astype(F32)).astype(BF16)
            send(unit, made.at[unit, x, 1 - near], got_b, b_sends, b_arrivals, over_near)

        @pl.when(jnp.logical_not(pair_first(unit)))
        def _():
            made[unit, :, near] = (made[unit, :, near].astype(F32) + got_a[unit].astype(F32)).astype(BF16)
            send(unit, made.at[unit, 1 - x, near], got_b, b_sends, b_arrivals, over_x)

    def third_add(unit):
        await_arrival(got_b.at[unit], b_arrivals.at[unit])
        made[unit, x, near] = (made[unit, x, near].astype(F32) + got_b[unit].astype(F32)).astype(BF16)
        send(unit, made.at[unit, x, near, 1 - far], got_c, c_sends, c_arrivals, over_far)

    def finish(unit):
        await_arrival(got_c.at[unit], c_arrivals.at[unit])
        total[unit] = made[unit, x, near, far].astype(F32) + got_c[unit].astype(F32)
        deliver(unit)

    def deliver(unit):
        for first, end, ref in ((0, 9, o_qkv), (9, 12, o_out), (12, NARROW, o_up)):

            @pl.when((unit >= first) & (unit < end))
            def _():
                columns = pl.ds(pl.multiple_of((unit - first) * UNIT, UNIT), UNIT)
                pltpu.make_async_copy(total.at[unit], ref.at[:, columns], out_sem).start()

        @pl.when(unit >= NARROW)
        def _():
            column, row = (unit - NARROW) // 4, lax.rem(unit - NARROW, 4)
            columns = pl.ds(pl.multiple_of(column * UNIT, UNIT), UNIT)
            rows = pl.ds(pl.multiple_of(row * 96, 96), 96)
            pltpu.make_async_copy(total.at[unit], o_down.at[rows, columns], out_sem).start()

    def advance(now):
        for lag, action in zip(LAGS[::-1], (finish, third_add, second_add)):

            @pl.when((now >= lag) & (now - lag < UNITS))
            def _():
                action(now - lag)

    def narrow(unit, carry):
        slot = lax.rem(unit, 2)
        side = jnp.where((unit >= 9) & (unit < 12), 1, 0)

        @pl.when(unit == 9)
        def _():
            load_left(s_nm, 0).start()

        @pl.when(unit == 12)
        def _():
            load_left(s_db, 1).start()

        start_right(unit + 1)

        @pl.when((unit == 0) | (unit == 12))
        def _():
            load_left(s_na, 0).wait()

        @pl.when(unit == 9)
        def _():
            load_left(s_mixed, 1).wait()

        load_right(s_dt, 0, slot).wait()
        grad = dot_tn(left[side], right[slot]).astype(BF16)
        for shard in range(8):
            made[unit, shard % 2, shard // 2 % 2, shard // 4] = grad[shard * 96 : (shard + 1) * 96]
        first_add(unit)
        advance(unit)
        return carry

    lax.fori_loop(0, NARROW, narrow, 0)
    load_left(s_db, 1).wait()
    pltpu.make_async_copy(s_act, act, act_sem).wait()

    def wide(step, carry):
        column, shard = step // 8, lax.rem(step, 8)
        columns = pl.ds(pl.multiple_of(column * UNIT, UNIT), UNIT)
        rows = pl.ds(pl.multiple_of(shard * 384, 384), 384)
        grad = dot_tn(act[:, rows], left[1, :, columns]).astype(BF16)
        first = NARROW + 4 * column
        for part in range(4):
            made[first + part, lax.rem(shard, 2), lax.rem(shard // 2, 2), shard // 4] = grad[part * 96 : (part + 1) * 96]

        @pl.when(shard == 7)
        def _():
            for part in range(4):
                first_add(first + part)

        @pl.when(lax.rem(step, 2) == 1)
        def _():
            advance(NARROW + step // 2)

        return carry

    lax.fori_loop(0, 24, wide, 0)

    def drain(now, carry):
        advance(now)
        return carry

    lax.fori_loop(UNITS, UNITS + LAGS[-1], drain, 0)
    for step in range(1, 8):
        gain_copy(step).wait()
    sums = gain_own[:, 0:1]
    for step in range(7):
        sums = sums + gain_in[step, :, 0:1]
    o_gains[...] = sums

    def sent(unit, carry):
        await_arrival(got_a.at[unit], a_sends.at[unit])
        await_arrival(got_b.at[unit], b_sends.at[unit])
        await_arrival(got_c.at[unit], c_sends.at[unit])
        return carry

    lax.fori_loop(0, UNITS, sent, 0)
    await_arrival(total, out_sem)


def weight_grads(na, dt, mixed, da, nm, dh, act, db, gains):
    tokens = na.shape[0] * na.shape[1]
    sds = jax.ShapeDtypeStruct
    operands = [v.reshape(tokens, -1) for v in (na, dt, mixed, da, nm, dh, act, db)]
    return pl.pallas_call(
        weight_grad_kernel,
        out_shape=[
            sds((96, 3 * D), F32),
            sds((96, D), F32),
            sds((96, FF), F32),
            sds((384, D), F32),
            sds((2, 1, D), F32),
        ],
        in_specs=[ANY] * 8 + [IN_VMEM],
        out_specs=[ANY] * 4 + [IN_VMEM],
        scratch_shapes=[
            pltpu.VMEM((2, tokens, D), BF16),
            pltpu.VMEM((2, tokens, UNIT), BF16),
            pltpu.VMEM((tokens, FF), BF16),
            pltpu.VMEM((UNITS, 2, 2, 2, 96, UNIT), BF16),
            pltpu.VMEM((UNITS, 2, 2, 96, UNIT), BF16),
            pltpu.VMEM((UNITS, 2, 96, UNIT), BF16),
            pltpu.VMEM((UNITS, 96, UNIT), BF16),
            pltpu.VMEM((UNITS, 96, UNIT), F32),
            pltpu.VMEM((2, 8, D), F32),
            pltpu.VMEM((7, 2, 8, D), F32),
            DMA((2,)),
            DMA((2,)),
            DMA,
            DMA((UNITS,)),
            DMA((UNITS,)),
            DMA((UNITS,)),
            DMA((UNITS,)),
            DMA((UNITS,)),
            DMA((UNITS,)),
            DMA,
            DMA((7,)),
            DMA((7,)),
        ],
        compiler_params=pltpu.CompilerParams(
            collective_id=2, has_side_effects=True, vmem_limit_bytes=VMEM_LIMIT
        ),
        name="weight_grads",
    )(*operands, gains)


def hand_over_kernel(gains, *refs):
    sources, results, (gain_attn, gain_mlp), held = refs[:6], refs[6:12], refs[12:14], refs[14:20]
    come, go = refs[20], refs[21]
    arriving = [
        pltpu.make_async_copy(src, buf, come.at[at]) for at, (src, buf) in enumerate(zip(sources, held))
    ]
    leaving = [
        pltpu.make_async_copy(buf, dst, go.at[at]) for at, (buf, dst) in enumerate(zip(held, results))
    ]
    for copy in arriving:
        copy.start()
    shift = lax.rem(D - 96 * lax.axis_index("dp"), D)
    for kind, ref in enumerate((gain_attn, gain_mlp)):
        turned = pltpu.roll(jnp.broadcast_to(gains[kind], (8, D)), shift, 1)
        ref[...] = turned[:1, :96]
    for copy, onward in zip(arriving, leaving):
        copy.wait()
        onward.start()
    for copy in leaving:
        copy.wait()


def hand_over(output, input_grad, shards, gains):
    sds = jax.ShapeDtypeStruct
    sources = (output, input_grad, *shards)
    outs = pl.pallas_call(
        hand_over_kernel,
        out_shape=[sds(v.shape, v.dtype) for v in sources] + [sds((1, 96), F32)] * 2,
        in_specs=[IN_VMEM] + [ANY] * 6,
        out_specs=[ANY] * 6 + [IN_VMEM] * 2,
        scratch_shapes=[pltpu.VMEM(v.shape, v.dtype) for v in sources] + [DMA((6,)), DMA((6,))],
        compiler_params=pltpu.CompilerParams(vmem_limit_bytes=VMEM_LIMIT),
        name="hand_over",
    )(gains, *sources)
    output, input_grad, qkv, out, up, down, gain_attn, gain_mlp = outs
    return output, input_grad, gain_attn, qkv[None], out[None], gain_mlp, up[None], down[None]


def body(tokens, cotangent, doc_ids, gain_attn, w_qkv, w_out, gain_mlp, w_up, w_down):
    sections = lax.axis_size("section")
    rows, seq = doc_ids.shape
    chunks = rows * seq // C
    weights = (gain_attn, gain_mlp, w_qkv[0], w_out[0], w_up[0], w_down[0])
    output, kept = forward(sections, chunks, tokens, doc_ids, weights)
    input_grad, gains, db, dh, da, dt = backward(
        sections, chunks, cotangent, doc_ids, weights, kept
    )
    if lax.axis_size("dp") == 8 and chunks == 8:
        qkv, out, up, down, gains = weight_grads(
            kept["na"], dt, kept["mixed"], da, kept["nm"], dh, kept["act"], db, gains
        )
        return hand_over(
            output.reshape(tokens.shape), input_grad.reshape(cotangent.shape), (qkv, out, up, down), gains
        )
    gains = jnp.sum(gains, axis=1)
    grads = (
        gains[0],
        matmul_lt(kept["na"], dt),
        matmul_lt(kept["mixed"], da),
        gains[1],
        matmul_lt(kept["nm"], dh),
        matmul_lt(kept["act"], db),
    )
    shards = lax.psum_scatter(grads, "dp", scatter_dimension=0, tiled=True)
    return (
        output.reshape(tokens.shape),
        input_grad.reshape(cotangent.shape),
        *(shard[None] for shard in shards),
    )


def solution(mesh):
    rows = P(("dp", "section"), None)
    layer = P("section", None)
    matrix = P("section", None, None)
    in_specs = (rows, rows, P("dp", None), layer, matrix, matrix, layer, matrix, matrix)
    split = P("section", "dp")
    split_matrix = P("section", "dp", None)
    out_specs = (rows, rows, split, split_matrix, split_matrix, split, split_matrix, split_matrix)
    return jax.shard_map(body, mesh=mesh, in_specs=in_specs, out_specs=out_specs, check_vma=False)
```

```python
import functools

import jax
import jax.numpy as jnp
from jax import lax
from jax.experimental import pallas as pl
from jax.experimental.pallas import tpu as pltpu
from jax.sharding import PartitionSpec as P

D = 768
HEADS = 12
HD = 64
FF = 3072
C = 256
WIN = 3
PAIRS = HEADS // 2
EPS = 1e-05
NEG = -1e30
MESH = pl.DeviceIdType.MESH
BF16 = jnp.bfloat16
F32 = jnp.float32
VMEM_LIMIT = 60 * 1024 * 1024


def dot(a, b):
    return jnp.dot(a, b, preferred_element_type=F32)


def dot_nt(a, b):
    return lax.dot_general(a, b, (((1,), (1,)), ((), ())), preferred_element_type=F32)


def row_mean(v):
    return jnp.mean(v, axis=-1, keepdims=True)


def greet(section, sections):
    dp = lax.axis_index("dp")
    barrier = pltpu.get_barrier_semaphore()
    for step in range(1, sections):
        other = lax.rem(section + step, sections)
        pl.semaphore_signal(barrier, inc=1, device_id=(dp, other), device_id_type=MESH)
    pl.semaphore_wait(barrier, sections - 1)


def lane_masks():
    lane = lax.broadcasted_iota(jnp.int32, (1, 2 * HD), 1)
    low = (lane < HD).astype(F32)
    return low.astype(BF16), (1.0 - low).astype(BF16), lane < HD


def two_heads(pair, low, high):
    return jnp.concatenate([pair * low, pair * high], axis=0)


def await_arrival(buf, sem):
    pltpu.make_async_copy(buf, buf, sem).wait()


def scatter_rows(section, sections, per, rows, inbox, sems, send_sems, target):
    dp = lax.axis_index("dp")
    for piece in range(per):
        slot = section * per + piece

        @pl.when(section != target)
        def _():
            pltpu.make_async_remote_copy(
                rows.at[piece],
                inbox.at[slot],
                send_sems.at[piece],
                sems.at[slot],
                device_id=(dp, target),
                device_id_type=MESH,
            ).start()

        @pl.when(section == target)
        def _():
            pltpu.make_async_copy(rows.at[piece], inbox.at[slot], sems.at[slot]).start()


def drain_rows(section, sections, per, rows, send_sems, target):
    for piece in range(per):

        @pl.when(section != target)
        def _():
            pltpu.make_async_copy(rows.at[piece], rows.at[piece], send_sems.at[piece]).wait()


def pass_on(section, chunk, per, last, step, source, inbox, result, sends, arrivals, landed):
    dp = lax.axis_index("dp")
    owner = chunk // per

    @pl.when(section != last)
    def _():
        pltpu.make_async_remote_copy(
            source,
            inbox.at[chunk],
            sends.at[chunk],
            arrivals.at[chunk],
            device_id=(dp, section + step),
            device_id_type=MESH,
        ).start()

    @pl.when((section == last) & (owner != last))
    def _():
        pltpu.make_async_remote_copy(
            source,
            result.at[lax.rem(chunk, per)],
            sends.at[chunk],
            landed.at[lax.rem(chunk, per)],
            device_id=(dp, owner),
            device_id_type=MESH,
        ).start()

    @pl.when((section == last) & (owner == last))
    def _():
        pltpu.make_async_copy(source, result.at[lax.rem(chunk, per)], sends.at[chunk]).start()


def settle(section, first, end, per, last, source, result, sends, landed):
    def one(chunk, carry):
        await_arrival(source, sends.at[chunk])
        return carry

    lax.fori_loop(first, end, one, 0)
    for piece in range(per):

        @pl.when(section != last)
        def _():
            await_arrival(result.at[piece], landed.at[piece])


def fill_bias(docs, chunk, bias, keys_down):
    per_row = docs.shape[1] // C
    row, place = chunk // per_row, lax.rem(chunk, per_row)

    def numbers(block):
        start = pl.multiple_of(jnp.maximum(block, 0) * C, C)
        return docs[pl.ds(row, 1), pl.ds(start, C)].astype(F32)

    def upright(line):
        return jnp.transpose(jnp.broadcast_to(line, (128, C)))

    queries = numbers(place)
    if not keys_down:
        queries = upright(queries)
    for part in range(WIN):
        keys = numbers(place - (WIN - 1) + part)
        if keys_down:
            keys = upright(keys)
        for half in range(C // 128):
            lanes = slice(half * 128, (half + 1) * 128)
            allowed = keys == queries[:, lanes] if keys_down else queries == keys[:, lanes]
            if part == WIN - 1:
                down = lax.broadcasted_iota(jnp.int32, (C, 128), 0)
                across = lax.broadcasted_iota(jnp.int32, (C, 128), 1) + half * 128
                allowed = allowed & ((down <= across) if keys_down else (across <= down))
            term = jnp.where(allowed, 0.0, NEG)
            if keys_down:
                bias[part * C : (part + 1) * C, lanes] = term
            else:
                bias[:, part * C + half * 128 : part * C + (half + 1) * 128] = term


def by_blocks(docs, chunk, attend):
    place = lax.rem(chunk, docs.shape[1] // C)
    for blocks in range(1, WIN + 1):

        @pl.when((place == blocks - 1) if blocks < WIN else (place >= WIN - 1))
        def _():
            attend(blocks)


def layer_kernel(
    sections,
    tokens,
    cotangent,
    docs,
    gain_a,
    gain_m,
    h_qkv,
    h_out,
    h_up,
    h_down,
    result,
    grad_result,
    gains,
    s_q,
    s_na,
    s_mixed,
    s_lse,
    s_mid,
    s_nm,
    s_act,
    s_dg,
    s_db,
    s_dh,
    s_da,
    s_dt,
    w_qkv,
    w_out,
    w_up,
    w_down,
    inbox,
    outbox,
    grads,
    kbuf,
    vbuf,
    bias_f,
    bias_b,
    dk_acc,
    dv_acc,
    lse_d,
    b_dmix,
    marks,
    b_q,
    b_na,
    b_mixed,
    b_lse,
    b_mid,
    b_nm,
    b_act,
    b_dg,
    b_dt,
    arrivals,
    sends,
    first_sends,
    landed,
    grad_arrivals,
    grad_sends,
    grad_first_sends,
    grad_landed,
    kept_f,
    kept_b,
    loads,
    weight_sems,
):
    section = lax.axis_index("section")
    chunks = inbox.shape[0]
    per = tokens.shape[0]
    last = sections - 1
    weights = [
        pltpu.make_async_copy(src, dst, weight_sems.at[kind])
        for kind, (src, dst) in enumerate(
            ((h_qkv, w_qkv), (h_out, w_out), (h_up, w_up), (h_down, w_down))
        )
    ]
    for copy in weights:
        copy.start()

    def at_first(chunk, copy):
        @pl.when(chunk == 0)
        def _():
            copy.wait()

    def clear():
        dk_acc[...] = jnp.zeros_like(dk_acc)
        dv_acc[...] = jnp.zeros_like(dv_acc)
        gains[...] = jnp.zeros_like(gains)
        owner_of = lax.broadcasted_iota(jnp.int32, (D, 128), 0) // HD
        own = owner_of == lax.broadcasted_iota(jnp.int32, (D, 128), 1)
        marks[...] = own.astype(F32).astype(BF16)

    greet(section, sections)
    scatter_rows(section, sections, per, tokens, inbox, arrivals, first_sends, 0)
    scatter_rows(section, sections, per, cotangent, grads, grad_arrivals, grad_first_sends, last)
    low, high, is_low = lane_masks()
    centered = jnp.where(section == 0, 1.0, 0.0).astype(F32)

    @pl.when(section != 0)
    def _():
        clear()

    def keep_forward(chunk, slot):
        pairs = (
            (b_q, s_q),
            (b_na, s_na),
            (b_mixed, s_mixed),
            (b_lse, s_lse),
            (b_mid, s_mid),
            (b_nm, s_nm),
            (b_act, s_act),
            (b_dg, s_dg),
        )
        return [
            pltpu.make_async_copy(src.at[slot], dst.at[chunk], kept_f.at[kind, slot])
            for kind, (src, dst) in enumerate(pairs)
        ]

    def forward_chunk(chunk, carry):
        slot = lax.rem(chunk, 2)

        @pl.when(chunk >= 2)
        def _():
            for copy in keep_forward(chunk - 2, slot):
                copy.wait()

        todo = keep_forward(chunk, slot)
        at_first(chunk, weights[0])
        fill_bias(docs, chunk, bias_f, False)
        await_arrival(inbox.at[chunk], arrivals.at[chunk])
        x = inbox[chunk].astype(F32)
        x = x - centered * row_mean(x)
        na = (x * lax.rsqrt(row_mean(x * x) + EPS) * gain_a[...]).astype(BF16)
        b_na[slot] = na
        todo[1].start()
        b_q[slot] = (dot(na, w_qkv[:, :D]).astype(BF16) * (HD**-0.5)).astype(BF16)
        here = pl.ds(pl.multiple_of(chunk * C, C), C)
        kbuf[here, :] = dot(na, w_qkv[:, D : 2 * D]).astype(BF16)
        vbuf[here, :] = dot(na, w_qkv[:, 2 * D :]).astype(BF16)
        todo[0].start()
        lane = lax.broadcasted_iota(jnp.int32, (1, 128), 1)

        def attend(blocks):
            window = pl.ds(pl.multiple_of((chunk - blocks + 1) * C, C), blocks * C)
            masked = slice((WIN - blocks) * C, WIN * C)
            lse_all = jnp.zeros((C, 128), F32)
            for pair in range(PAIRS):
                lanes = slice(pair * 2 * HD, (pair + 1) * 2 * HD)
                q2 = two_heads(b_q[slot, :, lanes], low, high)
                s = dot_nt(q2, kbuf[window, lanes]).reshape(2, C, blocks * C) + bias_f[:, masked][None]
                top = jnp.max(s, axis=-1, keepdims=True)
                e = jnp.exp(s - top)
                total = jnp.sum(e, axis=-1, keepdims=True)
                o = dot(e.astype(BF16).reshape(2 * C, blocks * C), vbuf[window, lanes])
                o = o.reshape(2, C, 2 * HD) * (1.0 / total)
                b_mixed[slot, :, lanes] = jnp.where(is_low, o[0], o[1]).astype(BF16)
                lse = top + jnp.log(total)
                lse_all = jnp.where(lane == 2 * pair, lse[0], lse_all)
                lse_all = jnp.where(lane == 2 * pair + 1, lse[1], lse_all)
            b_lse[slot] = jnp.transpose(lse_all)[:16]

        by_blocks(docs, chunk, attend)
        todo[2].start()
        todo[3].start()
        at_first(chunk, weights[1])
        branch = dot(b_mixed[slot], w_out[...])
        mid = x + branch - row_mean(branch)
        b_mid[slot] = mid
        todo[4].start()
        nm = (mid * lax.rsqrt(row_mean(mid * mid) + EPS) * gain_m[...]).astype(BF16)
        b_nm[slot] = nm
        todo[5].start()
        at_first(chunk, weights[2])
        k0 = 0.7978845608028654
        k1 = 0.044715
        for part in range(FF // D):
            cols = slice(part * D, (part + 1) * D)
            h = dot(nm, w_up[:, cols])
            h2 = h * h
            t = jnp.tanh(h * (k0 + (k0 * k1) * h2))
            half = 0.5 + 0.5 * t
            b_act[slot, :, cols] = (h * half).astype(BF16)
            slope = half + (h * (1.0 - t * t)) * (0.5 * k0 + (1.5 * k0 * k1) * h2)
            b_dg[slot, :, cols] = slope.astype(BF16)
        todo[6].start()
        todo[7].start()
        at_first(chunk, weights[3])
        branch = dot(b_act[slot], w_down[...])

        @pl.when(chunk >= 2)
        def _():
            await_arrival(outbox.at[slot], sends.at[chunk - 2])

        outbox[slot] = (b_mid[slot] + branch - row_mean(branch)).astype(BF16)
        pass_on(section, chunk, per, last, 1, outbox.at[slot], inbox, result, sends, arrivals, landed)
        return carry

    lax.fori_loop(0, chunks, forward_chunk, 0)
    for chunk in (chunks - 2, chunks - 1):
        for copy in keep_forward(chunk, chunk % 2):
            copy.wait()

    @pl.when(section == 0)
    def _():
        clear()

    def fetches(chunk, slot):
        pairs = ((s_dg, b_dg), (s_mid, b_mid), (s_mixed, b_mixed), (s_q, b_q), (s_lse, b_lse))
        return [
            pltpu.make_async_copy(src.at[chunk], dst.at[slot], loads.at[kind, slot])
            for kind, (src, dst) in enumerate(pairs)
        ]

    def keep_backward(chunk, slot):
        pairs = ((b_nm, s_db), (b_act, s_dh), (b_na, s_da), (b_dt, s_dt))
        return [
            pltpu.make_async_copy(src.at[slot], dst.at[chunk], kept_b.at[kind, slot])
            for kind, (src, dst) in enumerate(pairs)
        ]

    def folded(v):
        return jnp.sum(v.reshape(C // 8, 8, D), axis=0)

    def backward_chunk(step, carry):
        chunk = chunks - 1 - step
        slot = lax.rem(chunk, 2)

        @pl.when((step >= 1) & (chunk >= 1))
        def _():
            for copy in fetches(chunk - 1, 1 - slot):
                copy.start()

        @pl.when(step >= 2)
        def _():
            for copy in keep_backward(chunk + 2, slot):
                copy.wait()

        @pl.when(step >= 2)
        def _():
            for copy in fetches(chunk, slot):
                copy.wait()

        todo = keep_backward(chunk, slot)
        fill_bias(docs, chunk, bias_b, True)
        await_arrival(grads.at[chunk], grad_arrivals.at[chunk])
        g = grads[chunk].astype(F32)
        db = (g - row_mean(g)).astype(BF16)
        b_nm[slot] = db
        todo[0].start()
        for part in range(FF // D):
            cols = slice(part * D, (part + 1) * D)
            d_active = dot_nt(db, w_down[cols, :])
            b_act[slot, :, cols] = (d_active * b_dg[slot, :, cols].astype(F32)).astype(BF16)
        todo[1].start()
        dn = dot_nt(b_act[slot], w_up[...])
        mid = b_mid[slot]
        factor = lax.rsqrt(row_mean(mid * mid) + EPS)
        unit = mid * factor
        gains[1] += folded(dn * unit)
        dn = dn * gain_m[...]
        d_mid = g + factor * (dn - unit * row_mean(dn * unit))
        da = (d_mid - row_mean(d_mid)).astype(BF16)
        b_na[slot] = da
        todo[2].start()
        b_mid[slot] = d_mid
        dmix = dot_nt(da, w_out[...]).astype(BF16)
        b_dmix[...] = dmix
        prod = dmix.astype(F32) * b_mixed[slot].astype(F32)
        top = prod.astype(BF16)
        rest = (prod - top.astype(F32)).astype(BF16)
        inner = dot(top, marks[...]) + dot(rest, marks[...])
        lse_d[...] = jnp.transpose(inner)[:16]
        def attend(blocks):
            window = pl.ds(pl.multiple_of((chunk - blocks + 1) * C, C), blocks * C)
            masked = slice((WIN - blocks) * C, WIN * C)
            for pair in range(PAIRS):
                lanes = slice(pair * 2 * HD, (pair + 1) * 2 * HD)
                q2 = two_heads(b_q[slot, :, lanes], low, high)
                do2 = two_heads(b_dmix[:, lanes], low, high)
                keys = kbuf[window, lanes]
                values = vbuf[window, lanes]
                both = jnp.concatenate([bias_b[masked, :], bias_b[masked, :]], axis=1)
                even, odd = slice(2 * pair, 2 * pair + 1), slice(2 * pair + 1, 2 * pair + 2)
                lse = jnp.concatenate([b_lse[slot, even, :], b_lse[slot, odd, :]], axis=1)
                inner = jnp.concatenate([lse_d[even, :], lse_d[odd, :]], axis=1)
                probs = jnp.exp(dot_nt(keys, q2) + both - lse)
                ds = (probs * (dot_nt(values, do2) - inner)).astype(BF16)
                dv = dot(probs.astype(BF16), do2)
                dk = dot(ds, q2)
                for part in range(blocks):
                    place = lax.rem(chunk - blocks + 1 + part, WIN)
                    rows = slice(part * C, (part + 1) * C)
                    dv_acc[place, :, lanes] += dv[rows]
                    dk_acc[place, :, lanes] += dk[rows]
                dq = dot(jnp.transpose(keys), ds)
                dq = jnp.concatenate([dq[:HD, :C], dq[HD:, C:]], axis=0)
                b_dt[slot, :, lanes] = (jnp.transpose(dq) * (HD**-0.5)).astype(BF16)

        by_blocks(docs, chunk, attend)
        done = lax.rem(chunk, WIN)
        b_dt[slot, :, D : 2 * D] = dk_acc[done].astype(BF16)
        b_dt[slot, :, 2 * D :] = dv_acc[done].astype(BF16)
        dk_acc[done] = jnp.zeros((C, D), F32)
        dv_acc[done] = jnp.zeros((C, D), F32)
        todo[3].start()
        dn = dot_nt(b_dt[slot], w_qkv[...])
        x = inbox[chunk].astype(F32)
        x = x - centered * row_mean(x)
        factor = lax.rsqrt(row_mean(x * x) + EPS)
        unit = x * factor
        gains[0] += folded(dn * unit)
        dn = dn * gain_a[...]
        grad = b_mid[slot] + factor * (dn - unit * row_mean(dn * unit))
        grad = grad - centered * row_mean(grad)
        inbox[chunk] = grad.astype(BF16)
        pass_on(
            section, chunk, per, 0, -1, inbox.at[chunk], grads, grad_result, grad_sends, grad_arrivals, grad_landed
        )
        return carry

    lax.fori_loop(0, chunks, backward_chunk, 0)
    for chunk in (0, 1):
        for copy in keep_backward(chunk, chunk):
            copy.wait()
    drain_rows(section, sections, per, tokens, first_sends, 0)
    drain_rows(section, sections, per, cotangent, grad_first_sends, last)
    settle(section, chunks - 2, chunks, per, last, outbox.at[0], result, sends, landed)
    settle(section, 0, chunks, per, 0, inbox.at[0], grad_result, grad_sends, grad_landed)


ANY = pl.BlockSpec(memory_space=pl.ANY)
IN_VMEM = pl.BlockSpec(memory_space=pltpu.VMEM)
DMA = pltpu.SemaphoreType.DMA


def layers(sections, chunks, tokens, cotangent, docs, weights):
    per = chunks // sections
    sds = jax.ShapeDtypeStruct
    staged = (
        ("q", (C, D), BF16),
        ("na", (C, D), BF16),
        ("mixed", (C, D), BF16),
        ("lse", (16, C), F32),
        ("mid", (C, D), F32),
        ("nm", (C, D), BF16),
        ("act", (C, FF), BF16),
        ("dg", (C, FF), BF16),
    )
    saved = staged + (
        ("db", (C, D), BF16),
        ("dh", (C, FF), BF16),
        ("da", (C, D), BF16),
        ("dt", (C, 3 * D), BF16),
    )
    outs = pl.pallas_call(
        functools.partial(layer_kernel, sections),
        out_shape=[sds((per, C, D), BF16)] * 2
        + [sds((2, 8, D), F32)]
        + [sds((chunks,) + s, t) for _, s, t in saved],
        in_specs=[ANY] * 2 + [IN_VMEM] * 3 + [ANY] * 4,
        out_specs=[ANY] * 2 + [IN_VMEM] + [ANY] * len(saved),
        scratch_shapes=[pltpu.VMEM(shape, BF16) for shape in ((D, 3 * D), (D, D), (D, FF), (FF, D))]
        + [
            pltpu.VMEM((chunks, C, D), BF16),
            pltpu.VMEM((2, C, D), BF16),
            pltpu.VMEM((chunks, C, D), BF16),
            pltpu.VMEM((chunks * C, D), BF16),
            pltpu.VMEM((chunks * C, D), BF16),
            pltpu.VMEM((C, WIN * C), F32),
            pltpu.VMEM((WIN * C, C), F32),
            pltpu.VMEM((WIN, C, D), F32),
            pltpu.VMEM((WIN, C, D), F32),
            pltpu.VMEM((16, C), F32),
            pltpu.VMEM((C, D), BF16),
            pltpu.VMEM((D, 128), BF16),
        ]
        + [pltpu.VMEM((2,) + s, t) for _, s, t in staged]
        + [pltpu.VMEM((2, C, 3 * D), BF16)]
        + [DMA((chunks,)), DMA((chunks,)), DMA((per,)), DMA((per,))] * 2
        + [DMA((8, 2)), DMA((4, 2)), DMA((5, 2)), DMA((4,))],
        compiler_params=pltpu.CompilerParams(
            collective_id=0, has_side_effects=True, vmem_limit_bytes=VMEM_LIMIT
        ),
        name="layers",
    )(tokens.reshape(per, C, D), cotangent.reshape(per, C, D), docs, *weights)
    return outs[0], outs[1], outs[2], {name: out for (name, _, _), out in zip(saved, outs[3:])}


def matmul_lt(left_side, right_side):
    rows = left_side.shape[0] * left_side.shape[1]
    return lax.dot_general(
        left_side.reshape(rows, -1),
        right_side.reshape(rows, -1),
        (((0,), (0,)), ((), ())),
        preferred_element_type=F32,
    )


UNIT = 256
UNITS = 9 + 3 + 12 + 12
NARROW = 9 + 3 + 12
LAGS = (4, 8, 12)


def pair_first(unit):
    return lax.rem(unit, 4) != 3


def dot_tn(a, b):
    return lax.dot_general(a, b, (((0,), (0,)), ((), ())), preferred_element_type=F32)


def weight_grad_kernel(
    s_na,
    s_dt,
    s_mixed,
    s_da,
    s_nm,
    s_dh,
    s_act,
    s_db,
    gains,
    o_qkv,
    o_out,
    o_up,
    o_down,
    o_gains,
    left,
    right,
    act,
    made,
    got_a,
    got_b,
    got_c,
    total,
    gain_own,
    gain_in,
    left_sems,
    right_sems,
    act_sem,
    a_sends,
    a_arrivals,
    b_sends,
    b_arrivals,
    c_sends,
    c_arrivals,
    out_sem,
    gain_sends,
    gain_arrivals,
):
    section = lax.axis_index("section")
    dp = lax.axis_index("dp")
    x, near, far = lax.rem(dp, 2), lax.rem(dp // 2, 2), dp // 4
    over_x, over_near, over_far = dp + 1 - 2 * x, dp + 2 - 4 * near, dp + 4 - 8 * far

    def load_left(src, slot):
        return pltpu.make_async_copy(src, left.at[slot], left_sems.at[slot])

    def load_right(src, column, slot):
        columns = pl.ds(pl.multiple_of(column * UNIT, UNIT), UNIT)
        return pltpu.make_async_copy(src.at[:, columns], right.at[slot], right_sems.at[slot])

    def start_right(unit):
        slot = lax.rem(unit, 2)

        @pl.when(unit < 9)
        def _():
            load_right(s_dt, unit, slot).start()

        @pl.when((unit >= 9) & (unit < 12))
        def _():
            load_right(s_da, unit - 9, slot).start()

        @pl.when((unit >= 12) & (unit < NARROW))
        def _():
            load_right(s_dh, unit - 12, slot).start()

    load_left(s_na, 0).start()
    start_right(0)
    load_left(s_mixed, 1).start()
    pltpu.make_async_copy(s_act, act, act_sem).start()
    gain_own[...] = jnp.sum(gains[...], axis=1, keepdims=True) + jnp.zeros((2, 8, D), F32)

    barrier = pltpu.get_barrier_semaphore()
    for step in range(1, 8):
        other = lax.rem(dp + step, 8)
        pl.semaphore_signal(barrier, inc=1, device_id=(other, section), device_id_type=MESH)
    pl.semaphore_wait(barrier, 7)

    def gain_copy(step):
        other = lax.rem(dp + step, 8)
        return pltpu.make_async_remote_copy(
            gain_own,
            gain_in.at[step - 1],
            gain_sends.at[step - 1],
            gain_arrivals.at[step - 1],
            device_id=(other, section),
            device_id_type=MESH,
        )

    for step in range(1, 8):
        gain_copy(step).start()

    def send(unit, src, dst, sends, arrivals, to):
        pltpu.make_async_remote_copy(
            src,
            dst.at[unit],
            sends.at[unit],
            arrivals.at[unit],
            device_id=(to, section),
            device_id_type=MESH,
        ).start()

    def first_add(unit):
        @pl.when(pair_first(unit))
        def _():
            send(unit, made.at[unit, 1 - x], got_a, a_sends, a_arrivals, over_x)

        @pl.when(jnp.logical_not(pair_first(unit)))
        def _():
            send(unit, made.at[unit, :, 1 - near], got_a, a_sends, a_arrivals, over_near)

    def second_add(unit):
        await_arrival(got_a.at[unit], a_arrivals.at[unit])

        @pl.when(pair_first(unit))
        def _():
            made[unit, x] = (made[unit, x].astype(F32) + got_a[unit].astype(F32)).astype(BF16)
            send(unit, made.at[unit, x, 1 - near], got_b, b_sends, b_arrivals, over_near)

        @pl.when(jnp.logical_not(pair_first(unit)))
        def _():
            made[unit, :, near] = (made[unit, :, near].astype(F32) + got_a[unit].astype(F32)).astype(BF16)
            send(unit, made.at[unit, 1 - x, near], got_b, b_sends, b_arrivals, over_x)

    def third_add(unit):
        await_arrival(got_b.at[unit], b_arrivals.at[unit])
        made[unit, x, near] = (made[unit, x, near].astype(F32) + got_b[unit].astype(F32)).astype(BF16)
        send(unit, made.at[unit, x, near, 1 - far], got_c, c_sends, c_arrivals, over_far)

    def finish(unit):
        await_arrival(got_c.at[unit], c_arrivals.at[unit])
        total[unit] = made[unit, x, near, far].astype(F32) + got_c[unit].astype(F32)
        deliver(unit)

    def deliver(unit):
        for first, end, ref in ((0, 9, o_qkv), (9, 12, o_out), (12, NARROW, o_up)):

            @pl.when((unit >= first) & (unit < end))
            def _():
                columns = pl.ds(pl.multiple_of((unit - first) * UNIT, UNIT), UNIT)
                pltpu.make_async_copy(total.at[unit], ref.at[:, columns], out_sem).start()

        @pl.when(unit >= NARROW)
        def _():
            column, row = (unit - NARROW) // 4, lax.rem(unit - NARROW, 4)
            columns = pl.ds(pl.multiple_of(column * UNIT, UNIT), UNIT)
            rows = pl.ds(pl.multiple_of(row * 96, 96), 96)
            pltpu.make_async_copy(total.at[unit], o_down.at[rows, columns], out_sem).start()

    def advance(now):
        for lag, action in zip(LAGS[::-1], (finish, third_add, second_add)):

            @pl.when((now >= lag) & (now - lag < UNITS))
            def _():
                action(now - lag)

    def narrow(unit, carry):
        slot = lax.rem(unit, 2)
        side = jnp.where((unit >= 9) & (unit < 12), 1, 0)

        @pl.when(unit == 9)
        def _():
            load_left(s_nm, 0).start()

        @pl.when(unit == 12)
        def _():
            load_left(s_db, 1).start()

        start_right(unit + 1)

        @pl.when((unit == 0) | (unit == 12))
        def _():
            load_left(s_na, 0).wait()

        @pl.when(unit == 9)
        def _():
            load_left(s_mixed, 1).wait()

        load_right(s_dt, 0, slot).wait()
        grad = dot_tn(left[side], right[slot]).astype(BF16)
        for shard in range(8):
            made[unit, shard % 2, shard // 2 % 2, shard // 4] = grad[shard * 96 : (shard + 1) * 96]
        first_add(unit)
        advance(unit)
        return carry

    lax.fori_loop(0, NARROW, narrow, 0)
    load_left(s_db, 1).wait()
    pltpu.make_async_copy(s_act, act, act_sem).wait()

    def wide(step, carry):
        column, shard = step // 8, lax.rem(step, 8)
        columns = pl.ds(pl.multiple_of(column * UNIT, UNIT), UNIT)
        rows = pl.ds(pl.multiple_of(shard * 384, 384), 384)
        grad = dot_tn(act[:, rows], left[1, :, columns]).astype(BF16)
        first = NARROW + 4 * column
        for part in range(4):
            made[first + part, lax.rem(shard, 2), lax.rem(shard // 2, 2), shard // 4] = grad[part * 96 : (part + 1) * 96]

        @pl.when(shard == 7)
        def _():
            for part in range(4):
                first_add(first + part)

        @pl.when(lax.rem(step, 2) == 1)
        def _():
            advance(NARROW + step // 2)

        return carry

    lax.fori_loop(0, 24, wide, 0)

    def drain(now, carry):
        advance(now)
        return carry

    lax.fori_loop(UNITS, UNITS + LAGS[-1], drain, 0)
    for step in range(1, 8):
        gain_copy(step).wait()
    sums = gain_own[:, 0:1]
    for step in range(7):
        sums = sums + gain_in[step, :, 0:1]
    o_gains[...] = sums

    def sent(unit, carry):
        await_arrival(got_a.at[unit], a_sends.at[unit])
        await_arrival(got_b.at[unit], b_sends.at[unit])
        await_arrival(got_c.at[unit], c_sends.at[unit])
        return carry

    lax.fori_loop(0, UNITS, sent, 0)
    await_arrival(total, out_sem)


def weight_grads(na, dt, mixed, da, nm, dh, act, db, gains):
    tokens = na.shape[0] * na.shape[1]
    sds = jax.ShapeDtypeStruct
    operands = [v.reshape(tokens, -1) for v in (na, dt, mixed, da, nm, dh, act, db)]
    return pl.pallas_call(
        weight_grad_kernel,
        out_shape=[
            sds((96, 3 * D), F32),
            sds((96, D), F32),
            sds((96, FF), F32),
            sds((384, D), F32),
            sds((2, 1, D), F32),
        ],
        in_specs=[ANY] * 8 + [IN_VMEM],
        out_specs=[ANY] * 4 + [IN_VMEM],
        scratch_shapes=[
            pltpu.VMEM((2, tokens, D), BF16),
            pltpu.VMEM((2, tokens, UNIT), BF16),
            pltpu.VMEM((tokens, FF), BF16),
            pltpu.VMEM((UNITS, 2, 2, 2, 96, UNIT), BF16),
            pltpu.VMEM((UNITS, 2, 2, 96, UNIT), BF16),
            pltpu.VMEM((UNITS, 2, 96, UNIT), BF16),
            pltpu.VMEM((UNITS, 96, UNIT), BF16),
            pltpu.VMEM((UNITS, 96, UNIT), F32),
            pltpu.VMEM((2, 8, D), F32),
            pltpu.VMEM((7, 2, 8, D), F32),
            DMA((2,)),
            DMA((2,)),
            DMA,
            DMA((UNITS,)),
            DMA((UNITS,)),
            DMA((UNITS,)),
            DMA((UNITS,)),
            DMA((UNITS,)),
            DMA((UNITS,)),
            DMA,
            DMA((7,)),
            DMA((7,)),
        ],
        compiler_params=pltpu.CompilerParams(
            collective_id=2, has_side_effects=True, vmem_limit_bytes=VMEM_LIMIT
        ),
        name="weight_grads",
    )(*operands, gains)


def hand_over_kernel(gains, *refs):
    sources, results, (gain_attn, gain_mlp), held = refs[:6], refs[6:12], refs[12:14], refs[14:20]
    come, go = refs[20], refs[21]
    arriving = [
        pltpu.make_async_copy(src, buf, come.at[at]) for at, (src, buf) in enumerate(zip(sources, held))
    ]
    leaving = [
        pltpu.make_async_copy(buf, dst, go.at[at]) for at, (buf, dst) in enumerate(zip(held, results))
    ]
    for copy in arriving:
        copy.start()
    shift = lax.rem(D - 96 * lax.axis_index("dp"), D)
    for kind, ref in enumerate((gain_attn, gain_mlp)):
        turned = pltpu.roll(jnp.broadcast_to(gains[kind], (8, D)), shift, 1)
        ref[...] = turned[:1, :96]
    for copy, onward in zip(arriving, leaving):
        copy.wait()
        onward.start()
    for copy in leaving:
        copy.wait()


def hand_over(output, input_grad, shards, gains):
    sds = jax.ShapeDtypeStruct
    sources = (output, input_grad, *shards)
    outs = pl.pallas_call(
        hand_over_kernel,
        out_shape=[sds(v.shape, v.dtype) for v in sources] + [sds((1, 96), F32)] * 2,
        in_specs=[IN_VMEM] + [ANY] * 6,
        out_specs=[ANY] * 6 + [IN_VMEM] * 2,
        scratch_shapes=[pltpu.VMEM(v.shape, v.dtype) for v in sources] + [DMA((6,)), DMA((6,))],
        compiler_params=pltpu.CompilerParams(vmem_limit_bytes=VMEM_LIMIT),
        name="hand_over",
    )(gains, *sources)
    output, input_grad, qkv, out, up, down, gain_attn, gain_mlp = outs
    return output, input_grad, gain_attn, qkv[None], out[None], gain_mlp, up[None], down[None]


def body(tokens, cotangent, doc_ids, gain_attn, w_qkv, w_out, gain_mlp, w_up, w_down):
    sections = lax.axis_size("section")
    rows, seq = doc_ids.shape
    chunks = rows * seq // C
    weights = (gain_attn, gain_mlp, w_qkv[0], w_out[0], w_up[0], w_down[0])
    output, input_grad, gains, kept = layers(sections, chunks, tokens, cotangent, doc_ids, weights)
    db, dh, da, dt = kept["db"], kept["dh"], kept["da"], kept["dt"]
    if lax.axis_size("dp") == 8 and chunks == 8:
        qkv, out, up, down, gains = weight_grads(
            kept["na"], dt, kept["mixed"], da, kept["nm"], dh, kept["act"], db, gains
        )
        return hand_over(
            output.reshape(tokens.shape), input_grad.reshape(cotangent.shape), (qkv, out, up, down), gains
        )
    gains = jnp.sum(gains, axis=1)
    grads = (
        gains[0],
        matmul_lt(kept["na"], dt),
        matmul_lt(kept["mixed"], da),
        gains[1],
        matmul_lt(kept["nm"], dh),
        matmul_lt(kept["act"], db),
    )
    shards = lax.psum_scatter(grads, "dp", scatter_dimension=0, tiled=True)
    return (
        output.reshape(tokens.shape),
        input_grad.reshape(cotangent.shape),
        *(shard[None] for shard in shards),
    )


def solution(mesh):
    rows = P(("dp", "section"), None)
    layer = P("section", None)
    matrix = P("section", None, None)
    in_specs = (rows, rows, P("dp", None), layer, matrix, matrix, layer, matrix, matrix)
    split = P("section", "dp")
    split_matrix = P("section", "dp", None)
    out_specs = (rows, rows, split, split_matrix, split_matrix, split, split_matrix, split_matrix)
    return jax.shard_map(body, mesh=mesh, in_specs=in_specs, out_specs=out_specs, check_vma=False)
```

```python
import functools

import jax
import jax.numpy as jnp
from jax import lax
from jax.experimental import pallas as pl
from jax.experimental.pallas import tpu as pltpu
from jax.sharding import PartitionSpec as P

D = 768
HEADS = 12
HD = 64
FF = 3072
C = 256
WIN = 3
PAIRS = HEADS // 2
EPS = 1e-05
NEG = -1e30
MESH = pl.DeviceIdType.MESH
BF16 = jnp.bfloat16
F32 = jnp.float32
VMEM_LIMIT = 60 * 1024 * 1024


def dot(a, b):
    return jnp.dot(a, b, preferred_element_type=F32)


def dot_nt(a, b):
    return lax.dot_general(a, b, (((1,), (1,)), ((), ())), preferred_element_type=F32)


def row_mean(v):
    return jnp.mean(v, axis=-1, keepdims=True)


def greet(section, sections):
    dp = lax.axis_index("dp")
    barrier = pltpu.get_barrier_semaphore()
    for step in range(1, sections):
        other = lax.rem(section + step, sections)
        pl.semaphore_signal(barrier, inc=1, device_id=(dp, other), device_id_type=MESH)
    pl.semaphore_wait(barrier, sections - 1)


def lane_masks():
    lane = lax.broadcasted_iota(jnp.int32, (1, 2 * HD), 1)
    low = (lane < HD).astype(F32)
    return low.astype(BF16), (1.0 - low).astype(BF16), lane < HD


def two_heads(pair, low, high):
    return jnp.concatenate([pair * low, pair * high], axis=0)


def await_arrival(buf, sem):
    pltpu.make_async_copy(buf, buf, sem).wait()


def scatter_rows(section, sections, per, rows, inbox, sems, send_sems, target):
    dp = lax.axis_index("dp")
    for piece in range(per):
        slot = section * per + piece

        @pl.when(section != target)
        def _():
            pltpu.make_async_remote_copy(
                rows.at[piece],
                inbox.at[slot],
                send_sems.at[piece],
                sems.at[slot],
                device_id=(dp, target),
                device_id_type=MESH,
            ).start()

        @pl.when(section == target)
        def _():
            pltpu.make_async_copy(rows.at[piece], inbox.at[slot], sems.at[slot]).start()


def drain_rows(section, sections, per, rows, send_sems, target):
    for piece in range(per):

        @pl.when(section != target)
        def _():
            pltpu.make_async_copy(rows.at[piece], rows.at[piece], send_sems.at[piece]).wait()


def pass_on(section, chunk, per, last, step, source, inbox, result, sends, arrivals, landed):
    dp = lax.axis_index("dp")
    owner = chunk // per

    @pl.when(section != last)
    def _():
        pltpu.make_async_remote_copy(
            source,
            inbox.at[chunk],
            sends.at[chunk],
            arrivals.at[chunk],
            device_id=(dp, section + step),
            device_id_type=MESH,
        ).start()

    @pl.when((section == last) & (owner != last))
    def _():
        pltpu.make_async_remote_copy(
            source,
            result.at[lax.rem(chunk, per)],
            sends.at[chunk],
            landed.at[lax.rem(chunk, per)],
            device_id=(dp, owner),
            device_id_type=MESH,
        ).start()

    @pl.when((section == last) & (owner == last))
    def _():
        pltpu.make_async_copy(source, result.at[lax.rem(chunk, per)], sends.at[chunk]).start()


def settle(section, first, end, per, last, source, result, sends, landed):
    def one(chunk, carry):
        await_arrival(source, sends.at[chunk])
        return carry

    lax.fori_loop(first, end, one, 0)
    for piece in range(per):

        @pl.when(section != last)
        def _():
            await_arrival(result.at[piece], landed.at[piece])


def fill_bias(docs, chunk, bias, keys_down):
    per_row = docs.shape[1] // C
    row, place = chunk // per_row, lax.rem(chunk, per_row)

    def numbers(block):
        start = pl.multiple_of(jnp.maximum(block, 0) * C, C)
        return docs[pl.ds(row, 1), pl.ds(start, C)].astype(F32)

    def upright(line):
        return jnp.transpose(jnp.broadcast_to(line, (128, C)))

    queries = numbers(place)
    if not keys_down:
        queries = upright(queries)
    for part in range(WIN):
        keys = numbers(place - (WIN - 1) + part)
        if keys_down:
            keys = upright(keys)
        for half in range(C // 128):
            lanes = slice(half * 128, (half + 1) * 128)
            allowed = keys == queries[:, lanes] if keys_down else queries == keys[:, lanes]
            if part == WIN - 1:
                down = lax.broadcasted_iota(jnp.int32, (C, 128), 0)
                across = lax.broadcasted_iota(jnp.int32, (C, 128), 1) + half * 128
                allowed = allowed & ((down <= across) if keys_down else (across <= down))
            term = jnp.where(allowed, 0.0, NEG)
            if keys_down:
                bias[part * C : (part + 1) * C, lanes] = term
            else:
                bias[:, part * C + half * 128 : part * C + (half + 1) * 128] = term


def by_blocks(docs, chunk, attend):
    place = lax.rem(chunk, docs.shape[1] // C)
    for blocks in range(1, WIN + 1):

        @pl.when((place == blocks - 1) if blocks < WIN else (place >= WIN - 1))
        def _():
            attend(blocks)


def layer_kernel(
    sections,
    tokens,
    cotangent,
    docs,
    gain_a,
    gain_m,
    h_qkv,
    h_out,
    h_up,
    h_down,
    result,
    grad_result,
    gains,
    s_q,
    s_na,
    s_mixed,
    s_lse,
    s_mid,
    s_nm,
    s_act,
    s_dg,
    s_db,
    s_dh,
    s_da,
    s_dt,
    w_qkv,
    w_out,
    w_up,
    w_down,
    inbox,
    outbox,
    grads,
    kbuf,
    vbuf,
    bias_f,
    bias_b,
    dk_acc,
    dv_acc,
    lse_d,
    b_dmix,
    marks,
    b_q,
    b_na,
    b_mixed,
    b_lse,
    b_mid,
    b_nm,
    b_act,
    b_dg,
    b_dt,
    arrivals,
    sends,
    first_sends,
    landed,
    grad_arrivals,
    grad_sends,
    grad_first_sends,
    grad_landed,
    kept_f,
    kept_b,
    loads,
    weight_sems,
):
    section = lax.axis_index("section")
    chunks = inbox.shape[0]
    per = tokens.shape[0]
    last = sections - 1
    weights = [
        pltpu.make_async_copy(src, dst, weight_sems.at[kind])
        for kind, (src, dst) in enumerate(
            ((h_qkv, w_qkv), (h_out, w_out), (h_up, w_up), (h_down, w_down))
        )
    ]
    for copy in weights:
        copy.start()

    def at_first(chunk, copy):
        @pl.when(chunk == 0)
        def _():
            copy.wait()

    def clear():
        dk_acc[...] = jnp.zeros_like(dk_acc)
        dv_acc[...] = jnp.zeros_like(dv_acc)
        gains[...] = jnp.zeros_like(gains)
        owner_of = lax.broadcasted_iota(jnp.int32, (D, 128), 0) // HD
        own = owner_of == lax.broadcasted_iota(jnp.int32, (D, 128), 1)
        marks[...] = own.astype(F32).astype(BF16)

    greet(section, sections)
    scatter_rows(section, sections, per, tokens, inbox, arrivals, first_sends, 0)
    scatter_rows(section, sections, per, cotangent, grads, grad_arrivals, grad_first_sends, last)
    low, high, is_low = lane_masks()
    centered = jnp.where(section == 0, 1.0, 0.0).astype(F32)

    @pl.when(section != 0)
    def _():
        clear()

    def keep_forward(chunk, slot):
        pairs = (
            (b_q, s_q),
            (b_na, s_na),
            (b_mixed, s_mixed),
            (b_lse, s_lse),
            (b_mid, s_mid),
            (b_nm, s_nm),
            (b_act, s_act),
            (b_dg, s_dg),
        )
        return [
            pltpu.make_async_copy(src.at[slot], dst.at[chunk], kept_f.at[kind, slot])
            for kind, (src, dst) in enumerate(pairs)
        ]

    def forward_chunk(chunk, carry):
        slot = lax.rem(chunk, 2)

        @pl.when(chunk >= 2)
        def _():
            for copy in keep_forward(chunk - 2, slot):
                copy.wait()

        todo = keep_forward(chunk, slot)
        at_first(chunk, weights[0])
        fill_bias(docs, chunk, bias_f, False)
        await_arrival(inbox.at[chunk], arrivals.at[chunk])
        x = inbox[chunk].astype(F32)
        x = x - centered * row_mean(x)
        na = (x * lax.rsqrt(row_mean(x * x) + EPS) * gain_a[...]).astype(BF16)
        b_na[slot] = na
        todo[1].start()
        b_q[slot] = (dot(na, w_qkv[:, :D]).astype(BF16) * (HD**-0.5)).astype(BF16)
        here = pl.ds(pl.multiple_of(chunk * C, C), C)
        kbuf[here, :] = dot(na, w_qkv[:, D : 2 * D]).astype(BF16)
        vbuf[here, :] = dot(na, w_qkv[:, 2 * D :]).astype(BF16)
        todo[0].start()
        lane = lax.broadcasted_iota(jnp.int32, (1, 128), 1)

        def attend(blocks):
            window = pl.ds(pl.multiple_of((chunk - blocks + 1) * C, C), blocks * C)
            masked = slice((WIN - blocks) * C, WIN * C)
            lse_all = jnp.zeros((C, 128), F32)
            for pair in range(PAIRS):
                lanes = slice(pair * 2 * HD, (pair + 1) * 2 * HD)
                q2 = two_heads(b_q[slot, :, lanes], low, high)
                s = dot_nt(q2, kbuf[window, lanes]).reshape(2, C, blocks * C) + bias_f[:, masked][None]
                top = jnp.max(s, axis=-1, keepdims=True)
                e = jnp.exp(s - top)
                total = jnp.sum(e, axis=-1, keepdims=True)
                o = dot(e.astype(BF16).reshape(2 * C, blocks * C), vbuf[window, lanes])
                o = o.reshape(2, C, 2 * HD) * (1.0 / total)
                b_mixed[slot, :, lanes] = jnp.where(is_low, o[0], o[1]).astype(BF16)
                lse = top + jnp.log(total)
                lse_all = jnp.where(lane == 2 * pair, lse[0], lse_all)
                lse_all = jnp.where(lane == 2 * pair + 1, lse[1], lse_all)
            b_lse[slot] = jnp.transpose(lse_all)[:16]

        by_blocks(docs, chunk, attend)
        todo[2].start()
        todo[3].start()
        at_first(chunk, weights[1])
        branch = dot(b_mixed[slot], w_out[...])
        mid = x + branch - row_mean(branch)
        b_mid[slot] = mid
        todo[4].start()
        nm = (mid * lax.rsqrt(row_mean(mid * mid) + EPS) * gain_m[...]).astype(BF16)
        b_nm[slot] = nm
        todo[5].start()
        at_first(chunk, weights[2])
        k0 = 0.7978845608028654
        k1 = 0.044715
        for part in range(FF // D):
            cols = slice(part * D, (part + 1) * D)
            h = dot(nm, w_up[:, cols])
            h2 = h * h
            t = jnp.tanh(h * (k0 + (k0 * k1) * h2))
            half = 0.5 + 0.5 * t
            b_act[slot, :, cols] = (h * half).astype(BF16)
            slope = half + (h * (1.0 - t * t)) * (0.5 * k0 + (1.5 * k0 * k1) * h2)
            b_dg[slot, :, cols] = slope.astype(BF16)
        todo[6].start()
        todo[7].start()
        at_first(chunk, weights[3])
        branch = dot(b_act[slot], w_down[...])

        @pl.when(chunk >= 2)
        def _():
            await_arrival(outbox.at[slot], sends.at[chunk - 2])

        outbox[slot] = (b_mid[slot] + branch - row_mean(branch)).astype(BF16)
        pass_on(section, chunk, per, last, 1, outbox.at[slot], inbox, result, sends, arrivals, landed)
        return carry

    lax.fori_loop(0, chunks, forward_chunk, 0)
    for chunk in (chunks - 2, chunks - 1):
        for copy in keep_forward(chunk, chunk % 2):
            copy.wait()

    @pl.when(section == 0)
    def _():
        clear()

    def fetches(chunk, slot):
        pairs = ((s_dg, b_dg), (s_mid, b_mid), (s_mixed, b_mixed), (s_q, b_q), (s_lse, b_lse))
        return [
            pltpu.make_async_copy(src.at[chunk], dst.at[slot], loads.at[kind, slot])
            for kind, (src, dst) in enumerate(pairs)
        ]

    def keep_backward(chunk, slot):
        pairs = ((b_nm, s_db), (b_act, s_dh), (b_na, s_da), (b_dt, s_dt))
        return [
            pltpu.make_async_copy(src.at[slot], dst.at[chunk], kept_b.at[kind, slot])
            for kind, (src, dst) in enumerate(pairs)
        ]

    def folded(v):
        return jnp.sum(v.reshape(C // 8, 8, D), axis=0)

    def backward_chunk(step, carry):
        chunk = chunks - 1 - step
        slot = lax.rem(chunk, 2)

        @pl.when((step >= 1) & (chunk >= 1))
        def _():
            for copy in fetches(chunk - 1, 1 - slot):
                copy.start()

        @pl.when(step >= 2)
        def _():
            for copy in keep_backward(chunk + 2, slot):
                copy.wait()

        @pl.when(step >= 2)
        def _():
            for copy in fetches(chunk, slot):
                copy.wait()

        todo = keep_backward(chunk, slot)
        fill_bias(docs, chunk, bias_b, True)
        await_arrival(grads.at[chunk], grad_arrivals.at[chunk])
        g = grads[chunk].astype(F32)
        db = (g - row_mean(g)).astype(BF16)
        b_nm[slot] = db
        todo[0].start()
        for part in range(FF // D):
            cols = slice(part * D, (part + 1) * D)
            d_active = dot_nt(db, w_down[cols, :])
            b_act[slot, :, cols] = (d_active * b_dg[slot, :, cols].astype(F32)).astype(BF16)
        todo[1].start()
        dn = dot_nt(b_act[slot], w_up[...])
        mid = b_mid[slot]
        factor = lax.rsqrt(row_mean(mid * mid) + EPS)
        unit = mid * factor
        gains[1] += folded(dn * unit)
        dn = dn * gain_m[...]
        d_mid = g + factor * (dn - unit * row_mean(dn * unit))
        da = (d_mid - row_mean(d_mid)).astype(BF16)
        b_na[slot] = da
        todo[2].start()
        b_mid[slot] = d_mid
        dmix = dot_nt(da, w_out[...]).astype(BF16)
        b_dmix[...] = dmix
        prod = dmix.astype(F32) * b_mixed[slot].astype(F32)
        top = prod.astype(BF16)
        rest = (prod - top.astype(F32)).astype(BF16)
        inner = dot(top, marks[...]) + dot(rest, marks[...])
        lse_d[...] = jnp.transpose(inner)[:16]
        def attend(blocks):
            window = pl.ds(pl.multiple_of((chunk - blocks + 1) * C, C), blocks * C)
            masked = slice((WIN - blocks) * C, WIN * C)
            for pair in range(PAIRS):
                lanes = slice(pair * 2 * HD, (pair + 1) * 2 * HD)
                q2 = two_heads(b_q[slot, :, lanes], low, high)
                do2 = two_heads(b_dmix[:, lanes], low, high)
                keys = kbuf[window, lanes]
                values = vbuf[window, lanes]
                both = jnp.concatenate([bias_b[masked, :], bias_b[masked, :]], axis=1)
                even, odd = slice(2 * pair, 2 * pair + 1), slice(2 * pair + 1, 2 * pair + 2)
                lse = jnp.concatenate([b_lse[slot, even, :], b_lse[slot, odd, :]], axis=1)
                inner = jnp.concatenate([lse_d[even, :], lse_d[odd, :]], axis=1)
                probs = jnp.exp(dot_nt(keys, q2) + both - lse)
                ds = (probs * (dot_nt(values, do2) - inner)).astype(BF16)
                dv = dot(probs.astype(BF16), do2)
                dk = dot(ds, q2)
                for part in range(blocks):
                    place = lax.rem(chunk - blocks + 1 + part, WIN)
                    rows = slice(part * C, (part + 1) * C)
                    dv_acc[place, :, lanes] += dv[rows]
                    dk_acc[place, :, lanes] += dk[rows]
                dq = dot(jnp.transpose(keys), ds)
                dq = jnp.concatenate([dq[:HD, :C], dq[HD:, C:]], axis=0)
                b_dt[slot, :, lanes] = (jnp.transpose(dq) * (HD**-0.5)).astype(BF16)

        by_blocks(docs, chunk, attend)
        done = lax.rem(chunk, WIN)
        b_dt[slot, :, D : 2 * D] = dk_acc[done].astype(BF16)
        b_dt[slot, :, 2 * D :] = dv_acc[done].astype(BF16)
        dk_acc[done] = jnp.zeros((C, D), F32)
        dv_acc[done] = jnp.zeros((C, D), F32)
        todo[3].start()
        dn = dot_nt(b_dt[slot], w_qkv[...])
        x = inbox[chunk].astype(F32)
        x = x - centered * row_mean(x)
        factor = lax.rsqrt(row_mean(x * x) + EPS)
        unit = x * factor
        gains[0] += folded(dn * unit)
        dn = dn * gain_a[...]
        grad = b_mid[slot] + factor * (dn - unit * row_mean(dn * unit))
        grad = grad - centered * row_mean(grad)
        inbox[chunk] = grad.astype(BF16)
        pass_on(
            section, chunk, per, 0, -1, inbox.at[chunk], grads, grad_result, grad_sends, grad_arrivals, grad_landed
        )
        return carry

    lax.fori_loop(0, chunks, backward_chunk, 0)
    for chunk in (0, 1):
        for copy in keep_backward(chunk, chunk):
            copy.wait()
    drain_rows(section, sections, per, tokens, first_sends, 0)
    drain_rows(section, sections, per, cotangent, grad_first_sends, last)
    settle(section, chunks - 2, chunks, per, last, outbox.at[0], result, sends, landed)
    settle(section, 0, chunks, per, 0, inbox.at[0], grad_result, grad_sends, grad_landed)


ANY = pl.BlockSpec(memory_space=pl.ANY)
IN_VMEM = pl.BlockSpec(memory_space=pltpu.VMEM)
DMA = pltpu.SemaphoreType.DMA


def layers(sections, chunks, tokens, cotangent, docs, weights):
    per = chunks // sections
    sds = jax.ShapeDtypeStruct
    staged = (
        ("q", (C, D), BF16),
        ("na", (C, D), BF16),
        ("mixed", (C, D), BF16),
        ("lse", (16, C), F32),
        ("mid", (C, D), F32),
        ("nm", (C, D), BF16),
        ("act", (C, FF), BF16),
        ("dg", (C, FF), BF16),
    )
    saved = staged + (
        ("db", (C, D), BF16),
        ("dh", (C, FF), BF16),
        ("da", (C, D), BF16),
        ("dt", (C, 3 * D), BF16),
    )
    outs = pl.pallas_call(
        functools.partial(layer_kernel, sections),
        out_shape=[sds((per, C, D), BF16)] * 2
        + [sds((2, 8, D), F32)]
        + [sds((chunks,) + s, t) for _, s, t in saved],
        in_specs=[ANY] * 2 + [IN_VMEM] * 3 + [ANY] * 4,
        out_specs=[ANY] * 2 + [IN_VMEM] + [ANY] * len(saved),
        scratch_shapes=[pltpu.VMEM(shape, BF16) for shape in ((D, 3 * D), (D, D), (D, FF), (FF, D))]
        + [
            pltpu.VMEM((chunks, C, D), BF16),
            pltpu.VMEM((2, C, D), BF16),
            pltpu.VMEM((chunks, C, D), BF16),
            pltpu.VMEM((chunks * C, D), BF16),
            pltpu.VMEM((chunks * C, D), BF16),
            pltpu.VMEM((C, WIN * C), F32),
            pltpu.VMEM((WIN * C, C), F32),
            pltpu.VMEM((WIN, C, D), F32),
            pltpu.VMEM((WIN, C, D), F32),
            pltpu.VMEM((16, C), F32),
            pltpu.VMEM((C, D), BF16),
            pltpu.VMEM((D, 128), BF16),
        ]
        + [pltpu.VMEM((2,) + s, t) for _, s, t in staged]
        + [pltpu.VMEM((2, C, 3 * D), BF16)]
        + [DMA((chunks,)), DMA((chunks,)), DMA((per,)), DMA((per,))] * 2
        + [DMA((8, 2)), DMA((4, 2)), DMA((5, 2)), DMA((4,))],
        compiler_params=pltpu.CompilerParams(
            collective_id=0, has_side_effects=True, vmem_limit_bytes=VMEM_LIMIT
        ),
        name="layers",
    )(tokens.reshape(per, C, D), cotangent.reshape(per, C, D), docs, *weights)
    return outs[0], outs[1], outs[2], {name: out for (name, _, _), out in zip(saved, outs[3:])}


def matmul_lt(left_side, right_side):
    rows = left_side.shape[0] * left_side.shape[1]
    return lax.dot_general(
        left_side.reshape(rows, -1),
        right_side.reshape(rows, -1),
        (((0,), (0,)), ((), ())),
        preferred_element_type=F32,
    )


UNIT = 256
UNITS = 9 + 3 + 12 + 12
NARROW = 9 + 3 + 12
LENT = 6
LENT_SHORT = 3
LAGS = (4, 8, 12)


def pair_first(unit):
    return lax.rem(unit, 4) != 3


def dot_tn(a, b):
    return lax.dot_general(a, b, (((0,), (0,)), ((), ())), preferred_element_type=F32)


def weight_grad_kernel(
    s_na,
    s_dt,
    s_mixed,
    s_da,
    s_nm,
    s_dh,
    s_act,
    s_db,
    gains,
    o_qkv,
    o_out,
    o_up,
    o_down,
    o_gains,
    left,
    right,
    act,
    made,
    got_a,
    got_b,
    got_c,
    total,
    gain_own,
    gain_in,
    left_sems,
    right_sems,
    act_sem,
    a_sends,
    a_arrivals,
    b_sends,
    b_arrivals,
    c_sends,
    c_arrivals,
    out_sem,
    gain_sends,
    gain_arrivals,
    lent_sends,
    lent_arrivals,
    back_sends,
    back_arrivals,
    here,
):
    section = lax.axis_index("section")
    dp = lax.axis_index("dp")
    x, near, far = lax.rem(dp, 2), lax.rem(dp // 2, 2), dp // 4
    lender = section < 2
    across = 3 - section
    loan = jnp.where((section == 0) | (section == 3), LENT, LENT_SHORT)

    def lent(unit):
        return (unit < 2 * loan) & (lax.rem(unit, 2) == 1)

    over_x, over_near, over_far = dp + 1 - 2 * x, dp + 2 - 4 * near, dp + 4 - 8 * far

    def load_left(src, slot):
        return pltpu.make_async_copy(src, left.at[slot], left_sems.at[slot])

    def load_right(src, column, slot):
        columns = pl.ds(pl.multiple_of(column * UNIT, UNIT), UNIT)
        return pltpu.make_async_copy(src.at[:, columns], right.at[slot], right_sems.at[slot])

    def start_right(unit):
        slot = lax.rem(unit, 2)

        @pl.when(unit < 9)
        def _():
            load_right(s_dt, unit, slot).start()

        @pl.when((unit >= 9) & (unit < 12))
        def _():
            load_right(s_da, unit - 9, slot).start()

        @pl.when((unit >= 12) & (unit < NARROW))
        def _():
            load_right(s_dh, unit - 12, slot).start()

    load_left(s_na, 0).start()
    start_right(0)
    load_left(s_mixed, 1).start()
    pltpu.make_async_copy(s_act, act, act_sem).start()
    gain_own[...] = jnp.sum(gains[...], axis=1, keepdims=True) + jnp.zeros((2, 8, D), F32)

    barrier = pltpu.get_barrier_semaphore()
    for step in range(1, 8):
        other = lax.rem(dp + step, 8)
        pl.semaphore_signal(barrier, inc=1, device_id=(other, section), device_id_type=MESH)

    @pl.when(lender)
    def _():
        pl.semaphore_wait(barrier, 8)
        pl.semaphore_signal(here, inc=1, device_id=(dp, across), device_id_type=MESH)

    @pl.when(jnp.logical_not(lender))
    def _():
        pl.semaphore_signal(barrier, inc=1, device_id=(dp, across), device_id_type=MESH)
        pl.semaphore_wait(barrier, 7)

    def gain_copy(step):
        other = lax.rem(dp + step, 8)
        return pltpu.make_async_remote_copy(
            gain_own,
            gain_in.at[step - 1],
            gain_sends.at[step - 1],
            gain_arrivals.at[step - 1],
            device_id=(other, section),
            device_id_type=MESH,
        )

    for step in range(1, 8):
        gain_copy(step).start()

    def send(unit, src, dst, sends, arrivals, to):
        pltpu.make_async_remote_copy(
            src,
            dst.at[unit],
            sends.at[unit],
            arrivals.at[unit],
            device_id=(to, section),
            device_id_type=MESH,
        ).start()

    def first_add(unit):
        @pl.when(pair_first(unit))
        def _():
            send(unit, made.at[unit, 1 - x], got_a, a_sends, a_arrivals, over_x)

        @pl.when(jnp.logical_not(pair_first(unit)))
        def _():
            send(unit, made.at[unit, :, 1 - near], got_a, a_sends, a_arrivals, over_near)

    def second_add(unit):
        await_arrival(got_a.at[unit], a_arrivals.at[unit])

        @pl.when(pair_first(unit))
        def _():
            made[unit, x] = (made[unit, x].astype(F32) + got_a[unit].astype(F32)).astype(BF16)
            send(unit, made.at[unit, x, 1 - near], got_b, b_sends, b_arrivals, over_near)

        @pl.when(jnp.logical_not(pair_first(unit)))
        def _():
            made[unit, :, near] = (made[unit, :, near].astype(F32) + got_a[unit].astype(F32)).astype(BF16)
            send(unit, made.at[unit, 1 - x, near], got_b, b_sends, b_arrivals, over_x)

    def third_add(unit):
        await_arrival(got_b.at[unit], b_arrivals.at[unit])
        made[unit, x, near] = (made[unit, x, near].astype(F32) + got_b[unit].astype(F32)).astype(BF16)
        send(unit, made.at[unit, x, near, 1 - far], got_c, c_sends, c_arrivals, over_far)

    def finish(unit):
        await_arrival(got_c.at[unit], c_arrivals.at[unit])
        total[unit] = made[unit, x, near, far].astype(F32) + got_c[unit].astype(F32)

        @pl.when(unit < UNITS)
        def _():
            deliver(unit)

        @pl.when(unit >= UNITS)
        def _():
            give_back(unit - UNITS)

    def lend(place):
        pltpu.make_async_remote_copy(
            made.at[2 * place + 1],
            made.at[UNITS + place],
            lent_sends.at[place],
            lent_arrivals.at[place],
            device_id=(dp, across),
            device_id_type=MESH,
        ).start()

    def give_back(place):
        pltpu.make_async_remote_copy(
            total.at[UNITS + place],
            total.at[2 * place + 1],
            back_sends.at[place],
            back_arrivals.at[place],
            device_id=(dp, across),
            device_id_type=MESH,
        ).start()

    def added_here(unit):
        kept = lender & (unit < UNITS) & jnp.logical_not(lent(unit))
        return kept | (jnp.logical_not(lender) & (unit < UNITS + loan))

    def deliver(unit):
        for first, end, ref in ((0, 9, o_qkv), (9, 12, o_out), (12, NARROW, o_up)):

            @pl.when((unit >= first) & (unit < end))
            def _():
                columns = pl.ds(pl.multiple_of((unit - first) * UNIT, UNIT), UNIT)
                pltpu.make_async_copy(total.at[unit], ref.at[:, columns], out_sem).start()

        @pl.when(unit >= NARROW)
        def _():
            column, row = (unit - NARROW) // 4, lax.rem(unit - NARROW, 4)
            columns = pl.ds(pl.multiple_of(column * UNIT, UNIT), UNIT)
            rows = pl.ds(pl.multiple_of(row * 96, 96), 96)
            pltpu.make_async_copy(total.at[unit], o_down.at[rows, columns], out_sem).start()

    def advance(now):
        for lag, action in zip(LAGS[::-1], (finish, third_add, second_add)):

            @pl.when((now >= lag) & added_here(now - lag))
            def _():
                action(now - lag)

    def narrow(unit, carry):
        slot = lax.rem(unit, 2)
        side = jnp.where((unit >= 9) & (unit < 12), 1, 0)

        @pl.when(unit == 9)
        def _():
            load_left(s_nm, 0).start()

        @pl.when(unit == 12)
        def _():
            load_left(s_db, 1).start()

        start_right(unit + 1)

        @pl.when((unit == 0) | (unit == 12))
        def _():
            load_left(s_na, 0).wait()

        @pl.when(unit == 9)
        def _():
            load_left(s_mixed, 1).wait()

        load_right(s_dt, 0, slot).wait()
        grad = dot_tn(left[side], right[slot]).astype(BF16)
        for shard in range(8):
            made[unit, shard % 2, shard // 2 % 2, shard // 4] = grad[shard * 96 : (shard + 1) * 96]

        @pl.when(lender & lent(unit))
        def _():
            lend(lax.rem(unit, 2 * LENT) // 2)

        @pl.when(added_here(unit))
        def _():
            first_add(unit)

        advance(unit)
        return carry

    lax.fori_loop(0, NARROW, narrow, 0)
    load_left(s_db, 1).wait()
    pltpu.make_async_copy(s_act, act, act_sem).wait()

    def wide(step, carry):
        column, shard = step // 8, lax.rem(step, 8)
        columns = pl.ds(pl.multiple_of(column * UNIT, UNIT), UNIT)
        rows = pl.ds(pl.multiple_of(shard * 384, 384), 384)
        grad = dot_tn(act[:, rows], left[1, :, columns]).astype(BF16)
        first = NARROW + 4 * column
        for part in range(4):
            made[first + part, lax.rem(shard, 2), lax.rem(shard // 2, 2), shard // 4] = grad[part * 96 : (part + 1) * 96]

        @pl.when(shard == 7)
        def _():
            for part in range(4):
                first_add(first + part)

        @pl.when(lax.rem(step, 2) == 1)
        def _():
            advance(NARROW + step // 2)

        return carry

    lax.fori_loop(0, 24, wide, 0)

    def drain(now, carry):
        advance(now)
        return carry

    @pl.when(jnp.logical_not(lender))
    def _():
        pl.semaphore_wait(here, 1)

        def borrowed(unit, carry):
            await_arrival(made.at[unit], lent_arrivals.at[unit - UNITS])
            first_add(unit)
            advance(unit)
            return carry

        lax.fori_loop(UNITS, UNITS + loan, borrowed, 0)
        lax.fori_loop(UNITS + loan, UNITS + loan + LAGS[-1], drain, 0)

    @pl.when(lender)
    def _():
        lax.fori_loop(UNITS, UNITS + LAGS[-1], drain, 0)

    for step in range(1, 8):
        gain_copy(step).wait()
    sums = gain_own[:, 0:1]
    for step in range(7):
        sums = sums + gain_in[step, :, 0:1]
    o_gains[...] = sums

    def sent(unit, carry):
        @pl.when(added_here(unit))
        def _():
            await_arrival(got_a.at[unit], a_sends.at[unit])
            await_arrival(got_b.at[unit], b_sends.at[unit])
            await_arrival(got_c.at[unit], c_sends.at[unit])

        return carry

    lax.fori_loop(0, UNITS + LENT, sent, 0)

    @pl.when(lender)
    def _():
        def returned(place, carry):
            await_arrival(made.at[UNITS + place], lent_sends.at[place])
            await_arrival(total.at[2 * place + 1], back_arrivals.at[place])
            deliver(2 * place + 1)
            return carry

        lax.fori_loop(0, loan, returned, 0)

    @pl.when(jnp.logical_not(lender))
    def _():
        def returned(place, carry):
            await_arrival(total.at[UNITS + place], back_sends.at[place])
            return carry

        lax.fori_loop(0, loan, returned, 0)

    await_arrival(total.at[pl.ds(0, UNITS)], out_sem)


def weight_grads(na, dt, mixed, da, nm, dh, act, db, gains):
    tokens = na.shape[0] * na.shape[1]
    sds = jax.ShapeDtypeStruct
    operands = [v.reshape(tokens, -1) for v in (na, dt, mixed, da, nm, dh, act, db)]
    return pl.pallas_call(
        weight_grad_kernel,
        out_shape=[
            sds((96, 3 * D), F32),
            sds((96, D), F32),
            sds((96, FF), F32),
            sds((384, D), F32),
            sds((2, 1, D), F32),
        ],
        in_specs=[ANY] * 8 + [IN_VMEM],
        out_specs=[ANY] * 4 + [IN_VMEM],
        scratch_shapes=[
            pltpu.VMEM((2, tokens, D), BF16),
            pltpu.VMEM((2, tokens, UNIT), BF16),
            pltpu.VMEM((tokens, FF), BF16),
            pltpu.VMEM((UNITS + LENT, 2, 2, 2, 96, UNIT), BF16),
            pltpu.VMEM((UNITS + LENT, 2, 2, 96, UNIT), BF16),
            pltpu.VMEM((UNITS + LENT, 2, 96, UNIT), BF16),
            pltpu.VMEM((UNITS + LENT, 96, UNIT), BF16),
            pltpu.VMEM((UNITS + LENT, 96, UNIT), F32),
            pltpu.VMEM((2, 8, D), F32),
            pltpu.VMEM((7, 2, 8, D), F32),
            DMA((2,)),
            DMA((2,)),
            DMA,
            DMA((UNITS + LENT,)),
            DMA((UNITS + LENT,)),
            DMA((UNITS + LENT,)),
            DMA((UNITS + LENT,)),
            DMA((UNITS + LENT,)),
            DMA((UNITS + LENT,)),
            DMA,
            DMA((7,)),
            DMA((7,)),
            DMA((LENT,)),
            DMA((LENT,)),
            DMA((LENT,)),
            DMA((LENT,)),
            pltpu.SemaphoreType.REGULAR,
        ],
        compiler_params=pltpu.CompilerParams(
            collective_id=2, has_side_effects=True, vmem_limit_bytes=VMEM_LIMIT
        ),
        name="weight_grads",
    )(*operands, gains)


def hand_over_kernel(gains, *refs):
    sources, results, (gain_attn, gain_mlp), held = refs[:6], refs[6:12], refs[12:14], refs[14:20]
    come, go = refs[20], refs[21]
    arriving = [
        pltpu.make_async_copy(src, buf, come.at[at]) for at, (src, buf) in enumerate(zip(sources, held))
    ]
    leaving = [
        pltpu.make_async_copy(buf, dst, go.at[at]) for at, (buf, dst) in enumerate(zip(held, results))
    ]
    for copy in arriving:
        copy.start()
    shift = lax.rem(D - 96 * lax.axis_index("dp"), D)
    for kind, ref in enumerate((gain_attn, gain_mlp)):
        turned = pltpu.roll(jnp.broadcast_to(gains[kind], (8, D)), shift, 1)
        ref[...] = turned[:1, :96]
    for copy, onward in zip(arriving, leaving):
        copy.wait()
        onward.start()
    for copy in leaving:
        copy.wait()


def hand_over(output, input_grad, shards, gains):
    sds = jax.ShapeDtypeStruct
    sources = (output, input_grad, *shards)
    outs = pl.pallas_call(
        hand_over_kernel,
        out_shape=[sds(v.shape, v.dtype) for v in sources] + [sds((1, 96), F32)] * 2,
        in_specs=[IN_VMEM] + [ANY] * 6,
        out_specs=[ANY] * 6 + [IN_VMEM] * 2,
        scratch_shapes=[pltpu.VMEM(v.shape, v.dtype) for v in sources] + [DMA((6,)), DMA((6,))],
        compiler_params=pltpu.CompilerParams(vmem_limit_bytes=VMEM_LIMIT),
        name="hand_over",
    )(gains, *sources)
    output, input_grad, qkv, out, up, down, gain_attn, gain_mlp = outs
    return output, input_grad, gain_attn, qkv[None], out[None], gain_mlp, up[None], down[None]


def body(tokens, cotangent, doc_ids, gain_attn, w_qkv, w_out, gain_mlp, w_up, w_down):
    sections = lax.axis_size("section")
    rows, seq = doc_ids.shape
    chunks = rows * seq // C
    weights = (gain_attn, gain_mlp, w_qkv[0], w_out[0], w_up[0], w_down[0])
    output, input_grad, gains, kept = layers(sections, chunks, tokens, cotangent, doc_ids, weights)
    db, dh, da, dt = kept["db"], kept["dh"], kept["da"], kept["dt"]
    if lax.axis_size("dp") == 8 and sections == 4 and chunks == 8:
        qkv, out, up, down, gains = weight_grads(
            kept["na"], dt, kept["mixed"], da, kept["nm"], dh, kept["act"], db, gains
        )
        return hand_over(
            output.reshape(tokens.shape), input_grad.reshape(cotangent.shape), (qkv, out, up, down), gains
        )
    gains = jnp.sum(gains, axis=1)
    grads = (
        gains[0],
        matmul_lt(kept["na"], dt),
        matmul_lt(kept["mixed"], da),
        gains[1],
        matmul_lt(kept["nm"], dh),
        matmul_lt(kept["act"], db),
    )
    shards = lax.psum_scatter(grads, "dp", scatter_dimension=0, tiled=True)
    return (
        output.reshape(tokens.shape),
        input_grad.reshape(cotangent.shape),
        *(shard[None] for shard in shards),
    )


def solution(mesh):
    rows = P(("dp", "section"), None)
    layer = P("section", None)
    matrix = P("section", None, None)
    in_specs = (rows, rows, P("dp", None), layer, matrix, matrix, layer, matrix, matrix)
    split = P("section", "dp")
    split_matrix = P("section", "dp", None)
    out_specs = (rows, rows, split, split_matrix, split_matrix, split, split_matrix, split_matrix)
    return jax.shard_map(body, mesh=mesh, in_specs=in_specs, out_specs=out_specs, check_vma=False)
```

```python
import functools

import jax
import jax.numpy as jnp
from jax import lax
from jax.experimental import pallas as pl
from jax.experimental.pallas import tpu as pltpu
from jax.sharding import PartitionSpec as P

D = 768
HEADS = 12
HD = 64
FF = 3072
C = 256
WIN = 3
PAIRS = HEADS // 2
EPS = 1e-05
NEG = -1e30
MESH = pl.DeviceIdType.MESH
BF16 = jnp.bfloat16
F32 = jnp.float32
VMEM_LIMIT = 60 * 1024 * 1024


def dot(a, b):
    return jnp.dot(a, b, preferred_element_type=F32)


def dot_nt(a, b):
    return lax.dot_general(a, b, (((1,), (1,)), ((), ())), preferred_element_type=F32)


def row_mean(v):
    return jnp.mean(v, axis=-1, keepdims=True)


def greet(section, sections):
    dp = lax.axis_index("dp")
    barrier = pltpu.get_barrier_semaphore()
    for step in range(1, sections):
        other = lax.rem(section + step, sections)
        pl.semaphore_signal(barrier, inc=1, device_id=(dp, other), device_id_type=MESH)
    pl.semaphore_wait(barrier, sections - 1)


def lane_masks():
    lane = lax.broadcasted_iota(jnp.int32, (1, 2 * HD), 1)
    low = (lane < HD).astype(F32)
    return low.astype(BF16), (1.0 - low).astype(BF16), lane < HD


def two_heads(pair, low, high):
    return jnp.concatenate([pair * low, pair * high], axis=0)


def await_arrival(buf, sem):
    pltpu.make_async_copy(buf, buf, sem).wait()


def scatter_rows(section, sections, per, rows, inbox, sems, send_sems, target):
    dp = lax.axis_index("dp")
    for piece in range(per):
        slot = section * per + piece

        @pl.when(section != target)
        def _():
            pltpu.make_async_remote_copy(
                rows.at[piece],
                inbox.at[slot],
                send_sems.at[piece],
                sems.at[slot],
                device_id=(dp, target),
                device_id_type=MESH,
            ).start()

        @pl.when(section == target)
        def _():
            pltpu.make_async_copy(rows.at[piece], inbox.at[slot], sems.at[slot]).start()


def drain_rows(section, sections, per, rows, send_sems, target):
    for piece in range(per):

        @pl.when(section != target)
        def _():
            pltpu.make_async_copy(rows.at[piece], rows.at[piece], send_sems.at[piece]).wait()


def pass_on(section, chunk, per, last, step, source, inbox, result, sends, arrivals, landed):
    dp = lax.axis_index("dp")
    owner = chunk // per

    @pl.when(section != last)
    def _():
        pltpu.make_async_remote_copy(
            source,
            inbox.at[chunk],
            sends.at[chunk],
            arrivals.at[chunk],
            device_id=(dp, section + step),
            device_id_type=MESH,
        ).start()

    @pl.when((section == last) & (owner != last))
    def _():
        pltpu.make_async_remote_copy(
            source,
            result.at[lax.rem(chunk, per)],
            sends.at[chunk],
            landed.at[lax.rem(chunk, per)],
            device_id=(dp, owner),
            device_id_type=MESH,
        ).start()

    @pl.when((section == last) & (owner == last))
    def _():
        pltpu.make_async_copy(source, result.at[lax.rem(chunk, per)], sends.at[chunk]).start()


def settle(section, first, end, per, last, source, result, sends, landed):
    def one(chunk, carry):
        await_arrival(source, sends.at[chunk])
        return carry

    lax.fori_loop(first, end, one, 0)
    for piece in range(per):

        @pl.when(section != last)
        def _():
            await_arrival(result.at[piece], landed.at[piece])


def fill_bias(docs, chunk, bias):
    per_row = docs.shape[1] // C
    row, place = chunk // per_row, lax.rem(chunk, per_row)

    def numbers(block):
        start = pl.multiple_of(jnp.maximum(block, 0) * C, C)
        return docs[pl.ds(row, 1), pl.ds(start, C)].astype(F32)

    queries = numbers(place)
    for part in range(WIN):
        keys = jnp.transpose(jnp.broadcast_to(numbers(place - (WIN - 1) + part), (128, C)))
        for half in range(C // 128):
            lanes = slice(half * 128, (half + 1) * 128)
            allowed = keys == queries[:, lanes]
            if part == WIN - 1:
                down = lax.broadcasted_iota(jnp.int32, (C, 128), 0)
                across = lax.broadcasted_iota(jnp.int32, (C, 128), 1) + half * 128
                allowed = allowed & (down <= across)
            bias[part * C : (part + 1) * C, lanes] = jnp.where(allowed, 0.0, NEG)


def by_blocks(docs, chunk, attend):
    place = lax.rem(chunk, docs.shape[1] // C)
    for blocks in range(1, WIN + 1):

        @pl.when((place == blocks - 1) if blocks < WIN else (place >= WIN - 1))
        def _():
            attend(blocks)


def layer_kernel(
    sections,
    tokens,
    cotangent,
    docs,
    gain_a,
    gain_m,
    h_qkv,
    h_out,
    h_up,
    h_down,
    result,
    grad_result,
    gains,
    s_q,
    s_na,
    s_mixed,
    s_probs,
    s_mid,
    s_nm,
    s_act,
    s_dg,
    s_db,
    s_dh,
    s_da,
    s_dt,
    w_qkv,
    w_out,
    w_up,
    w_down,
    inbox,
    outbox,
    grads,
    kbuf,
    vbuf,
    bias,
    dk_acc,
    dv_acc,
    inner,
    b_dmix,
    marks,
    b_q,
    b_na,
    b_mixed,
    b_probs,
    b_mid,
    b_nm,
    b_act,
    b_dg,
    b_dt,
    arrivals,
    sends,
    first_sends,
    landed,
    grad_arrivals,
    grad_sends,
    grad_first_sends,
    grad_landed,
    kept_f,
    kept_b,
    loads,
    weight_sems,
):
    section = lax.axis_index("section")
    chunks = inbox.shape[0]
    per = tokens.shape[0]
    last = sections - 1
    weights = [
        pltpu.make_async_copy(src, dst, weight_sems.at[kind])
        for kind, (src, dst) in enumerate(
            ((h_qkv, w_qkv), (h_out, w_out), (h_up, w_up), (h_down, w_down))
        )
    ]
    weights[0].start()

    def at_first(chunk, copy, *later):
        @pl.when(chunk == 0)
        def _():
            copy.wait()
            for other in later:
                other.start()

    def clear():
        dk_acc[...] = jnp.zeros_like(dk_acc)
        dv_acc[...] = jnp.zeros_like(dv_acc)
        gains[...] = jnp.zeros_like(gains)
        owner_of = lax.broadcasted_iota(jnp.int32, (D, 128), 0) // HD
        own = owner_of == lax.broadcasted_iota(jnp.int32, (D, 128), 1)
        marks[...] = own.astype(F32).astype(BF16)

    greet(section, sections)
    scatter_rows(section, sections, per, tokens, inbox, arrivals, first_sends, 0)
    scatter_rows(section, sections, per, cotangent, grads, grad_arrivals, grad_first_sends, last)
    low, high, is_low = lane_masks()
    centered = jnp.where(section == 0, 1.0, 0.0).astype(F32)

    @pl.when(section != 0)
    def _():
        clear()

    def keep_forward(chunk, slot):
        pairs = (
            (b_q, s_q),
            (b_na, s_na),
            (b_mixed, s_mixed),
            (b_probs, s_probs),
            (b_mid, s_mid),
            (b_nm, s_nm),
            (b_act, s_act),
            (b_dg, s_dg),
        )
        return [
            pltpu.make_async_copy(src.at[slot], dst.at[chunk], kept_f.at[kind, slot])
            for kind, (src, dst) in enumerate(pairs)
        ]

    def forward_chunk(chunk, carry):
        slot = lax.rem(chunk, 2)

        @pl.when(chunk >= 2)
        def _():
            for copy in keep_forward(chunk - 2, slot):
                copy.wait()

        todo = keep_forward(chunk, slot)
        at_first(chunk, *weights)
        fill_bias(docs, chunk, bias)
        await_arrival(inbox.at[chunk], arrivals.at[chunk])
        x = inbox[chunk].astype(F32)
        x = x - centered * row_mean(x)
        na = (x * lax.rsqrt(row_mean(x * x) + EPS) * gain_a[...]).astype(BF16)
        b_na[slot] = na
        todo[1].start()
        b_q[slot] = (dot(na, w_qkv[:, :D]).astype(BF16) * (HD**-0.5)).astype(BF16)
        here = pl.ds(pl.multiple_of(chunk * C, C), C)
        kbuf[here, :] = dot(na, w_qkv[:, D : 2 * D]).astype(BF16)
        vbuf[here, :] = dot(na, w_qkv[:, 2 * D :]).astype(BF16)
        todo[0].start()
        def attend(blocks):
            window = pl.ds(pl.multiple_of((chunk - blocks + 1) * C, C), blocks * C)
            masked = slice((WIN - blocks) * C, WIN * C)
            def lanes_of(pair):
                return slice(pair * 2 * HD, (pair + 1) * 2 * HD)

            def scores(pair):
                q2 = two_heads(b_q[slot, :, lanes_of(pair)], low, high)
                return dot_nt(kbuf[window, lanes_of(pair)], q2)

            both = jnp.concatenate([bias[masked, :], bias[masked, :]], axis=1)
            ahead = scores(0)
            for pair in range(PAIRS):
                s = ahead + both
                if pair + 1 < PAIRS:
                    ahead = scores(pair + 1)
                e = jnp.exp(s - jnp.max(s, axis=0, keepdims=True))
                probs = (e * (1.0 / jnp.sum(e, axis=0, keepdims=True))).astype(BF16)
                b_probs[slot, pair, masked, :] = probs
                o = lax.dot_general(
                    probs, vbuf[window, lanes_of(pair)], (((0,), (0,)), ((), ())), preferred_element_type=F32
                )
                b_mixed[slot, :, lanes_of(pair)] = jnp.where(is_low, o[:C], o[C:]).astype(BF16)

        by_blocks(docs, chunk, attend)
        todo[2].start()
        todo[3].start()
        at_first(chunk, weights[1])
        branch = dot(b_mixed[slot], w_out[...])
        mid = x + branch - row_mean(branch)
        b_mid[slot] = mid
        todo[4].start()
        nm = (mid * lax.rsqrt(row_mean(mid * mid) + EPS) * gain_m[...]).astype(BF16)
        b_nm[slot] = nm
        todo[5].start()
        at_first(chunk, weights[2])
        k0 = 0.7978845608028654
        k1 = 0.044715
        for part in range(FF // D):
            cols = slice(part * D, (part + 1) * D)
            h = dot(nm, w_up[:, cols])
            h2 = h * h
            t = jnp.tanh(h * (k0 + (k0 * k1) * h2))
            half = 0.5 + 0.5 * t
            b_act[slot, :, cols] = (h * half).astype(BF16)
            slope = half + (h * (1.0 - t * t)) * (0.5 * k0 + (1.5 * k0 * k1) * h2)
            b_dg[slot, :, cols] = slope.astype(BF16)
        todo[6].start()
        todo[7].start()
        at_first(chunk, weights[3])
        branch = dot(b_act[slot], w_down[...])

        @pl.when(chunk >= 2)
        def _():
            await_arrival(outbox.at[slot], sends.at[chunk - 2])

        outbox[slot] = (b_mid[slot] + branch - row_mean(branch)).astype(BF16)
        pass_on(section, chunk, per, last, 1, outbox.at[slot], inbox, result, sends, arrivals, landed)
        return carry

    lax.fori_loop(0, chunks, forward_chunk, 0)
    for chunk in (chunks - 2, chunks - 1):
        for copy in keep_forward(chunk, chunk % 2):
            copy.wait()

    @pl.when(section == 0)
    def _():
        clear()

    def fetches(chunk, slot):
        pairs = ((s_dg, b_dg), (s_mid, b_mid), (s_mixed, b_mixed), (s_q, b_q), (s_probs, b_probs))
        return [
            pltpu.make_async_copy(src.at[chunk], dst.at[slot], loads.at[kind, slot])
            for kind, (src, dst) in enumerate(pairs)
        ]

    def keep_backward(chunk, slot):
        pairs = ((b_nm, s_db), (b_act, s_dh), (b_na, s_da), (b_dt, s_dt))
        return [
            pltpu.make_async_copy(src.at[slot], dst.at[chunk], kept_b.at[kind, slot])
            for kind, (src, dst) in enumerate(pairs)
        ]

    def folded(v):
        return jnp.sum(v.reshape(C // 8, 8, D), axis=0)

    def backward_chunk(step, carry):
        chunk = chunks - 1 - step
        slot = lax.rem(chunk, 2)

        @pl.when((step >= 1) & (chunk >= 1))
        def _():
            for copy in fetches(chunk - 1, 1 - slot):
                copy.start()

        @pl.when(step >= 2)
        def _():
            for copy in keep_backward(chunk + 2, slot):
                copy.wait()

        @pl.when(step >= 2)
        def _():
            for copy in fetches(chunk, slot):
                copy.wait()

        todo = keep_backward(chunk, slot)
        await_arrival(grads.at[chunk], grad_arrivals.at[chunk])
        g = grads[chunk].astype(F32)
        db = (g - row_mean(g)).astype(BF16)
        b_nm[slot] = db
        todo[0].start()
        for part in range(FF // D):
            cols = slice(part * D, (part + 1) * D)
            d_active = dot_nt(db, w_down[cols, :])
            b_act[slot, :, cols] = (d_active * b_dg[slot, :, cols].astype(F32)).astype(BF16)
        todo[1].start()
        dn = dot_nt(b_act[slot], w_up[...])
        mid = b_mid[slot]
        factor = lax.rsqrt(row_mean(mid * mid) + EPS)
        unit = mid * factor
        gains[1] += folded(dn * unit)
        dn = dn * gain_m[...]
        d_mid = g + factor * (dn - unit * row_mean(dn * unit))
        da = (d_mid - row_mean(d_mid)).astype(BF16)
        b_na[slot] = da
        todo[2].start()
        b_mid[slot] = d_mid
        dmix = dot_nt(da, w_out[...]).astype(BF16)
        b_dmix[...] = dmix
        prod = dmix.astype(F32) * b_mixed[slot].astype(F32)
        inner[...] = jnp.transpose(dot(prod.astype(BF16), marks[...]))[:16]
        def attend(blocks):
            window = pl.ds(pl.multiple_of((chunk - blocks + 1) * C, C), blocks * C)
            masked = slice((WIN - blocks) * C, WIN * C)
            for pair in range(PAIRS):
                lanes = slice(pair * 2 * HD, (pair + 1) * 2 * HD)
                q2 = two_heads(b_q[slot, :, lanes], low, high)
                do2 = two_heads(b_dmix[:, lanes], low, high)
                keys = kbuf[window, lanes]
                even, odd = slice(2 * pair, 2 * pair + 1), slice(2 * pair + 1, 2 * pair + 2)
                mean = jnp.concatenate([inner[even, :], inner[odd, :]], axis=1)
                probs = b_probs[slot, pair, masked, :]
                ds = (probs.astype(F32) * (dot_nt(vbuf[window, lanes], do2) - mean)).astype(BF16)
                dv = dot(probs, do2)
                dk = dot(ds, q2)
                for part in range(blocks):
                    place = lax.rem(chunk - blocks + 1 + part, WIN)
                    rows = slice(part * C, (part + 1) * C)
                    dv_acc[place, :, lanes] += dv[rows]
                    dk_acc[place, :, lanes] += dk[rows]
                dq = dot(jnp.transpose(keys), ds)
                dq = jnp.concatenate([dq[:HD, :C], dq[HD:, C:]], axis=0)
                b_dt[slot, :, lanes] = (jnp.transpose(dq) * (HD**-0.5)).astype(BF16)

        by_blocks(docs, chunk, attend)
        done = lax.rem(chunk, WIN)
        b_dt[slot, :, D : 2 * D] = dk_acc[done].astype(BF16)
        b_dt[slot, :, 2 * D :] = dv_acc[done].astype(BF16)
        dk_acc[done] = jnp.zeros((C, D), F32)
        dv_acc[done] = jnp.zeros((C, D), F32)
        todo[3].start()
        dn = dot_nt(b_dt[slot], w_qkv[...])
        x = inbox[chunk].astype(F32)
        x = x - centered * row_mean(x)
        factor = lax.rsqrt(row_mean(x * x) + EPS)
        unit = x * factor
        gains[0] += folded(dn * unit)
        dn = dn * gain_a[...]
        grad = b_mid[slot] + factor * (dn - unit * row_mean(dn * unit))
        grad = grad - centered * row_mean(grad)
        inbox[chunk] = grad.astype(BF16)
        pass_on(
            section, chunk, per, 0, -1, inbox.at[chunk], grads, grad_result, grad_sends, grad_arrivals, grad_landed
        )
        return carry

    lax.fori_loop(0, chunks, backward_chunk, 0)
    for chunk in (0, 1):
        for copy in keep_backward(chunk, chunk):
            copy.wait()
    drain_rows(section, sections, per, tokens, first_sends, 0)
    drain_rows(section, sections, per, cotangent, grad_first_sends, last)
    settle(section, chunks - 2, chunks, per, last, outbox.at[0], result, sends, landed)
    settle(section, 0, chunks, per, 0, inbox.at[0], grad_result, grad_sends, grad_landed)


ANY = pl.BlockSpec(memory_space=pl.ANY)
IN_VMEM = pl.BlockSpec(memory_space=pltpu.VMEM)
DMA = pltpu.SemaphoreType.DMA


def layers(sections, chunks, tokens, cotangent, docs, weights):
    per = chunks // sections
    sds = jax.ShapeDtypeStruct
    staged = (
        ("q", (C, D), BF16),
        ("na", (C, D), BF16),
        ("mixed", (C, D), BF16),
        ("probs", (PAIRS, WIN * C, 2 * C), BF16),
        ("mid", (C, D), F32),
        ("nm", (C, D), BF16),
        ("act", (C, FF), BF16),
        ("dg", (C, FF), BF16),
    )
    saved = staged + (
        ("db", (C, D), BF16),
        ("dh", (C, FF), BF16),
        ("da", (C, D), BF16),
        ("dt", (C, 3 * D), BF16),
    )
    outs = pl.pallas_call(
        functools.partial(layer_kernel, sections),
        out_shape=[sds((per, C, D), BF16)] * 2
        + [sds((2, 8, D), F32)]
        + [sds((chunks,) + s, t) for _, s, t in saved],
        in_specs=[ANY] * 2 + [IN_VMEM] * 3 + [ANY] * 4,
        out_specs=[ANY] * 2 + [IN_VMEM] + [ANY] * len(saved),
        scratch_shapes=[pltpu.VMEM(shape, BF16) for shape in ((D, 3 * D), (D, D), (D, FF), (FF, D))]
        + [
            pltpu.VMEM((chunks, C, D), BF16),
            pltpu.VMEM((2, C, D), BF16),
            pltpu.VMEM((chunks, C, D), BF16),
            pltpu.VMEM((chunks * C, D), BF16),
            pltpu.VMEM((chunks * C, D), BF16),
            pltpu.VMEM((WIN * C, C), F32),
            pltpu.VMEM((WIN, C, D), F32),
            pltpu.VMEM((WIN, C, D), F32),
            pltpu.VMEM((16, C), F32),
            pltpu.VMEM((C, D), BF16),
            pltpu.VMEM((D, 128), BF16),
        ]
        + [pltpu.VMEM((2,) + s, t) for _, s, t in staged]
        + [pltpu.VMEM((2, C, 3 * D), BF16)]
        + [DMA((chunks,)), DMA((chunks,)), DMA((per,)), DMA((per,))] * 2
        + [DMA((8, 2)), DMA((4, 2)), DMA((5, 2)), DMA((4,))],
        compiler_params=pltpu.CompilerParams(
            collective_id=0, has_side_effects=True, vmem_limit_bytes=VMEM_LIMIT
        ),
        name="layers",
    )(tokens.reshape(per, C, D), cotangent.reshape(per, C, D), docs, *weights)
    return outs[0], outs[1], outs[2], {name: out for (name, _, _), out in zip(saved, outs[3:])}


def matmul_lt(left_side, right_side):
    rows = left_side.shape[0] * left_side.shape[1]
    return lax.dot_general(
        left_side.reshape(rows, -1),
        right_side.reshape(rows, -1),
        (((0,), (0,)), ((), ())),
        preferred_element_type=F32,
    )


UNIT = 256
UNITS = 9 + 3 + 12 + 12
NARROW = 9 + 3 + 12
LENT = 6
LENT_SHORT = 3
LAGS = (4, 8, 12)


def pair_first(unit):
    return lax.rem(unit, 4) != 3


def dot_tn(a, b):
    return lax.dot_general(a, b, (((0,), (0,)), ((), ())), preferred_element_type=F32)


def weight_grad_kernel(
    s_na,
    s_dt,
    s_mixed,
    s_da,
    s_nm,
    s_dh,
    s_act,
    s_db,
    gains,
    o_qkv,
    o_out,
    o_up,
    o_down,
    o_gains,
    left,
    right,
    act,
    made,
    got_a,
    got_b,
    got_c,
    total,
    gain_own,
    gain_in,
    left_sems,
    right_sems,
    act_sem,
    a_sends,
    a_arrivals,
    b_sends,
    b_arrivals,
    c_sends,
    c_arrivals,
    out_sem,
    gain_sends,
    gain_arrivals,
    lent_sends,
    lent_arrivals,
    back_sends,
    back_arrivals,
    here,
):
    section = lax.axis_index("section")
    dp = lax.axis_index("dp")
    x, near, far = lax.rem(dp, 2), lax.rem(dp // 2, 2), dp // 4
    lender = section < 2
    across = 3 - section
    loan = jnp.where((section == 0) | (section == 3), LENT, LENT_SHORT)

    def lent(unit):
        return (unit < 2 * loan) & (lax.rem(unit, 2) == 1)

    over_x, over_near, over_far = dp + 1 - 2 * x, dp + 2 - 4 * near, dp + 4 - 8 * far

    def load_left(src, slot):
        return pltpu.make_async_copy(src, left.at[slot], left_sems.at[slot])

    def load_right(src, column, slot):
        columns = pl.ds(pl.multiple_of(column * UNIT, UNIT), UNIT)
        return pltpu.make_async_copy(src.at[:, columns], right.at[slot], right_sems.at[slot])

    def start_right(unit):
        slot = lax.rem(unit, 2)

        @pl.when(unit < 9)
        def _():
            load_right(s_dt, unit, slot).start()

        @pl.when((unit >= 9) & (unit < 12))
        def _():
            load_right(s_da, unit - 9, slot).start()

        @pl.when((unit >= 12) & (unit < NARROW))
        def _():
            load_right(s_dh, unit - 12, slot).start()

    load_left(s_na, 0).start()
    start_right(0)
    gain_own[...] = jnp.sum(gains[...], axis=1, keepdims=True) + jnp.zeros((2, 8, D), F32)

    barrier = pltpu.get_barrier_semaphore()
    for step in range(1, 8):
        other = lax.rem(dp + step, 8)
        pl.semaphore_signal(barrier, inc=1, device_id=(other, section), device_id_type=MESH)

    @pl.when(lender)
    def _():
        pl.semaphore_wait(barrier, 8)
        pl.semaphore_signal(here, inc=1, device_id=(dp, across), device_id_type=MESH)

    @pl.when(jnp.logical_not(lender))
    def _():
        pl.semaphore_signal(barrier, inc=1, device_id=(dp, across), device_id_type=MESH)
        pl.semaphore_wait(barrier, 7)

    def gain_copy(step):
        other = lax.rem(dp + step, 8)
        return pltpu.make_async_remote_copy(
            gain_own,
            gain_in.at[step - 1],
            gain_sends.at[step - 1],
            gain_arrivals.at[step - 1],
            device_id=(other, section),
            device_id_type=MESH,
        )

    for step in range(1, 8):
        gain_copy(step).start()

    def send(unit, src, dst, sends, arrivals, to):
        pltpu.make_async_remote_copy(
            src,
            dst.at[unit],
            sends.at[unit],
            arrivals.at[unit],
            device_id=(to, section),
            device_id_type=MESH,
        ).start()

    def first_add(unit):
        @pl.when(pair_first(unit))
        def _():
            send(unit, made.at[unit, 1 - x], got_a, a_sends, a_arrivals, over_x)

        @pl.when(jnp.logical_not(pair_first(unit)))
        def _():
            send(unit, made.at[unit, :, 1 - near], got_a, a_sends, a_arrivals, over_near)

    def second_add(unit):
        await_arrival(got_a.at[unit], a_arrivals.at[unit])

        @pl.when(pair_first(unit))
        def _():
            made[unit, x] = (made[unit, x].astype(F32) + got_a[unit].astype(F32)).astype(BF16)
            send(unit, made.at[unit, x, 1 - near], got_b, b_sends, b_arrivals, over_near)

        @pl.when(jnp.logical_not(pair_first(unit)))
        def _():
            made[unit, :, near] = (made[unit, :, near].astype(F32) + got_a[unit].astype(F32)).astype(BF16)
            send(unit, made.at[unit, 1 - x, near], got_b, b_sends, b_arrivals, over_x)

    def third_add(unit):
        await_arrival(got_b.at[unit], b_arrivals.at[unit])
        made[unit, x, near] = (made[unit, x, near].astype(F32) + got_b[unit].astype(F32)).astype(BF16)
        send(unit, made.at[unit, x, near, 1 - far], got_c, c_sends, c_arrivals, over_far)

    def finish(unit):
        await_arrival(got_c.at[unit], c_arrivals.at[unit])
        total[unit] = made[unit, x, near, far].astype(F32) + got_c[unit].astype(F32)

        @pl.when(unit < UNITS)
        def _():
            deliver(unit)

        @pl.when(unit >= UNITS)
        def _():
            give_back(unit - UNITS)

    def lend(place):
        pltpu.make_async_remote_copy(
            made.at[2 * place + 1],
            made.at[UNITS + place],
            lent_sends.at[place],
            lent_arrivals.at[place],
            device_id=(dp, across),
            device_id_type=MESH,
        ).start()

    def give_back(place):
        pltpu.make_async_remote_copy(
            total.at[UNITS + place],
            total.at[2 * place + 1],
            back_sends.at[place],
            back_arrivals.at[place],
            device_id=(dp, across),
            device_id_type=MESH,
        ).start()

    def added_here(unit):
        kept = lender & (unit < UNITS) & jnp.logical_not(lent(unit))
        return kept | (jnp.logical_not(lender) & (unit < UNITS + loan))

    def deliver(unit):
        for first, end, ref in ((0, 9, o_qkv), (9, 12, o_out), (12, NARROW, o_up)):

            @pl.when((unit >= first) & (unit < end))
            def _():
                columns = pl.ds(pl.multiple_of((unit - first) * UNIT, UNIT), UNIT)
                pltpu.make_async_copy(total.at[unit], ref.at[:, columns], out_sem).start()

        @pl.when(unit >= NARROW)
        def _():
            column, row = (unit - NARROW) // 4, lax.rem(unit - NARROW, 4)
            columns = pl.ds(pl.multiple_of(column * UNIT, UNIT), UNIT)
            rows = pl.ds(pl.multiple_of(row * 96, 96), 96)
            pltpu.make_async_copy(total.at[unit], o_down.at[rows, columns], out_sem).start()

    def advance(now):
        for lag, action in zip(LAGS[::-1], (finish, third_add, second_add)):

            @pl.when((now >= lag) & added_here(now - lag))
            def _():
                action(now - lag)

    def narrow(unit, carry):
        slot = lax.rem(unit, 2)
        side = jnp.where((unit >= 9) & (unit < 12), 1, 0)

        @pl.when(unit == 1)
        def _():
            load_left(s_mixed, 1).start()
            pltpu.make_async_copy(s_act, act, act_sem).start()

        @pl.when(unit == 9)
        def _():
            load_left(s_nm, 0).start()

        @pl.when(unit == 12)
        def _():
            load_left(s_db, 1).start()

        start_right(unit + 1)

        @pl.when((unit == 0) | (unit == 12))
        def _():
            load_left(s_na, 0).wait()

        @pl.when(unit == 9)
        def _():
            load_left(s_mixed, 1).wait()

        load_right(s_dt, 0, slot).wait()
        grad = dot_tn(left[side], right[slot]).astype(BF16)
        for shard in range(8):
            made[unit, shard % 2, shard // 2 % 2, shard // 4] = grad[shard * 96 : (shard + 1) * 96]

        @pl.when(lender & lent(unit))
        def _():
            lend(lax.rem(unit, 2 * LENT) // 2)

        @pl.when(added_here(unit))
        def _():
            first_add(unit)

        advance(unit)
        return carry

    lax.fori_loop(0, NARROW, narrow, 0)
    load_left(s_db, 1).wait()
    pltpu.make_async_copy(s_act, act, act_sem).wait()

    def wide(step, carry):
        column, shard = step // 8, lax.rem(step, 8)
        columns = pl.ds(pl.multiple_of(column * UNIT, UNIT), UNIT)
        rows = pl.ds(pl.multiple_of(shard * 384, 384), 384)
        grad = dot_tn(act[:, rows], left[1, :, columns]).astype(BF16)
        first = NARROW + 4 * column
        for part in range(4):
            made[first + part, lax.rem(shard, 2), lax.rem(shard // 2, 2), shard // 4] = grad[part * 96 : (part + 1) * 96]

        @pl.when(shard == 7)
        def _():
            for part in range(4):
                first_add(first + part)

        @pl.when(lax.rem(step, 2) == 1)
        def _():
            advance(NARROW + step // 2)

        return carry

    lax.fori_loop(0, 24, wide, 0)

    def drain(now, carry):
        advance(now)
        return carry

    @pl.when(jnp.logical_not(lender))
    def _():
        pl.semaphore_wait(here, 1)

        def borrowed(unit, carry):
            await_arrival(made.at[unit], lent_arrivals.at[unit - UNITS])
            first_add(unit)
            advance(unit)
            return carry

        lax.fori_loop(UNITS, UNITS + loan, borrowed, 0)
        lax.fori_loop(UNITS + loan, UNITS + loan + LAGS[-1], drain, 0)

    @pl.when(lender)
    def _():
        lax.fori_loop(UNITS, UNITS + LAGS[-1], drain, 0)

    for step in range(1, 8):
        gain_copy(step).wait()
    sums = gain_own[:, 0:1]
    for step in range(7):
        sums = sums + gain_in[step, :, 0:1]
    o_gains[...] = sums

    def sent(unit, carry):
        @pl.when(added_here(unit))
        def _():
            await_arrival(got_a.at[unit], a_sends.at[unit])
            await_arrival(got_b.at[unit], b_sends.at[unit])
            await_arrival(got_c.at[unit], c_sends.at[unit])

        return carry

    lax.fori_loop(0, UNITS + LENT, sent, 0)

    @pl.when(lender)
    def _():
        def returned(place, carry):
            await_arrival(made.at[UNITS + place], lent_sends.at[place])
            await_arrival(total.at[2 * place + 1], back_arrivals.at[place])
            deliver(2 * place + 1)
            return carry

        lax.fori_loop(0, loan, returned, 0)

    @pl.when(jnp.logical_not(lender))
    def _():
        def returned(place, carry):
            await_arrival(total.at[UNITS + place], back_sends.at[place])
            return carry

        lax.fori_loop(0, loan, returned, 0)

    await_arrival(total.at[pl.ds(0, UNITS)], out_sem)


def weight_grads(na, dt, mixed, da, nm, dh, act, db, gains):
    tokens = na.shape[0] * na.shape[1]
    sds = jax.ShapeDtypeStruct
    operands = [v.reshape(tokens, -1) for v in (na, dt, mixed, da, nm, dh, act, db)]
    return pl.pallas_call(
        weight_grad_kernel,
        out_shape=[
            sds((96, 3 * D), F32),
            sds((96, D), F32),
            sds((96, FF), F32),
            sds((384, D), F32),
            sds((2, 1, D), F32),
        ],
        in_specs=[ANY] * 8 + [IN_VMEM],
        out_specs=[ANY] * 4 + [IN_VMEM],
        scratch_shapes=[
            pltpu.VMEM((2, tokens, D), BF16),
            pltpu.VMEM((2, tokens, UNIT), BF16),
            pltpu.VMEM((tokens, FF), BF16),
            pltpu.VMEM((UNITS + LENT, 2, 2, 2, 96, UNIT), BF16),
            pltpu.VMEM((UNITS + LENT, 2, 2, 96, UNIT), BF16),
            pltpu.VMEM((UNITS + LENT, 2, 96, UNIT), BF16),
            pltpu.VMEM((UNITS + LENT, 96, UNIT), BF16),
            pltpu.VMEM((UNITS + LENT, 96, UNIT), F32),
            pltpu.VMEM((2, 8, D), F32),
            pltpu.VMEM((7, 2, 8, D), F32),
            DMA((2,)),
            DMA((2,)),
            DMA,
            DMA((UNITS + LENT,)),
            DMA((UNITS + LENT,)),
            DMA((UNITS + LENT,)),
            DMA((UNITS + LENT,)),
            DMA((UNITS + LENT,)),
            DMA((UNITS + LENT,)),
            DMA,
            DMA((7,)),
            DMA((7,)),
            DMA((LENT,)),
            DMA((LENT,)),
            DMA((LENT,)),
            DMA((LENT,)),
            pltpu.SemaphoreType.REGULAR,
        ],
        compiler_params=pltpu.CompilerParams(
            collective_id=2, has_side_effects=True, vmem_limit_bytes=VMEM_LIMIT
        ),
        name="weight_grads",
    )(*operands, gains)


def hand_over_kernel(gains, *refs):
    sources, results, (gain_attn, gain_mlp), held = refs[:6], refs[6:12], refs[12:14], refs[14:20]
    come, go = refs[20], refs[21]
    arriving = [
        pltpu.make_async_copy(src, buf, come.at[at]) for at, (src, buf) in enumerate(zip(sources, held))
    ]
    leaving = [
        pltpu.make_async_copy(buf, dst, go.at[at]) for at, (buf, dst) in enumerate(zip(held, results))
    ]
    for copy in arriving:
        copy.start()
    shift = lax.rem(D - 96 * lax.axis_index("dp"), D)
    for kind, ref in enumerate((gain_attn, gain_mlp)):
        turned = pltpu.roll(jnp.broadcast_to(gains[kind], (8, D)), shift, 1)
        ref[...] = turned[:1, :96]
    for copy, onward in zip(arriving, leaving):
        copy.wait()
        onward.start()
    for copy in leaving:
        copy.wait()


def hand_over(output, input_grad, shards, gains):
    sds = jax.ShapeDtypeStruct
    sources = (output, input_grad, *shards)
    outs = pl.pallas_call(
        hand_over_kernel,
        out_shape=[sds(v.shape, v.dtype) for v in sources] + [sds((1, 96), F32)] * 2,
        in_specs=[IN_VMEM] + [ANY] * 6,
        out_specs=[ANY] * 6 + [IN_VMEM] * 2,
        scratch_shapes=[pltpu.VMEM(v.shape, v.dtype) for v in sources] + [DMA((6,)), DMA((6,))],
        compiler_params=pltpu.CompilerParams(vmem_limit_bytes=VMEM_LIMIT),
        name="hand_over",
    )(gains, *sources)
    output, input_grad, qkv, out, up, down, gain_attn, gain_mlp = outs
    return output, input_grad, gain_attn, qkv[None], out[None], gain_mlp, up[None], down[None]


def body(tokens, cotangent, doc_ids, gain_attn, w_qkv, w_out, gain_mlp, w_up, w_down):
    sections = lax.axis_size("section")
    rows, seq = doc_ids.shape
    chunks = rows * seq // C
    weights = (gain_attn, gain_mlp, w_qkv[0], w_out[0], w_up[0], w_down[0])
    output, input_grad, gains, kept = layers(sections, chunks, tokens, cotangent, doc_ids, weights)
    db, dh, da, dt = kept["db"], kept["dh"], kept["da"], kept["dt"]
    if lax.axis_size("dp") == 8 and sections == 4 and chunks == 8:
        qkv, out, up, down, gains = weight_grads(
            kept["na"], dt, kept["mixed"], da, kept["nm"], dh, kept["act"], db, gains
        )
        return hand_over(
            output.reshape(tokens.shape), input_grad.reshape(cotangent.shape), (qkv, out, up, down), gains
        )
    gains = jnp.sum(gains, axis=1)
    grads = (
        gains[0],
        matmul_lt(kept["na"], dt),
        matmul_lt(kept["mixed"], da),
        gains[1],
        matmul_lt(kept["nm"], dh),
        matmul_lt(kept["act"], db),
    )
    shards = lax.psum_scatter(grads, "dp", scatter_dimension=0, tiled=True)
    return (
        output.reshape(tokens.shape),
        input_grad.reshape(cotangent.shape),
        *(shard[None] for shard in shards),
    )


def solution(mesh):
    rows = P(("dp", "section"), None)
    layer = P("section", None)
    matrix = P("section", None, None)
    in_specs = (rows, rows, P("dp", None), layer, matrix, matrix, layer, matrix, matrix)
    split = P("section", "dp")
    split_matrix = P("section", "dp", None)
    out_specs = (rows, rows, split, split_matrix, split_matrix, split, split_matrix, split_matrix)
    return jax.shard_map(body, mesh=mesh, in_specs=in_specs, out_specs=out_specs, check_vma=False)
```

```python
import functools

import jax
import jax.numpy as jnp
from jax import lax
from jax.experimental import pallas as pl
from jax.experimental.pallas import tpu as pltpu
from jax.sharding import PartitionSpec as P

D = 768
HEADS = 12
HD = 64
FF = 3072
C = 256
WIN = 3
PAIRS = HEADS // 2
EPS = 1e-05
NEG = -1e30
MESH = pl.DeviceIdType.MESH
BF16 = jnp.bfloat16
F32 = jnp.float32
VMEM_LIMIT = 60 * 1024 * 1024


def dot(a, b):
    return jnp.dot(a, b, preferred_element_type=F32)


def dot_nt(a, b):
    return lax.dot_general(a, b, (((1,), (1,)), ((), ())), preferred_element_type=F32)


def row_mean(v):
    return jnp.mean(v, axis=-1, keepdims=True)


def greet(section, sections):
    dp = lax.axis_index("dp")
    barrier = pltpu.get_barrier_semaphore()
    for step in range(1, sections):
        other = lax.rem(section + step, sections)
        pl.semaphore_signal(barrier, inc=1, device_id=(dp, other), device_id_type=MESH)
    pl.semaphore_wait(barrier, sections - 1)


def lane_masks():
    lane = lax.broadcasted_iota(jnp.int32, (1, 2 * HD), 1)
    low = (lane < HD).astype(F32)
    return low.astype(BF16), (1.0 - low).astype(BF16), lane < HD


def two_heads(pair, low, high):
    return jnp.concatenate([pair * low, pair * high], axis=0)


def await_arrival(buf, sem):
    pltpu.make_async_copy(buf, buf, sem).wait()


def scatter_rows(section, sections, per, rows, inbox, sems, send_sems, target):
    dp = lax.axis_index("dp")
    for piece in range(per):
        slot = section * per + piece

        @pl.when(section != target)
        def _():
            pltpu.make_async_remote_copy(
                rows.at[piece],
                inbox.at[slot],
                send_sems.at[piece],
                sems.at[slot],
                device_id=(dp, target),
                device_id_type=MESH,
            ).start()

        @pl.when(section == target)
        def _():
            pltpu.make_async_copy(rows.at[piece], inbox.at[slot], sems.at[slot]).start()


def drain_rows(section, sections, per, rows, send_sems, target):
    for piece in range(per):

        @pl.when(section != target)
        def _():
            pltpu.make_async_copy(rows.at[piece], rows.at[piece], send_sems.at[piece]).wait()


def pass_on(section, chunk, per, last, step, source, inbox, result, sends, arrivals, landed):
    dp = lax.axis_index("dp")
    owner = chunk // per

    @pl.when(section != last)
    def _():
        pltpu.make_async_remote_copy(
            source,
            inbox.at[chunk],
            sends.at[chunk],
            arrivals.at[chunk],
            device_id=(dp, section + step),
            device_id_type=MESH,
        ).start()

    @pl.when((section == last) & (owner != last))
    def _():
        pltpu.make_async_remote_copy(
            source,
            result.at[lax.rem(chunk, per)],
            sends.at[chunk],
            landed.at[lax.rem(chunk, per)],
            device_id=(dp, owner),
            device_id_type=MESH,
        ).start()

    @pl.when((section == last) & (owner == last))
    def _():
        pltpu.make_async_copy(source, result.at[lax.rem(chunk, per)], sends.at[chunk]).start()


def settle(section, first, end, per, last, source, result, sends, landed):
    def one(chunk, carry):
        await_arrival(source, sends.at[chunk])
        return carry

    lax.fori_loop(first, end, one, 0)
    for piece in range(per):

        @pl.when(section != last)
        def _():
            await_arrival(result.at[piece], landed.at[piece])


def fill_bias(docs, chunk, bias):
    per_row = docs.shape[1] // C
    row, place = chunk // per_row, lax.rem(chunk, per_row)

    def numbers(block):
        start = pl.multiple_of(jnp.maximum(block, 0) * C, C)
        return docs[pl.ds(row, 1), pl.ds(start, C)].astype(F32)

    queries = numbers(place)
    for part in range(WIN):
        keys = jnp.transpose(jnp.broadcast_to(numbers(place - (WIN - 1) + part), (128, C)))
        for half in range(C // 128):
            lanes = slice(half * 128, (half + 1) * 128)
            allowed = keys == queries[:, lanes]
            if part == WIN - 1:
                down = lax.broadcasted_iota(jnp.int32, (C, 128), 0)
                across = lax.broadcasted_iota(jnp.int32, (C, 128), 1) + half * 128
                allowed = allowed & (down <= across)
            bias[part * C : (part + 1) * C, lanes] = jnp.where(allowed, 0.0, NEG)


def by_blocks(docs, chunk, attend):
    place = lax.rem(chunk, docs.shape[1] // C)
    for blocks in range(1, WIN + 1):

        @pl.when((place == blocks - 1) if blocks < WIN else (place >= WIN - 1))
        def _():
            attend(blocks)


def layer_kernel(
    sections,
    tokens,
    cotangent,
    docs,
    gain_a,
    gain_m,
    h_qkv,
    h_out,
    h_up,
    h_down,
    result,
    grad_result,
    gains,
    s_q,
    s_na,
    s_mixed,
    s_probs,
    s_mid,
    s_nm,
    s_act,
    s_dg,
    s_db,
    s_dh,
    s_da,
    s_dt,
    w_qkv,
    w_out,
    w_up,
    w_down,
    inbox,
    outbox,
    grads,
    kbuf,
    vbuf,
    bias,
    dk_acc,
    dv_acc,
    inner,
    b_dmix,
    marks,
    b_q,
    b_na,
    b_mixed,
    b_probs,
    b_mid,
    b_nm,
    b_act,
    b_dg,
    b_dt,
    arrivals,
    sends,
    first_sends,
    landed,
    grad_arrivals,
    grad_sends,
    grad_first_sends,
    grad_landed,
    kept_f,
    kept_b,
    loads,
    weight_sems,
):
    section = lax.axis_index("section")
    chunks = inbox.shape[0]
    per = tokens.shape[0]
    last = sections - 1
    weights = [
        pltpu.make_async_copy(src, dst, weight_sems.at[kind])
        for kind, (src, dst) in enumerate(
            ((h_qkv, w_qkv), (h_out, w_out), (h_up, w_up), (h_down, w_down))
        )
    ]
    weights[0].start()

    def at_first(chunk, copy, *later):
        @pl.when(chunk == 0)
        def _():
            copy.wait()
            for other in later:
                other.start()

    def clear():
        dk_acc[...] = jnp.zeros_like(dk_acc)
        dv_acc[...] = jnp.zeros_like(dv_acc)
        gains[...] = jnp.zeros_like(gains)
        owner_of = lax.broadcasted_iota(jnp.int32, (D, 128), 0) // HD
        own = owner_of == lax.broadcasted_iota(jnp.int32, (D, 128), 1)
        marks[...] = own.astype(F32).astype(BF16)

    greet(section, sections)
    scatter_rows(section, sections, per, tokens, inbox, arrivals, first_sends, 0)
    scatter_rows(section, sections, per, cotangent, grads, grad_arrivals, grad_first_sends, last)
    low, high, is_low = lane_masks()
    centered = jnp.where(section == 0, 1.0, 0.0).astype(F32)

    @pl.when(section != 0)
    def _():
        clear()

    def keep_forward(chunk, slot):
        pairs = (
            (b_q, s_q),
            (b_na, s_na),
            (b_mixed, s_mixed),
            (b_probs, s_probs),
            (b_mid, s_mid),
            (b_nm, s_nm),
            (b_act, s_act),
            (b_dg, s_dg),
        )
        return [
            pltpu.make_async_copy(src.at[slot], dst.at[chunk], kept_f.at[kind, slot])
            for kind, (src, dst) in enumerate(pairs)
        ]

    def forward_chunk(chunk, carry):
        slot = lax.rem(chunk, 2)

        @pl.when(chunk >= 2)
        def _():
            for copy in keep_forward(chunk - 2, slot):
                copy.wait()

        todo = keep_forward(chunk, slot)
        at_first(chunk, *weights)
        fill_bias(docs, chunk, bias)
        await_arrival(inbox.at[chunk], arrivals.at[chunk])
        x = inbox[chunk].astype(F32)
        x = x - centered * row_mean(x)
        na = (x * lax.rsqrt(row_mean(x * x) + EPS) * gain_a[...]).astype(BF16)
        b_na[slot] = na
        todo[1].start()
        b_q[slot] = (dot(na, w_qkv[:, :D]).astype(BF16) * (HD**-0.5)).astype(BF16)
        here = pl.ds(pl.multiple_of(chunk * C, C), C)
        kbuf[here, :] = dot(na, w_qkv[:, D : 2 * D]).astype(BF16)
        vbuf[here, :] = dot(na, w_qkv[:, 2 * D :]).astype(BF16)
        todo[0].start()
        def attend(blocks):
            window = pl.ds(pl.multiple_of((chunk - blocks + 1) * C, C), blocks * C)
            masked = slice((WIN - blocks) * C, WIN * C)
            def lanes_of(pair):
                return slice(pair * 2 * HD, (pair + 1) * 2 * HD)

            def scores(pair):
                q2 = two_heads(b_q[slot, :, lanes_of(pair)], low, high)
                return dot_nt(kbuf[window, lanes_of(pair)], q2)

            both = jnp.concatenate([bias[masked, :], bias[masked, :]], axis=1)
            ahead = scores(0)
            for pair in range(PAIRS):
                s = ahead + both
                if pair + 1 < PAIRS:
                    ahead = scores(pair + 1)
                e = jnp.exp(s - jnp.max(s, axis=0, keepdims=True))
                probs = (e * (1.0 / jnp.sum(e, axis=0, keepdims=True))).astype(BF16)
                b_probs[slot, pair, masked, :] = probs
                o = lax.dot_general(
                    probs, vbuf[window, lanes_of(pair)], (((0,), (0,)), ((), ())), preferred_element_type=F32
                )
                b_mixed[slot, :, lanes_of(pair)] = jnp.where(is_low, o[:C], o[C:]).astype(BF16)

        by_blocks(docs, chunk, attend)
        todo[2].start()
        todo[3].start()
        at_first(chunk, weights[1])
        branch = dot(b_mixed[slot], w_out[...])
        mid = x + branch - row_mean(branch)
        b_mid[slot] = mid
        todo[4].start()
        nm = (mid * lax.rsqrt(row_mean(mid * mid) + EPS) * gain_m[...]).astype(BF16)
        b_nm[slot] = nm
        todo[5].start()
        at_first(chunk, weights[2])
        k0 = 0.7978845608028654
        k1 = 0.044715
        for part in range(FF // D):
            cols = slice(part * D, (part + 1) * D)
            h = dot(nm, w_up[:, cols])
            h2 = h * h
            t = jnp.tanh(h * (k0 + (k0 * k1) * h2))
            half = 0.5 + 0.5 * t
            b_act[slot, :, cols] = (h * half).astype(BF16)
            slope = half + (h * (1.0 - t * t)) * (0.5 * k0 + (1.5 * k0 * k1) * h2)
            b_dg[slot, :, cols] = slope.astype(BF16)
        todo[6].start()
        todo[7].start()
        at_first(chunk, weights[3])
        branch = dot(b_act[slot], w_down[...])

        @pl.when(chunk >= 2)
        def _():
            await_arrival(outbox.at[slot], sends.at[chunk - 2])

        outbox[slot] = (b_mid[slot] + branch - row_mean(branch)).astype(BF16)
        pass_on(section, chunk, per, last, 1, outbox.at[slot], inbox, result, sends, arrivals, landed)
        return carry

    lax.fori_loop(0, chunks, forward_chunk, 0)
    for chunk in (chunks - 2, chunks - 1):
        for copy in keep_forward(chunk, chunk % 2):
            copy.wait()

    @pl.when(section == 0)
    def _():
        clear()

    def fetches(chunk, slot):
        pairs = ((s_dg, b_dg), (s_mid, b_mid), (s_mixed, b_mixed), (s_q, b_q), (s_probs, b_probs))
        return [
            pltpu.make_async_copy(src.at[chunk], dst.at[slot], loads.at[kind, slot])
            for kind, (src, dst) in enumerate(pairs)
        ]

    def keep_backward(chunk, slot):
        pairs = ((b_nm, s_db), (b_act, s_dh), (b_na, s_da), (b_dt, s_dt))
        return [
            pltpu.make_async_copy(src.at[slot], dst.at[chunk], kept_b.at[kind, slot])
            for kind, (src, dst) in enumerate(pairs)
        ]

    def folded(v):
        return jnp.sum(v.reshape(C // 8, 8, D), axis=0)

    def backward_chunk(step, carry):
        chunk = chunks - 1 - step
        slot = lax.rem(chunk, 2)

        @pl.when((step >= 1) & (chunk >= 1))
        def _():
            for copy in fetches(chunk - 1, 1 - slot):
                copy.start()

        @pl.when(step >= 2)
        def _():
            for copy in keep_backward(chunk + 2, slot):
                copy.wait()

        @pl.when(step >= 2)
        def _():
            for copy in fetches(chunk, slot):
                copy.wait()

        todo = keep_backward(chunk, slot)
        await_arrival(grads.at[chunk], grad_arrivals.at[chunk])
        g = grads[chunk].astype(F32)
        db = (g - row_mean(g)).astype(BF16)
        b_nm[slot] = db
        todo[0].start()
        for part in range(FF // D):
            cols = slice(part * D, (part + 1) * D)
            d_active = dot_nt(db, w_down[cols, :])
            b_act[slot, :, cols] = (d_active * b_dg[slot, :, cols].astype(F32)).astype(BF16)
        todo[1].start()
        dn = dot_nt(b_act[slot], w_up[...])
        mid = b_mid[slot]
        factor = lax.rsqrt(row_mean(mid * mid) + EPS)
        unit = mid * factor
        gains[1] += folded(dn * unit)
        dn = dn * gain_m[...]
        d_mid = g + factor * (dn - unit * row_mean(dn * unit))
        da = (d_mid - row_mean(d_mid)).astype(BF16)
        b_na[slot] = da
        todo[2].start()
        b_mid[slot] = d_mid
        dmix = dot_nt(da, w_out[...]).astype(BF16)
        b_dmix[...] = dmix
        prod = dmix.astype(F32) * b_mixed[slot].astype(F32)
        inner[...] = jnp.transpose(dot(prod.astype(BF16), marks[...]))[:16]
        def attend(blocks):
            window = pl.ds(pl.multiple_of((chunk - blocks + 1) * C, C), blocks * C)
            masked = slice((WIN - blocks) * C, WIN * C)
            for pair in range(PAIRS):
                lanes = slice(pair * 2 * HD, (pair + 1) * 2 * HD)
                q2 = two_heads(b_q[slot, :, lanes], low, high)
                do2 = two_heads(b_dmix[:, lanes], low, high)
                keys = kbuf[window, lanes]
                even, odd = slice(2 * pair, 2 * pair + 1), slice(2 * pair + 1, 2 * pair + 2)
                mean = jnp.concatenate([inner[even, :], inner[odd, :]], axis=1)
                probs = b_probs[slot, pair, masked, :]
                ds = (probs.astype(F32) * (dot_nt(vbuf[window, lanes], do2) - mean)).astype(BF16)
                dv = dot(probs, do2)
                dk = dot(ds, q2)
                for part in range(blocks):
                    place = lax.rem(chunk - blocks + 1 + part, WIN)
                    rows = slice(part * C, (part + 1) * C)
                    dv_acc[place, :, lanes] += dv[rows]
                    dk_acc[place, :, lanes] += dk[rows]
                dq = dot(jnp.transpose(keys), ds)
                dq = jnp.concatenate([dq[:HD, :C], dq[HD:, C:]], axis=0)
                b_dt[slot, :, lanes] = (jnp.transpose(dq) * (HD**-0.5)).astype(BF16)

        by_blocks(docs, chunk, attend)
        done = lax.rem(chunk, WIN)
        b_dt[slot, :, D : 2 * D] = dk_acc[done].astype(BF16)
        b_dt[slot, :, 2 * D :] = dv_acc[done].astype(BF16)
        dk_acc[done] = jnp.zeros((C, D), F32)
        dv_acc[done] = jnp.zeros((C, D), F32)
        todo[3].start()
        dn = dot_nt(b_dt[slot], w_qkv[...])
        x = inbox[chunk].astype(F32)
        x = x - centered * row_mean(x)
        factor = lax.rsqrt(row_mean(x * x) + EPS)
        unit = x * factor
        gains[0] += folded(dn * unit)
        dn = dn * gain_a[...]
        grad = b_mid[slot] + factor * (dn - unit * row_mean(dn * unit))
        grad = grad - centered * row_mean(grad)
        inbox[chunk] = grad.astype(BF16)
        pass_on(
            section, chunk, per, 0, -1, inbox.at[chunk], grads, grad_result, grad_sends, grad_arrivals, grad_landed
        )
        return carry

    lax.fori_loop(0, chunks, backward_chunk, 0)
    for chunk in (0, 1):
        for copy in keep_backward(chunk, chunk):
            copy.wait()
    drain_rows(section, sections, per, tokens, first_sends, 0)
    drain_rows(section, sections, per, cotangent, grad_first_sends, last)
    settle(section, chunks - 2, chunks, per, last, outbox.at[0], result, sends, landed)
    settle(section, 0, chunks, per, 0, inbox.at[0], grad_result, grad_sends, grad_landed)


ANY = pl.BlockSpec(memory_space=pl.ANY)
IN_VMEM = pl.BlockSpec(memory_space=pltpu.VMEM)
DMA = pltpu.SemaphoreType.DMA


def layers(sections, chunks, tokens, cotangent, docs, weights):
    per = chunks // sections
    sds = jax.ShapeDtypeStruct
    staged = (
        ("q", (C, D), BF16),
        ("na", (C, D), BF16),
        ("mixed", (C, D), BF16),
        ("probs", (PAIRS, WIN * C, 2 * C), BF16),
        ("mid", (C, D), F32),
        ("nm", (C, D), BF16),
        ("act", (C, FF), BF16),
        ("dg", (C, FF), BF16),
    )
    saved = staged + (
        ("db", (C, D), BF16),
        ("dh", (C, FF), BF16),
        ("da", (C, D), BF16),
        ("dt", (C, 3 * D), BF16),
    )
    outs = pl.pallas_call(
        functools.partial(layer_kernel, sections),
        out_shape=[sds((per, C, D), BF16)] * 2
        + [sds((2, 8, D), F32)]
        + [sds((chunks,) + s, t) for _, s, t in saved],
        in_specs=[ANY] * 2 + [IN_VMEM] * 3 + [ANY] * 4,
        out_specs=[ANY] * 2 + [IN_VMEM] + [ANY] * len(saved),
        scratch_shapes=[pltpu.VMEM(shape, BF16) for shape in ((D, 3 * D), (D, D), (D, FF), (FF, D))]
        + [
            pltpu.VMEM((chunks, C, D), BF16),
            pltpu.VMEM((2, C, D), BF16),
            pltpu.VMEM((chunks, C, D), BF16),
            pltpu.VMEM((chunks * C, D), BF16),
            pltpu.VMEM((chunks * C, D), BF16),
            pltpu.VMEM((WIN * C, C), F32),
            pltpu.VMEM((WIN, C, D), F32),
            pltpu.VMEM((WIN, C, D), F32),
            pltpu.VMEM((16, C), F32),
            pltpu.VMEM((C, D), BF16),
            pltpu.VMEM((D, 128), BF16),
        ]
        + [pltpu.VMEM((2,) + s, t) for _, s, t in staged]
        + [pltpu.VMEM((2, C, 3 * D), BF16)]
        + [DMA((chunks,)), DMA((chunks,)), DMA((per,)), DMA((per,))] * 2
        + [DMA((8, 2)), DMA((4, 2)), DMA((5, 2)), DMA((4,))],
        compiler_params=pltpu.CompilerParams(
            collective_id=0, has_side_effects=True, vmem_limit_bytes=VMEM_LIMIT
        ),
        name="layers",
    )(tokens.reshape(per, C, D), cotangent.reshape(per, C, D), docs, *weights)
    return outs[0], outs[1], outs[2], {name: out for (name, _, _), out in zip(saved, outs[3:])}


def matmul_lt(left_side, right_side):
    rows = left_side.shape[0] * left_side.shape[1]
    return lax.dot_general(
        left_side.reshape(rows, -1),
        right_side.reshape(rows, -1),
        (((0,), (0,)), ((), ())),
        preferred_element_type=F32,
    )


UNIT = 256
UNITS = 9 + 3 + 12 + 12
NARROW = 9 + 3 + 12
LENT = 6
LENT_SHORT = 3
LAGS = (4, 8, 12)


def pair_first(unit):
    return lax.rem(unit, 4) != 3


def dot_tn(a, b):
    return lax.dot_general(a, b, (((0,), (0,)), ((), ())), preferred_element_type=F32)


def weight_grad_kernel(
    s_na,
    s_dt,
    s_mixed,
    s_da,
    s_nm,
    s_dh,
    s_act,
    s_db,
    gains,
    o_qkv,
    o_out,
    o_up,
    o_down,
    o_gains,
    left,
    right,
    act,
    made,
    got_a,
    got_b,
    got_c,
    total,
    gain_own,
    gain_in,
    left_sems,
    right_sems,
    act_sem,
    a_sends,
    a_arrivals,
    b_sends,
    b_arrivals,
    c_sends,
    c_arrivals,
    out_sem,
    gain_sends,
    gain_arrivals,
    lent_sends,
    lent_arrivals,
    back_sends,
    back_arrivals,
    here,
):
    section = lax.axis_index("section")
    dp = lax.axis_index("dp")
    x, near, far = lax.rem(dp, 2), lax.rem(dp // 2, 2), dp // 4
    lender = section < 2
    across = 3 - section
    loan = jnp.where((section == 0) | (section == 3), LENT, LENT_SHORT)

    def lent(unit):
        return (unit < 2 * loan) & (lax.rem(unit, 2) == 1)

    over_x, over_near, over_far = dp + 1 - 2 * x, dp + 2 - 4 * near, dp + 4 - 8 * far

    def load_left(src, slot):
        return pltpu.make_async_copy(src, left.at[slot], left_sems.at[slot])

    def load_right(src, column, slot):
        columns = pl.ds(pl.multiple_of(column * UNIT, UNIT), UNIT)
        return pltpu.make_async_copy(src.at[:, columns], right.at[slot], right_sems.at[slot])

    def start_right(unit):
        slot = lax.rem(unit, 2)

        @pl.when(unit < 9)
        def _():
            load_right(s_dt, unit, slot).start()

        @pl.when((unit >= 9) & (unit < 12))
        def _():
            load_right(s_da, unit - 9, slot).start()

        @pl.when((unit >= 12) & (unit < NARROW))
        def _():
            load_right(s_dh, unit - 12, slot).start()

    load_left(s_na, 0).start()
    start_right(0)
    gain_own[...] = jnp.sum(gains[...], axis=1)

    barrier = pltpu.get_barrier_semaphore()
    for step in range(1, 8):
        other = lax.rem(dp + step, 8)
        pl.semaphore_signal(barrier, inc=1, device_id=(other, section), device_id_type=MESH)

    @pl.when(lender)
    def _():
        pl.semaphore_wait(barrier, 8)
        pl.semaphore_signal(here, inc=1, device_id=(dp, across), device_id_type=MESH)

    @pl.when(jnp.logical_not(lender))
    def _():
        pl.semaphore_signal(barrier, inc=1, device_id=(dp, across), device_id_type=MESH)
        pl.semaphore_wait(barrier, 7)

    def gain_copy(step):
        other = lax.rem(dp + step, 8)
        return pltpu.make_async_remote_copy(
            gain_own,
            gain_in.at[step - 1],
            gain_sends.at[step - 1],
            gain_arrivals.at[step - 1],
            device_id=(other, section),
            device_id_type=MESH,
        )

    for step in range(1, 8):
        gain_copy(step).start()

    def send(unit, src, dst, sends, arrivals, to):
        pltpu.make_async_remote_copy(
            src,
            dst.at[unit],
            sends.at[unit],
            arrivals.at[unit],
            device_id=(to, section),
            device_id_type=MESH,
        ).start()

    def first_add(unit):
        @pl.when(pair_first(unit))
        def _():
            send(unit, made.at[unit, 1 - x], got_a, a_sends, a_arrivals, over_x)

        @pl.when(jnp.logical_not(pair_first(unit)))
        def _():
            send(unit, made.at[unit, :, 1 - near], got_a, a_sends, a_arrivals, over_near)

    def second_add(unit):
        await_arrival(got_a.at[unit], a_arrivals.at[unit])

        @pl.when(pair_first(unit))
        def _():
            made[unit, x] = (made[unit, x].astype(F32) + got_a[unit].astype(F32)).astype(BF16)
            send(unit, made.at[unit, x, 1 - near], got_b, b_sends, b_arrivals, over_near)

        @pl.when(jnp.logical_not(pair_first(unit)))
        def _():
            made[unit, :, near] = (made[unit, :, near].astype(F32) + got_a[unit].astype(F32)).astype(BF16)
            send(unit, made.at[unit, 1 - x, near], got_b, b_sends, b_arrivals, over_x)

    def third_add(unit):
        await_arrival(got_b.at[unit], b_arrivals.at[unit])
        made[unit, x, near] = (made[unit, x, near].astype(F32) + got_b[unit].astype(F32)).astype(BF16)
        send(unit, made.at[unit, x, near, 1 - far], got_c, c_sends, c_arrivals, over_far)

    def finish(unit):
        await_arrival(got_c.at[unit], c_arrivals.at[unit])
        total[unit] = made[unit, x, near, far].astype(F32) + got_c[unit].astype(F32)

        @pl.when(unit < UNITS)
        def _():
            deliver(unit)

        @pl.when(unit >= UNITS)
        def _():
            give_back(unit - UNITS)

    def lend(place):
        pltpu.make_async_remote_copy(
            made.at[2 * place + 1],
            made.at[UNITS + place],
            lent_sends.at[place],
            lent_arrivals.at[place],
            device_id=(dp, across),
            device_id_type=MESH,
        ).start()

    def give_back(place):
        pltpu.make_async_remote_copy(
            total.at[UNITS + place],
            total.at[2 * place + 1],
            back_sends.at[place],
            back_arrivals.at[place],
            device_id=(dp, across),
            device_id_type=MESH,
        ).start()

    def added_here(unit):
        kept = lender & (unit < UNITS) & jnp.logical_not(lent(unit))
        return kept | (jnp.logical_not(lender) & (unit < UNITS + loan))

    def deliver(unit):
        for first, end, ref in ((0, 9, o_qkv), (9, 12, o_out), (12, NARROW, o_up)):

            @pl.when((unit >= first) & (unit < end))
            def _():
                columns = pl.ds(pl.multiple_of((unit - first) * UNIT, UNIT), UNIT)
                pltpu.make_async_copy(total.at[unit], ref.at[:, columns], out_sem).start()

        @pl.when(unit >= NARROW)
        def _():
            column, row = (unit - NARROW) // 4, lax.rem(unit - NARROW, 4)
            columns = pl.ds(pl.multiple_of(column * UNIT, UNIT), UNIT)
            rows = pl.ds(pl.multiple_of(row * 96, 96), 96)
            pltpu.make_async_copy(total.at[unit], o_down.at[rows, columns], out_sem).start()

    def advance(now):
        for lag, action in zip(LAGS[::-1], (finish, third_add, second_add)):

            @pl.when((now >= lag) & added_here(now - lag))
            def _():
                action(now - lag)

    def narrow(unit, carry):
        slot = lax.rem(unit, 2)
        side = jnp.where((unit >= 9) & (unit < 12), 1, 0)

        @pl.when(unit == 1)
        def _():
            load_left(s_mixed, 1).start()
            pltpu.make_async_copy(s_act, act, act_sem).start()

        @pl.when(unit == 9)
        def _():
            load_left(s_nm, 0).start()

        @pl.when(unit == 12)
        def _():
            load_left(s_db, 1).start()

        start_right(unit + 1)

        @pl.when((unit == 0) | (unit == 12))
        def _():
            load_left(s_na, 0).wait()

        @pl.when(unit == 9)
        def _():
            load_left(s_mixed, 1).wait()

        load_right(s_dt, 0, slot).wait()
        grad = dot_tn(left[side], right[slot]).astype(BF16)
        for shard in range(8):
            made[unit, shard % 2, shard // 2 % 2, shard // 4] = grad[shard * 96 : (shard + 1) * 96]

        @pl.when(lender & lent(unit))
        def _():
            lend(lax.rem(unit, 2 * LENT) // 2)

        @pl.when(added_here(unit))
        def _():
            first_add(unit)

        advance(unit)
        return carry

    lax.fori_loop(0, NARROW, narrow, 0)
    load_left(s_db, 1).wait()
    pltpu.make_async_copy(s_act, act, act_sem).wait()

    def wide(step, carry):
        column, shard = step // 8, lax.rem(step, 8)
        columns = pl.ds(pl.multiple_of(column * UNIT, UNIT), UNIT)
        rows = pl.ds(pl.multiple_of(shard * 384, 384), 384)
        grad = dot_tn(act[:, rows], left[1, :, columns]).astype(BF16)
        first = NARROW + 4 * column
        for part in range(4):
            made[first + part, lax.rem(shard, 2), lax.rem(shard // 2, 2), shard // 4] = grad[part * 96 : (part + 1) * 96]

        @pl.when(shard == 7)
        def _():
            for part in range(4):
                first_add(first + part)

        @pl.when(lax.rem(step, 2) == 1)
        def _():
            advance(NARROW + step // 2)

        return carry

    lax.fori_loop(0, 24, wide, 0)

    def drain(now, carry):
        advance(now)
        return carry

    @pl.when(jnp.logical_not(lender))
    def _():
        pl.semaphore_wait(here, 1)

        def borrowed(unit, carry):
            await_arrival(made.at[unit], lent_arrivals.at[unit - UNITS])
            first_add(unit)
            advance(unit)
            return carry

        lax.fori_loop(UNITS, UNITS + loan, borrowed, 0)
        lax.fori_loop(UNITS + loan, UNITS + loan + LAGS[-1], drain, 0)

    @pl.when(lender)
    def _():
        lax.fori_loop(UNITS, UNITS + LAGS[-1], drain, 0)

    for step in range(1, 8):
        gain_copy(step).wait()
    sums = gain_own[...]
    for step in range(7):
        sums = sums + gain_in[step]
    o_gains[...] = sums[:, None, :]

    def sent(unit, carry):
        @pl.when(added_here(unit))
        def _():
            await_arrival(got_a.at[unit], a_sends.at[unit])
            await_arrival(got_b.at[unit], b_sends.at[unit])
            await_arrival(got_c.at[unit], c_sends.at[unit])

        return carry

    lax.fori_loop(0, UNITS + LENT, sent, 0)

    @pl.when(lender)
    def _():
        def returned(place, carry):
            await_arrival(made.at[UNITS + place], lent_sends.at[place])
            await_arrival(total.at[2 * place + 1], back_arrivals.at[place])
            deliver(2 * place + 1)
            return carry

        lax.fori_loop(0, loan, returned, 0)

    @pl.when(jnp.logical_not(lender))
    def _():
        def returned(place, carry):
            await_arrival(total.at[UNITS + place], back_sends.at[place])
            return carry

        lax.fori_loop(0, loan, returned, 0)

    await_arrival(total.at[pl.ds(0, UNITS)], out_sem)


def weight_grads(na, dt, mixed, da, nm, dh, act, db, gains):
    tokens = na.shape[0] * na.shape[1]
    sds = jax.ShapeDtypeStruct
    operands = [v.reshape(tokens, -1) for v in (na, dt, mixed, da, nm, dh, act, db)]
    return pl.pallas_call(
        weight_grad_kernel,
        out_shape=[
            sds((96, 3 * D), F32),
            sds((96, D), F32),
            sds((96, FF), F32),
            sds((384, D), F32),
            sds((2, 1, D), F32),
        ],
        in_specs=[ANY] * 8 + [IN_VMEM],
        out_specs=[ANY] * 4 + [IN_VMEM],
        scratch_shapes=[
            pltpu.VMEM((2, tokens, D), BF16),
            pltpu.VMEM((2, tokens, UNIT), BF16),
            pltpu.VMEM((tokens, FF), BF16),
            pltpu.VMEM((UNITS + LENT, 2, 2, 2, 96, UNIT), BF16),
            pltpu.VMEM((UNITS + LENT, 2, 2, 96, UNIT), BF16),
            pltpu.VMEM((UNITS + LENT, 2, 96, UNIT), BF16),
            pltpu.VMEM((UNITS + LENT, 96, UNIT), BF16),
            pltpu.VMEM((UNITS + LENT, 96, UNIT), F32),
            pltpu.VMEM((2, D), F32),
            pltpu.VMEM((7, 2, D), F32),
            DMA((2,)),
            DMA((2,)),
            DMA,
            DMA((UNITS + LENT,)),
            DMA((UNITS + LENT,)),
            DMA((UNITS + LENT,)),
            DMA((UNITS + LENT,)),
            DMA((UNITS + LENT,)),
            DMA((UNITS + LENT,)),
            DMA,
            DMA((7,)),
            DMA((7,)),
            DMA((LENT,)),
            DMA((LENT,)),
            DMA((LENT,)),
            DMA((LENT,)),
            pltpu.SemaphoreType.REGULAR,
        ],
        compiler_params=pltpu.CompilerParams(
            collective_id=2, has_side_effects=True, vmem_limit_bytes=VMEM_LIMIT
        ),
        name="weight_grads",
    )(*operands, gains)


def hand_over_kernel(gains, *refs):
    sources, results, (gain_attn, gain_mlp), held = refs[:6], refs[6:12], refs[12:14], refs[14:20]
    come, go = refs[20], refs[21]
    arriving = [
        pltpu.make_async_copy(src, buf, come.at[at]) for at, (src, buf) in enumerate(zip(sources, held))
    ]
    leaving = [
        pltpu.make_async_copy(buf, dst, go.at[at]) for at, (buf, dst) in enumerate(zip(held, results))
    ]
    for copy in arriving:
        copy.start()
    shift = lax.rem(D - 96 * lax.axis_index("dp"), D)
    for kind, ref in enumerate((gain_attn, gain_mlp)):
        turned = pltpu.roll(jnp.broadcast_to(gains[kind], (8, D)), shift, 1)
        ref[...] = turned[:1, :96]
    for copy, onward in zip(arriving, leaving):
        copy.wait()
        onward.start()
    for copy in leaving:
        copy.wait()


def hand_over(output, input_grad, shards, gains):
    sds = jax.ShapeDtypeStruct
    sources = (output, input_grad, *shards)
    outs = pl.pallas_call(
        hand_over_kernel,
        out_shape=[sds(v.shape, v.dtype) for v in sources] + [sds((1, 96), F32)] * 2,
        in_specs=[IN_VMEM] + [ANY] * 6,
        out_specs=[ANY] * 6 + [IN_VMEM] * 2,
        scratch_shapes=[pltpu.VMEM(v.shape, v.dtype) for v in sources] + [DMA((6,)), DMA((6,))],
        compiler_params=pltpu.CompilerParams(vmem_limit_bytes=VMEM_LIMIT),
        name="hand_over",
    )(gains, *sources)
    output, input_grad, qkv, out, up, down, gain_attn, gain_mlp = outs
    return output, input_grad, gain_attn, qkv[None], out[None], gain_mlp, up[None], down[None]


def body(tokens, cotangent, doc_ids, gain_attn, w_qkv, w_out, gain_mlp, w_up, w_down):
    sections = lax.axis_size("section")
    rows, seq = doc_ids.shape
    chunks = rows * seq // C
    weights = (gain_attn, gain_mlp, w_qkv[0], w_out[0], w_up[0], w_down[0])
    output, input_grad, gains, kept = layers(sections, chunks, tokens, cotangent, doc_ids, weights)
    db, dh, da, dt = kept["db"], kept["dh"], kept["da"], kept["dt"]
    if lax.axis_size("dp") == 8 and sections == 4 and chunks == 8:
        qkv, out, up, down, gains = weight_grads(
            kept["na"], dt, kept["mixed"], da, kept["nm"], dh, kept["act"], db, gains
        )
        return hand_over(
            output.reshape(tokens.shape), input_grad.reshape(cotangent.shape), (qkv, out, up, down), gains
        )
    gains = jnp.sum(gains, axis=1)
    grads = (
        gains[0],
        matmul_lt(kept["na"], dt),
        matmul_lt(kept["mixed"], da),
        gains[1],
        matmul_lt(kept["nm"], dh),
        matmul_lt(kept["act"], db),
    )
    shards = lax.psum_scatter(grads, "dp", scatter_dimension=0, tiled=True)
    return (
        output.reshape(tokens.shape),
        input_grad.reshape(cotangent.shape),
        *(shard[None] for shard in shards),
    )


def solution(mesh):
    rows = P(("dp", "section"), None)
    layer = P("section", None)
    matrix = P("section", None, None)
    in_specs = (rows, rows, P("dp", None), layer, matrix, matrix, layer, matrix, matrix)
    split = P("section", "dp")
    split_matrix = P("section", "dp", None)
    out_specs = (rows, rows, split, split_matrix, split_matrix, split, split_matrix, split_matrix)
    return jax.shard_map(body, mesh=mesh, in_specs=in_specs, out_specs=out_specs, check_vma=False)
```
